256 devices in a mesh: row: 8 (over y, core), col: 32 (over x, z).
Axes of the slice: x: 4, y: 4, z: 8, core: 2. Of those that a mesh axis runs over, the one named last changes fastest.
Arguments:
- src_embed: bfloat16 [32768, 256], P(('row', 'col'))
- tgt_embed: bfloat16 [32768, 256], P(('col', 'row')), may hold values from -0.375 to 0.375
- tiles: int32 [8, 32, 2, 128], P('row', 'col'), may hold values from 0 to 31, as said below
- counts: int32 [8, 32], P('row', 'col'), may hold values from 1 to 128, as said below
Outputs:
- source_potential: float32 [32768], P('row')
- target_potential: float32 [32768], P('col')
The draws below stay inside these ranges and needn't reach their ends.
Inputs may be any that keep to these rules, and one draw needn't show every extreme that they name: tiles[r, c, 0, k] is a source block among the 32 of row index r and tiles[r, c, 1, k] a target block among the 8 of col index c; the first counts[r, c] slots of a device hold distinct pairs, the other slots hold pairs that are not part of the support; every source block and every target block appears in some counted slot of some device. `counts`: some device uses all 128 slots in every draw.
All inputs are finite; a program needn't handle non-finite values.
Results may differ from the reference program's by a relative error of at most 0.00035.
Values may be sent and summed in bfloat16 or wider, within the bound.
No kernel may reach another device: no remote copies, remote signals or barrier semaphores. Data moves between devices by JAX's collectives and lax.ppermute only.
A program may use at most 128 MiB of HBM per device.

```python
import math
import jax
import jax.numpy as jnp
from jax import lax

E = 256
TILE = 128
ITERS = 2
SB = 32
TB = 8
CAP = 128
SRC_DEV = 4096
TGT_DEV = 1024
NS = 32768
NT = 32768
N_ROW = 8
N_COL = 32


def draw_src_embed(key, part):
    key = jax.random.fold_in(key, 3)
    first = jax.random.fold_in(key, 0)
    third = jax.random.fold_in(key, 2)
    fourth = jax.random.fold_in(key, 3)
    flagged = jax.random.randint(third, (NS, 1), 0, 8, dtype=jnp.int32) == 0
    far_scale = jnp.sqrt(jax.random.uniform(fourth, (NS, 1), jnp.float32, 40.0, 60.0))
    values = jax.random.normal(first, (NS, E), jnp.float32)
    values = values * jnp.where(flagged, far_scale, 1.0)
    return (values * 0.0625).astype(jnp.bfloat16)


def draw_tgt_embed(key, part):
    key = jax.random.fold_in(key, 5)
    first, second, third = jax.random.split(key, 3)
    values = jax.random.normal(first, (NT, E), jnp.float32)
    values = jnp.clip(values * 0.0625, -0.375, 0.375)
    flagged = jax.random.randint(second, (NT, 1), 0, 64, dtype=jnp.int32) == 0
    signs = jnp.where(jax.random.uniform(third, (NT, E), jnp.float32) < 0.5, -0.375, 0.375)
    return jnp.where(flagged, signs, values).astype(jnp.bfloat16)


def draw_tiles(key, part):
    key = jax.random.fold_in(key, 7)
    row_devices = NS // SRC_DEV
    col_devices = NT // TGT_DEV
    fewest = max(-(-SB // col_devices), -(-TB // row_devices))
    pair_count = SB * TB
    pair_ids = jnp.arange(pair_count, dtype=jnp.int32)
    scores = jax.random.randint(key, (row_devices, col_devices, pair_count), 0, 2 ** 18, dtype=jnp.int32) * pair_count + pair_ids[None, None, :]
    row_ids = jnp.arange(row_devices, dtype=jnp.int32)[:, None, None]
    col_ids = jnp.arange(col_devices, dtype=jnp.int32)[None, :, None]
    for forced_slot in range(fewest):
        forced = (col_ids + forced_slot * col_devices) % SB * TB + (row_ids + forced_slot * row_devices) % TB
        scores = jnp.where(pair_ids[None, None, :] == forced, forced_slot - fewest, scores)
    ranking = jnp.argsort(scores, axis=-1)[..., :CAP]
    return jnp.stack([ranking // TB, ranking % TB], axis=2).astype(jnp.int32)


def draw_counts(key, part):
    key = jax.random.fold_in(key, 11)
    row_devices = NS // SRC_DEV
    col_devices = NT // TGT_DEV
    fewest = max(-(-SB // col_devices), -(-TB // row_devices))
    first, second = jax.random.split(key)
    spread = jax.random.randint(first, (row_devices, col_devices), 0, CAP + 1, dtype=jnp.int32)
    loads = jnp.maximum(fewest, spread * spread // CAP)
    busiest = jax.random.randint(second, (), 0, row_devices * col_devices, dtype=jnp.int32)
    flat_ids = jnp.arange(row_devices * col_devices, dtype=jnp.int32).reshape(row_devices, col_devices)
    return jnp.where(flat_ids == busiest, CAP, loads).astype(jnp.int32)


def setup_inputs(seed: int = 0) -> dict:
    streams_of = jax.random.split(jax.random.key(seed), 5)
    return {
        "src_embed": draw_src_embed(jax.random.fold_in(streams_of[4], 71), 0),
        "tgt_embed": draw_tgt_embed(jax.random.fold_in(streams_of[4], 71), 0),
        "tiles": draw_tiles(jax.random.fold_in(streams_of[4], 71), 0),
        "counts": draw_counts(jax.random.fold_in(streams_of[4], 71), 0),
    }


ENTROPY = 0.05
EMPTY_PEAK = -1e30


def block_stats(scores, in_use, block_ids, blocks, reduce_dim):
    masked = jnp.where(in_use[:, None, None], scores, -jnp.inf)
    tile_peak = jnp.max(masked, axis=reduce_dim)
    member = (block_ids[:, None] == jnp.arange(blocks, dtype=jnp.int32)[None, :]) & in_use[:, None]
    peaks = jnp.max(jnp.where(member[:, :, None], tile_peak[:, None, :], EMPTY_PEAK), axis=0)
    spread = jnp.expand_dims(peaks[block_ids], reduce_dim)
    weights = jnp.exp(masked - spread)
    tile_total = jnp.sum(weights, axis=reduce_dim)
    totals = jnp.dot(member.astype(jnp.float32).T, tile_total, precision=lax.Precision.HIGHEST, preferred_element_type=jnp.float32)
    return peaks.reshape(-1), totals.reshape(-1)


def device_costs(src_embed, tgt_embed, tiles, counts, flat):
    row_idx = flat // N_COL
    col_idx = flat % N_COL
    src_band = lax.dynamic_slice_in_dim(src_embed, row_idx * SRC_DEV, SRC_DEV, 0).astype(jnp.float32)
    tgt_band = lax.dynamic_slice_in_dim(tgt_embed, col_idx * TGT_DEV, TGT_DEV, 0).astype(jnp.float32)
    pairs = tiles[row_idx, col_idx]
    in_use = jnp.arange(CAP, dtype=jnp.int32) < counts[row_idx, col_idx]
    src_tiles = src_band.reshape(SB, TILE, E)[pairs[0]]
    tgt_tiles = tgt_band.reshape(TB, TILE, E)[pairs[1]]
    inner = jnp.einsum("kte,kue->ktu", src_tiles, tgt_tiles, precision=lax.Precision.HIGHEST)
    sq_src = jnp.sum(src_tiles * src_tiles, axis=2)
    sq_tgt = jnp.sum(tgt_tiles * tgt_tiles, axis=2)
    costs = sq_src[:, :, None] + sq_tgt[:, None, :] - 2.0 * inner
    return costs, pairs, in_use, row_idx, col_idx


def reference(src_embed, tgt_embed, tiles, counts):
    devices = jnp.arange(N_ROW * N_COL, dtype=jnp.int32)
    tgt_pot = jnp.zeros((NT,), jnp.float32)
    src_pot = jnp.zeros((NS,), jnp.float32)
    for sweep in range(ITERS):
        def source_side(flat):
            costs, pairs, in_use, row_idx, col_idx = device_costs(src_embed, tgt_embed, tiles, counts, flat)
            near = lax.dynamic_slice_in_dim(tgt_pot, col_idx * TGT_DEV, TGT_DEV, 0).reshape(TB, TILE)[pairs[1]]
            scores = (near[:, None, :] - costs) / ENTROPY
            return block_stats(scores, in_use, pairs[0], SB, 2)

        peaks, totals = lax.map(source_side, devices)
        peaks = peaks.reshape(N_ROW, N_COL, SRC_DEV)
        totals = totals.reshape(N_ROW, N_COL, SRC_DEV)
        highest = jnp.max(peaks, axis=1)
        whole = jnp.sum(totals * jnp.exp(peaks - highest[:, None, :]), axis=1)
        src_pot = (-ENTROPY * math.log(NS) - ENTROPY * (highest + jnp.log(whole))).reshape(NS)

        def target_side(flat):
            costs, pairs, in_use, row_idx, col_idx = device_costs(src_embed, tgt_embed, tiles, counts, flat)
            near = lax.dynamic_slice_in_dim(src_pot, row_idx * SRC_DEV, SRC_DEV, 0).reshape(SB, TILE)[pairs[0]]
            scores = (near[:, :, None] - costs) / ENTROPY
            return block_stats(scores, in_use, pairs[1], TB, 1)

        peaks, totals = lax.map(target_side, devices)
        peaks = peaks.reshape(N_ROW, N_COL, TGT_DEV)
        totals = totals.reshape(N_ROW, N_COL, TGT_DEV)
        highest = jnp.max(peaks, axis=0)
        whole = jnp.sum(totals * jnp.exp(peaks - highest[None, :, :]), axis=0)
        tgt_pot = (-ENTROPY * math.log(NT) - ENTROPY * (highest + jnp.log(whole))).reshape(NT)
    return src_pot, tgt_pot
```

```python
import functools
import math

import jax
import jax.numpy as jnp
from jax import lax
from jax.experimental import pallas as pl
from jax.experimental.pallas import tpu as pltpu
from jax.sharding import Mesh
from jax.sharding import PartitionSpec as P

TILE = 128
ITERS = 2
ENTROPY = 0.05
KAPPA = math.log2(math.e) / ENTROPY
EMPTY = -1e30
UNROLL = 4
F32 = jnp.float32
VMEM = pl.BlockSpec(memory_space=pltpu.VMEM)
SMEM = pl.BlockSpec(memory_space=pltpu.SMEM)


def square_rows(cells):
    wide = cells.astype(F32)
    square = wide * wide
    high = square.astype(jnp.bfloat16)
    low = (square - high.astype(F32)).astype(jnp.bfloat16)
    ones = jnp.ones((8, cells.shape[1]), jnp.bfloat16)
    dims = (((1,), (1,)), ((), ()))
    total = lax.dot_general(ones, high, dims, preferred_element_type=F32)
    total += lax.dot_general(ones, low, dims, preferred_element_type=F32)
    return total[0:1]


def log_sum(parts):
    highest = jnp.max(parts, axis=0)
    return highest + jnp.log2(jnp.sum(jnp.exp2(parts - highest[None]), axis=0))


def expand(weights, wide):
    blocks = weights.shape[0]
    if blocks < TILE:
        weights = jnp.concatenate([weights, jnp.zeros((TILE - blocks, TILE), F32)], axis=0)
    columns = weights.T
    for n in range(blocks):
        wide[n] = jnp.broadcast_to(columns[:, n : n + 1], (TILE, TILE))


def tile_sums(near_ids, far_ids, count, near, far, wide, peaks, totals, out):
    near_blocks, far_blocks = near.shape[0], far.shape[0]
    spare = near_blocks * far_blocks
    peaks[...] = jnp.full(peaks.shape, EMPTY, F32)
    totals[...] = jnp.zeros(totals.shape, F32)

    @pl.loop(0, (count + UNROLL - 1) // UNROLL)
    def _(step):
        for u in range(UNROLL):
            k = step * UNROLL + u
            n = jnp.where(k < count, near_ids(k), 0)
            f = jnp.where(k < count, far_ids(k), 0)
            inner = lax.dot_general(
                near[n], far[f], (((1,), (1,)), ((), ())), preferred_element_type=F32
            )
            score = (inner * (2.0 * KAPPA) + wide[n]).reshape(TILE // 8, 8, TILE)
            peak = jnp.max(score, axis=0)
            slot = jnp.where(k < count, f * near_blocks + n, spare)
            peaks[slot] = peak
            totals[slot] = jnp.sum(jnp.exp2(score - peak[None]), axis=0)

    rows = []
    for f in range(far_blocks):
        at = pl.ds(f * near_blocks, near_blocks)
        peak = peaks[at]
        highest = jnp.max(jnp.max(peak, axis=0), axis=0, keepdims=True)
        whole = jnp.sum(totals[at] * jnp.exp2(peak - highest[None]), axis=0)
        whole = jnp.sum(whole, axis=0, keepdims=True)
        rows.append(jnp.where(whole > 0.0, highest + jnp.log2(whole), EMPTY))
    result = jnp.concatenate(rows, axis=0)
    out[...] = jnp.broadcast_to(result[None], out.shape)


def first_kernel(tiles, count, src, tgt, out, sq_src, sq_tgt, wide, peaks, totals):
    for b in range(tgt.shape[0]):
        sq_tgt[b : b + 1, :] = square_rows(tgt[b])
    for a in range(src.shape[0]):
        sq_src[a : a + 1, :] = square_rows(src[a])
    expand(sq_tgt[...] * -KAPPA, wide)
    tile_sums(lambda k: tiles[1, k], lambda k: tiles[0, k], count[0, 0], tgt, src, wide, peaks, totals, out)


def source_kernel(log_cells, tiles, count, src, tgt, parts, out, wide, peaks, totals):
    expand(-log_cells - log_sum(parts[...]), wide)
    tile_sums(lambda k: tiles[1, k], lambda k: tiles[0, k], count[0, 0], tgt, src, wide, peaks, totals, out)


def target_kernel(log_cells, tiles, count, src, tgt, parts, sq_src, out, pot, wide, peaks, totals):
    weights = -log_cells - log_sum(parts[...])
    pot[...] = weights * (1.0 / KAPPA) + sq_src[...]
    expand(weights, wide)
    tile_sums(lambda k: tiles[0, k], lambda k: tiles[1, k], count[0, 0], src, tgt, wide, peaks, totals, out)


def last_kernel(log_cells, parts, sq_tgt, pot):
    pot[...] = (-log_cells - log_sum(parts[...])) * (1.0 / KAPPA) + sq_tgt[...]


def call(kernel, outs, near_blocks, spare, *args):
    scratch = []
    if near_blocks:
        scratch = [
            pltpu.VMEM((near_blocks, TILE, TILE), F32),
            pltpu.VMEM((spare + 1, 8, TILE), F32),
            pltpu.VMEM((spare + 1, 8, TILE), F32),
        ]
    smem = 2 if near_blocks else 0
    return pl.pallas_call(
        kernel,
        out_shape=[jax.ShapeDtypeStruct(s, F32) for s in outs],
        in_specs=[SMEM] * smem + [VMEM] * (len(args) - smem),
        out_specs=[VMEM] * len(outs),
        scratch_shapes=scratch,
        compiler_params=pltpu.CompilerParams(vmem_limit_bytes=24 * 2**20),
    )(*args)


def gather(block, axis, devices):
    return lax.all_to_all(
        jnp.broadcast_to(block[None], (devices,) + block.shape), axis, 0, 0, tiled=True
    )


def local(src_embed, tgt_embed, tiles, counts):
    rows, cols = lax.axis_size(("y", "core")), lax.axis_size(("x", "z"))
    tiles = tiles[0, 0]
    width = src_embed.shape[1]
    near_z = gather(src_embed, "z", lax.axis_size("z"))
    src = gather(near_z, "x", lax.axis_size("x")).reshape(cols, TILE, width)
    tgt = gather(tgt_embed, ("y", "core"), rows)
    log_src = math.log2(rows * cols * TILE)
    log_tgt = math.log2(rows * cols * TILE)
    spare = rows * cols
    swap_src = lambda v: lax.all_to_all(v, ("x", "z"), 0, 0, tiled=True)
    swap_tgt = lambda v: lax.all_to_all(v, ("y", "core"), 0, 0, tiled=True)
    src_out = (cols, cols, TILE)
    tgt_out = (rows, rows, TILE)
    for sweep in range(ITERS):
        if sweep == 0:
            parts, sq_src, sq_tgt = call(
                first_kernel, [src_out, (cols, TILE), (rows, TILE)], rows, spare, tiles, counts, src, tgt
            )
        else:
            (parts,) = call(
                functools.partial(source_kernel, log_tgt), [src_out], rows, spare, tiles, counts, src, tgt, parts
            )
        parts = swap_src(parts)
        parts, src_pot = call(
            functools.partial(target_kernel, log_src),
            [tgt_out, (cols, TILE)],
            cols,
            spare,
            tiles,
            counts,
            src,
            tgt,
            parts,
            sq_src,
        )
        parts = swap_tgt(parts)
    (tgt_pot,) = call(functools.partial(last_kernel, log_tgt), [(rows, TILE)], 0, 0, parts, sq_tgt)
    return (src_pot.reshape(-1), tgt_pot.reshape(-1))


def solution(mesh):
    fine = Mesh(mesh.devices.reshape(4, 2, 4, 8), ("y", "core", "x", "z"))
    row, col = ("y", "core"), ("x", "z")
    in_specs = (P(row + col, None), P(col + row, None), P(row, col, None, None), P(row, col))
    out_specs = (P(row), P(col))
    return jax.shard_map(local, mesh=fine, in_specs=in_specs, out_specs=out_specs, check_vma=False)
```

```python
import functools
import math

import jax
import jax.numpy as jnp
from jax import lax
from jax.experimental import pallas as pl
from jax.experimental.pallas import tpu as pltpu
from jax.sharding import Mesh
from jax.sharding import PartitionSpec as P

TILE = 128
ITERS = 2
ENTROPY = 0.05
KAPPA = math.log2(math.e) / ENTROPY
EMPTY = -1e30
UNROLL = 16
ROW = ("y", "core")
COL = ("x", "s", "p")
SRC_PEERS = ("x", "s")
TGT_PEERS = ("p", "y", "core")
F32 = jnp.float32
NT = (((1,), (1,)), ((), ()))
VMEM = pl.BlockSpec(memory_space=pltpu.VMEM)
SMEM = pl.BlockSpec(memory_space=pltpu.SMEM)
PARAMS = pltpu.CompilerParams(vmem_limit_bytes=24 * 2**20)


def square_rows(cells):
    wide = cells.astype(F32)
    square = wide * wide
    high = square.astype(jnp.bfloat16)
    low = (square - high.astype(F32)).astype(jnp.bfloat16)
    ones = jnp.ones((8, cells.shape[1]), jnp.bfloat16)
    total = lax.dot_general(ones, high, NT, preferred_element_type=F32)
    total += lax.dot_general(ones, low, NT, preferred_element_type=F32)
    return total[0:1]


def log_sum(parts):
    highest = jnp.max(parts, axis=0)
    return highest + jnp.log2(jnp.sum(jnp.exp2(parts - highest[None]), axis=0))


def expand(weights, wide):
    blocks = weights.shape[0]
    columns = jnp.concatenate([weights, jnp.zeros((TILE - blocks, TILE), F32)], axis=0).T
    for n in range(blocks):
        wide[n] = jnp.broadcast_to(columns[:, n : n + 1], (TILE, TILE))


def tile_sums(tile, count, near, far, wide, peaks, totals):
    near_blocks, far_blocks = near.shape[0], far.shape[0]
    spare = near_blocks * far_blocks
    peaks[...] = jnp.full(peaks.shape, EMPTY, F32)
    totals[...] = jnp.zeros(totals.shape, F32)

    @pl.loop(0, (count + UNROLL - 1) // UNROLL)
    def _(step):
        for u in range(UNROLL):
            k = step * UNROLL + u
            n, f = tile(jnp.where(k < count, k, 0))
            inner = lax.dot_general(near[n], far[f], NT, preferred_element_type=F32)
            score = (inner * (2.0 * KAPPA) + wide[n]).reshape(TILE // 8, 8, TILE)
            peak = jnp.max(score, axis=0)
            slot = jnp.where(k < count, f * near_blocks + n, spare)
            peaks[slot] = peak
            totals[slot] = jnp.sum(jnp.exp2(score - peak[None]), axis=0)

    rows = []
    for f in range(far_blocks):
        at = pl.ds(f * near_blocks, near_blocks)
        peak = peaks[at]
        highest = jnp.max(jnp.max(peak, axis=0), axis=0, keepdims=True)
        whole = jnp.sum(totals[at] * jnp.exp2(peak - highest[None]), axis=0)
        whole = jnp.sum(whole, axis=0, keepdims=True)
        rows.append(jnp.where(whole > 0.0, highest + jnp.log2(whole), EMPTY))
    return jnp.concatenate(rows, axis=0)


def pick_kernel(mine, other, parity, picked, total):
    p = parity[0]
    targets = 8

    def scan(lists, col, start):
        def step(k, at):
            a, b = lists[0, k], lists[1, k]
            picked[at] = (a // 2) * (2 * targets) + col * targets + b
            return at + jnp.where((k < lists[2, 0]) & (a % 2 == p), 1, 0)

        return lax.fori_loop(0, TILE, step, start, unroll=8)

    total[0] = scan(other, 1 - p, scan(mine, p, 0))


def source_tiles(tiles, tgt_blocks):
    def tile(k):
        code = tiles[k]
        return lax.rem(code, tgt_blocks), lax.div(code, tgt_blocks)

    return tile


def target_tiles(tiles, tgt_blocks):
    def tile(k):
        code = tiles[k]
        return lax.div(code, tgt_blocks), lax.rem(code, tgt_blocks)

    return tile


def first_kernel(tiles, count, src, tgt, out, sq_src, sq_tgt, wide, peaks, totals):
    for b in range(tgt.shape[0]):
        sq_tgt[b : b + 1, :] = square_rows(tgt[b])
    for a in range(src.shape[0]):
        sq_src[a : a + 1, :] = square_rows(src[a])
    expand(sq_tgt[...] * -KAPPA, wide)
    sums = tile_sums(source_tiles(tiles, tgt.shape[0]), count[0], tgt, src, wide, peaks, totals)
    out[...] = jnp.broadcast_to(sums[None], out.shape)


def source_kernel(log_cells, tiles, count, src, tgt, parts, out, wide, peaks, totals):
    expand(-log_cells - log_sum(parts[...]), wide)
    sums = tile_sums(source_tiles(tiles, tgt.shape[0]), count[0], tgt, src, wide, peaks, totals)
    out[...] = jnp.broadcast_to(sums[None], out.shape)


def target_kernel(log_cells, tiles, count, src, tgt, parts, sq_src, out, pot, wide, peaks, totals):
    weights = -log_cells - log_sum(parts[...])
    pot[...] = weights * (1.0 / KAPPA) + sq_src[...]
    expand(weights, wide)
    sums = tile_sums(target_tiles(tiles, tgt.shape[0]), count[0], src, tgt, wide, peaks, totals)
    copies, blocks = out.shape[0], out.shape[1]
    if blocks == sums.shape[0]:
        out[...] = jnp.broadcast_to(sums[None], out.shape)
    else:
        cols = sums.shape[0] // blocks
        each = copies // cols
        for col in range(cols):
            piece = sums[col * blocks : (col + 1) * blocks]
            out[col * each : (col + 1) * each] = jnp.broadcast_to(piece[None], (each,) + piece.shape)


def last_kernel(log_cells, parity, parts, sq_tgt, mine, other, tgt_pot, src_pot):
    p = parity[0]
    blocks = tgt_pot.shape[0]
    squares = jnp.where(p == 0, sq_tgt[0:blocks], sq_tgt[blocks : 2 * blocks])
    tgt_pot[...] = (-log_cells - log_sum(parts[...])) * (1.0 / KAPPA) + squares
    src_pot[:, 0, :] = jnp.where(p == 0, mine[...], other[...])
    src_pot[:, 1, :] = jnp.where(p == 0, other[...], mine[...])


def half_step(kernel, outs, near_blocks, slots, tiles, count, *args):
    return pl.pallas_call(
        kernel,
        out_shape=[jax.ShapeDtypeStruct(s, F32) for s in outs],
        in_specs=[SMEM] * 2 + [VMEM] * len(args),
        out_specs=[VMEM] * len(outs),
        scratch_shapes=[
            pltpu.VMEM((near_blocks, TILE, TILE), F32),
            pltpu.VMEM((slots + 1, 8, TILE), F32),
            pltpu.VMEM((slots + 1, 8, TILE), F32),
        ],
        compiler_params=PARAMS,
    )(tiles, count, *args)


def exchange(copies, peers):
    return lax.all_to_all(copies, peers, 0, 0, tiled=True)


def gather(block, peers):
    return exchange(jnp.broadcast_to(block[None], (lax.axis_size(peers),) + block.shape), peers)


def local(src_embed, tgt_embed, tiles, counts):
    rows, cols = lax.axis_size(ROW), lax.axis_size(COL)
    log_cells = math.log2(rows * cols * TILE)
    parity = lax.axis_index("p").astype(jnp.int32).reshape(1)
    partner = lambda v: lax.ppermute(v, "p", [(0, 1), (1, 0)])

    lists = jnp.concatenate([tiles[0, 0], jnp.broadcast_to(counts[0, 0], (1, TILE))], axis=0)
    other_lists = partner(lists)
    tgt = gather(tgt_embed, TGT_PEERS)
    src = gather(src_embed, SRC_PEERS)
    picked, count = pl.pallas_call(
        pick_kernel,
        out_shape=[jax.ShapeDtypeStruct((2 * TILE + UNROLL,), jnp.int32), jax.ShapeDtypeStruct((1,), jnp.int32)],
        in_specs=[SMEM] * 3,
        out_specs=[SMEM] * 2,
        compiler_params=PARAMS,
    )(lists, other_lists, parity)

    srcs, tgts = src.shape[0], tgt.shape[0]
    slots = srcs * tgts
    src_out, tgt_out = (srcs, srcs, TILE), (tgts, tgts, TILE)
    for sweep in range(ITERS):
        if sweep == 0:
            parts, sq_src, sq_tgt = half_step(
                first_kernel, [src_out, (srcs, TILE), (tgts, TILE)], tgts, slots, picked, count, src, tgt
            )
        else:
            (parts,) = half_step(
                functools.partial(source_kernel, log_cells), [src_out], tgts, slots, picked, count, src, tgt, parts
            )
        parts = exchange(parts, SRC_PEERS)
        last = sweep == ITERS - 1
        parts, src_pot = half_step(
            functools.partial(target_kernel, log_cells),
            [(tgts, rows, TILE) if last else tgt_out, (srcs, TILE)],
            srcs,
            slots,
            picked,
            count,
            src,
            tgt,
            parts,
            sq_src,
        )
        if last:
            other_pot = partner(src_pot)
        parts = exchange(parts, TGT_PEERS)
    tgt_pot, both = pl.pallas_call(
        functools.partial(last_kernel, log_cells),
        out_shape=[jax.ShapeDtypeStruct((rows, TILE), F32), jax.ShapeDtypeStruct((srcs, 2, TILE), F32)],
        in_specs=[SMEM] + [VMEM] * 4,
        out_specs=[VMEM] * 2,
        compiler_params=PARAMS,
    )(parity, parts, sq_tgt, src_pot, other_pot)
    return (both.reshape(-1), tgt_pot.reshape(-1))


def solution(mesh):
    fine = Mesh(mesh.devices.reshape(4, 2, 4, 4, 2), ROW + COL)
    in_specs = (P(ROW + COL, None), P(COL + ROW, None), P(ROW, COL, None, None), P(ROW, COL))
    return jax.shard_map(local, mesh=fine, in_specs=in_specs, out_specs=(P(ROW), P(COL)), check_vma=False)
```

```python
import functools
import math

import jax
import jax.numpy as jnp
from jax import lax
from jax.experimental import pallas as pl
from jax.experimental.pallas import tpu as pltpu
from jax.sharding import Mesh
from jax.sharding import PartitionSpec as P

TILE = 128
ITERS = 2
ENTROPY = 0.05
KAPPA = math.log2(math.e) / ENTROPY
EMPTY = -1e30
UNROLL = 16
ROW = ("y", "core")
COL = ("x", "s", "p")
SRC_PEERS = ("x", "s")
TGT_PEERS = ("p", "y", "core")
F32 = jnp.float32
NT = (((1,), (1,)), ((), ()))
VMEM = pl.BlockSpec(memory_space=pltpu.VMEM)
SMEM = pl.BlockSpec(memory_space=pltpu.SMEM)
PARAMS = pltpu.CompilerParams(vmem_limit_bytes=24 * 2**20)


def square_rows(cells):
    wide = cells.astype(F32)
    square = wide * wide
    high = square.astype(jnp.bfloat16)
    low = (square - high.astype(F32)).astype(jnp.bfloat16)
    ones = jnp.ones((8, cells.shape[1]), jnp.bfloat16)
    total = lax.dot_general(ones, high, NT, preferred_element_type=F32)
    total += lax.dot_general(ones, low, NT, preferred_element_type=F32)
    return total[0:1]


def log_sum(parts):
    highest = jnp.max(parts, axis=0)
    return highest + jnp.log2(jnp.sum(jnp.exp2(parts - highest[None]), axis=0))


def expand(weights, wide):
    blocks = weights.shape[0]
    columns = jnp.concatenate([weights, jnp.zeros((TILE - blocks, TILE), F32)], axis=0).T
    for n in range(blocks):
        wide[n] = jnp.broadcast_to(columns[:, n : n + 1], (TILE, TILE))


def tile_sums(tile, count, near, far, wide, peaks, totals):
    near_blocks, far_blocks = near.shape[0], far.shape[0]
    spare = near_blocks * far_blocks
    peaks[...] = jnp.full(peaks.shape, EMPTY, F32)
    totals[...] = jnp.zeros(totals.shape, F32)

    @pl.loop(0, (count + UNROLL - 1) // UNROLL)
    def _(step):
        for u in range(UNROLL):
            k = step * UNROLL + u
            n, f = tile(jnp.where(k < count, k, 0))
            inner = lax.dot_general(near[n], far[f], NT, preferred_element_type=F32)
            score = (inner * (2.0 * KAPPA) + wide[n]).reshape(TILE // 8, 8, TILE)
            peak = jnp.max(score, axis=0)
            slot = jnp.where(k < count, f * near_blocks + n, spare)
            peaks[slot] = peak
            totals[slot] = jnp.sum(jnp.exp2(score - peak[None]), axis=0)

    rows = []
    for f in range(far_blocks):
        at = pl.ds(f * near_blocks, near_blocks)
        peak = peaks[at]
        highest = jnp.max(jnp.max(peak, axis=0), axis=0, keepdims=True)
        whole = jnp.sum(totals[at] * jnp.exp2(peak - highest[None]), axis=0)
        whole = jnp.sum(whole, axis=0, keepdims=True)
        rows.append(jnp.where(whole > 0.0, highest + jnp.log2(whole), EMPTY))
    return jnp.concatenate(rows, axis=0)


def pick_kernel(mine, other, parity, picked, total):
    p = parity[0]
    targets = 8

    def scan(lists, col, start):
        def step(k, at):
            a, b = lists[0, k], lists[1, k]
            picked[at] = (a // 2) * (2 * targets) + col * targets + b
            return at + jnp.where((k < lists[2, 0]) & (a % 2 == p), 1, 0)

        return lax.fori_loop(0, TILE, step, start, unroll=8)

    total[0] = scan(other, 1 - p, scan(mine, p, 0))


def source_tiles(tiles, tgt_blocks):
    def tile(k):
        code = tiles[k]
        return lax.rem(code, tgt_blocks), lax.div(code, tgt_blocks)

    return tile


def target_tiles(tiles, tgt_blocks):
    def tile(k):
        code = tiles[k]
        return lax.div(code, tgt_blocks), lax.rem(code, tgt_blocks)

    return tile


def first_kernel(tiles, count, place, tgt, *rest):
    sides = len(rest) - 7
    pieces, (out, src, sq_src, sq_tgt, wide, peaks, totals) = rest[:sides], rest[sides:]
    deep = pieces[0].shape[0]
    for dx, piece in enumerate(pieces):
        x = lax.rem(place[0] + (sides - dx), sides)
        for ds in range(deep):
            s = lax.rem(place[1] + (deep - ds), deep)
            src[x * deep + s] = piece[ds]
    for b in range(tgt.shape[0]):
        sq_tgt[b : b + 1, :] = square_rows(tgt[b])
    for a in range(src.shape[0]):
        sq_src[a : a + 1, :] = square_rows(src[a])
    expand(sq_tgt[...] * -KAPPA, wide)
    sums = tile_sums(source_tiles(tiles, tgt.shape[0]), count[0], tgt, src, wide, peaks, totals)
    out[...] = jnp.broadcast_to(sums[None], out.shape)


def source_kernel(log_cells, tiles, count, src, tgt, parts, out, wide, peaks, totals):
    expand(-log_cells - log_sum(parts[...]), wide)
    sums = tile_sums(source_tiles(tiles, tgt.shape[0]), count[0], tgt, src, wide, peaks, totals)
    out[...] = jnp.broadcast_to(sums[None], out.shape)


def target_kernel(log_cells, tiles, count, src, tgt, parts, sq_src, out, pot, wide, peaks, totals):
    weights = -log_cells - log_sum(parts[...])
    pot[...] = weights * (1.0 / KAPPA) + sq_src[...]
    expand(weights, wide)
    sums = tile_sums(target_tiles(tiles, tgt.shape[0]), count[0], src, tgt, wide, peaks, totals)
    copies, blocks = out.shape[0], out.shape[1]
    if blocks == sums.shape[0]:
        out[...] = jnp.broadcast_to(sums[None], out.shape)
    else:
        cols = sums.shape[0] // blocks
        each = copies // cols
        for col in range(cols):
            piece = sums[col * blocks : (col + 1) * blocks]
            out[col * each : (col + 1) * each] = jnp.broadcast_to(piece[None], (each,) + piece.shape)


def last_kernel(log_cells, parity, parts, sq_tgt, mine, other, tgt_pot, src_pot):
    p = parity[0]
    blocks = tgt_pot.shape[0]
    squares = jnp.where(p == 0, sq_tgt[0:blocks], sq_tgt[blocks : 2 * blocks])
    tgt_pot[...] = (-log_cells - log_sum(parts[...])) * (1.0 / KAPPA) + squares
    src_pot[:, 0, :] = jnp.where(p == 0, mine[...], other[...])
    src_pot[:, 1, :] = jnp.where(p == 0, other[...], mine[...])


def half_step(kernel, outs, near_blocks, slots, scalars, *args):
    return pl.pallas_call(
        kernel,
        out_shape=[s if isinstance(s, jax.ShapeDtypeStruct) else jax.ShapeDtypeStruct(s, F32) for s in outs],
        in_specs=[SMEM] * len(scalars) + [VMEM] * len(args),
        out_specs=[VMEM] * len(outs),
        scratch_shapes=[
            pltpu.VMEM((near_blocks, TILE, TILE), F32),
            pltpu.VMEM((slots + 1, 8, TILE), F32),
            pltpu.VMEM((slots + 1, 8, TILE), F32),
        ],
        compiler_params=PARAMS,
    )(*scalars, *args)


def exchange(copies, peers):
    return lax.all_to_all(copies, peers, 0, 0, tiled=True)


def gather(block, peers):
    return exchange(jnp.broadcast_to(block[None], (lax.axis_size(peers),) + block.shape), peers)


def shifts(block, axis):
    n = lax.axis_size(axis)
    turn = lambda d: lax.ppermute(block, axis, [(i, (i + d) % n) for i in range(n)])
    return [block] + [turn(d) for d in range(1, n)]


def local(src_embed, tgt_embed, tiles, counts):
    rows, cols = lax.axis_size(ROW), lax.axis_size(COL)
    log_cells = math.log2(rows * cols * TILE)
    parity = lax.axis_index("p").astype(jnp.int32).reshape(1)
    partner = lambda v: lax.ppermute(v, "p", [(0, 1), (1, 0)])

    lists = jnp.concatenate([tiles[0, 0], jnp.broadcast_to(counts[0, 0], (1, TILE))], axis=0)
    other_lists = partner(lists)
    tgt = gather(tgt_embed, TGT_PEERS)
    src_pieces = shifts(jnp.concatenate([v[None] for v in shifts(src_embed, "s")]), "x")
    picked, count = pl.pallas_call(
        pick_kernel,
        out_shape=[jax.ShapeDtypeStruct((2 * TILE + UNROLL,), jnp.int32), jax.ShapeDtypeStruct((1,), jnp.int32)],
        in_specs=[SMEM] * 3,
        out_specs=[SMEM] * 2,
        compiler_params=PARAMS,
    )(lists, other_lists, parity)

    srcs, tgts = len(src_pieces) * src_pieces[0].shape[0], tgt.shape[0]
    src_shape = jax.ShapeDtypeStruct((srcs,) + src_embed.shape, src_embed.dtype)
    scalars = (picked, count)
    place = jnp.stack([lax.axis_index("x"), lax.axis_index("s")]).astype(jnp.int32)
    slots = srcs * tgts
    src_out, tgt_out = (srcs, srcs, TILE), (tgts, tgts, TILE)
    for sweep in range(ITERS):
        if sweep == 0:
            parts, src, sq_src, sq_tgt = half_step(
                first_kernel,
                [src_out, src_shape, (srcs, TILE), (tgts, TILE)],
                tgts,
                slots,
                scalars + (place,),
                tgt,
                *src_pieces,
            )
        else:
            (parts,) = half_step(
                functools.partial(source_kernel, log_cells), [src_out], tgts, slots, scalars, src, tgt, parts
            )
        parts = exchange(parts, SRC_PEERS)
        last = sweep == ITERS - 1
        parts, src_pot = half_step(
            functools.partial(target_kernel, log_cells),
            [(tgts, rows, TILE) if last else tgt_out, (srcs, TILE)],
            srcs,
            slots,
            scalars,
            src,
            tgt,
            parts,
            sq_src,
        )
        if last:
            other_pot = partner(src_pot)
        parts = exchange(parts, TGT_PEERS)
    tgt_pot, both = pl.pallas_call(
        functools.partial(last_kernel, log_cells),
        out_shape=[jax.ShapeDtypeStruct((rows, TILE), F32), jax.ShapeDtypeStruct((srcs, 2, TILE), F32)],
        in_specs=[SMEM] + [VMEM] * 4,
        out_specs=[VMEM] * 2,
        compiler_params=PARAMS,
    )(parity, parts, sq_tgt, src_pot, other_pot)
    return (both.reshape(-1), tgt_pot.reshape(-1))


def solution(mesh):
    fine = Mesh(mesh.devices.reshape(4, 2, 4, 4, 2), ROW + COL)
    in_specs = (P(ROW + COL, None), P(COL + ROW, None), P(ROW, COL, None, None), P(ROW, COL))
    return jax.shard_map(local, mesh=fine, in_specs=in_specs, out_specs=(P(ROW), P(COL)), check_vma=False)
```

```python
import functools
import math

import jax
import jax.numpy as jnp
from jax import lax
from jax.experimental import pallas as pl
from jax.experimental.pallas import tpu as pltpu
from jax.sharding import Mesh
from jax.sharding import PartitionSpec as P

TILE = 128
ITERS = 2
ENTROPY = 0.05
KAPPA = math.log2(math.e) / ENTROPY
EMPTY = -1e30
UNROLL = 16
ROW = ("y", "core")
COL = ("x", "s", "p")
SRC_PEERS = ("x", "s")
TGT_PEERS = ("p", "y", "core")
F32 = jnp.float32
NT = (((1,), (1,)), ((), ()))
VMEM = pl.BlockSpec(memory_space=pltpu.VMEM)
SMEM = pl.BlockSpec(memory_space=pltpu.SMEM)
PARAMS = pltpu.CompilerParams(vmem_limit_bytes=24 * 2**20)


def square_rows(cells):
    wide = cells.astype(F32)
    square = wide * wide
    high = square.astype(jnp.bfloat16)
    low = (square - high.astype(F32)).astype(jnp.bfloat16)
    ones = jnp.ones((8, cells.shape[1]), jnp.bfloat16)
    total = lax.dot_general(ones, high, NT, preferred_element_type=F32)
    total += lax.dot_general(ones, low, NT, preferred_element_type=F32)
    return total[0:1]


def log_sum(parts):
    highest = jnp.max(parts, axis=0)
    return highest + jnp.log2(jnp.sum(jnp.exp2(parts - highest[None]), axis=0))


def expand(weights, wide):
    blocks = weights.shape[0]
    columns = jnp.concatenate([weights, jnp.zeros((TILE - blocks, TILE), F32)], axis=0).T
    for n in range(blocks):
        wide[n] = jnp.broadcast_to(columns[:, n : n + 1], (TILE, TILE))


def tile_sums(tile, count, near, far, wide, peaks, totals):
    near_blocks, far_blocks = near.shape[0], far.shape[0]
    spare = near_blocks * far_blocks
    peaks[...] = jnp.full(peaks.shape, EMPTY, F32)
    totals[...] = jnp.zeros(totals.shape, F32)

    @pl.loop(0, (count + UNROLL - 1) // UNROLL)
    def _(step):
        for u in range(UNROLL):
            k = step * UNROLL + u
            n, f = tile(jnp.where(k < count, k, 0))
            inner = lax.dot_general(near[n], far[f], NT, preferred_element_type=F32)
            score = (inner * (2.0 * KAPPA) + wide[n]).reshape(TILE // 8, 8, TILE)
            peak = jnp.max(score, axis=0)
            slot = jnp.where(k < count, f * near_blocks + n, spare)
            peaks[slot] = peak
            totals[slot] = jnp.sum(jnp.exp2(score - peak[None]), axis=0)

    rows = []
    for f in range(far_blocks):
        at = pl.ds(f * near_blocks, near_blocks)
        peak = peaks[at]
        highest = jnp.max(jnp.max(peak, axis=0), axis=0, keepdims=True)
        whole = jnp.sum(totals[at] * jnp.exp2(peak - highest[None]), axis=0)
        whole = jnp.sum(whole, axis=0, keepdims=True)
        rows.append(jnp.where(whole > 0.0, highest + jnp.log2(whole), EMPTY))
    return jnp.concatenate(rows, axis=0)


def pick_kernel(mine, other, parity, picked, total):
    p = parity[0]
    targets = 8

    def scan(lists, col, start):
        def step(k, at):
            a, b = lists[0, k], lists[1, k]
            picked[at] = (a // 2) * (2 * targets) + col * targets + b
            return at + jnp.where((k < lists[2, 0]) & (a % 2 == p), 1, 0)

        return lax.fori_loop(0, TILE, step, start, unroll=8)

    total[0] = scan(other, 1 - p, scan(mine, p, 0))


def source_tiles(tiles, tgt_blocks):
    def tile(k):
        code = tiles[k]
        return lax.rem(code, tgt_blocks), lax.div(code, tgt_blocks)

    return tile


def target_tiles(tiles, tgt_blocks):
    def tile(k):
        code = tiles[k]
        return lax.div(code, tgt_blocks), lax.rem(code, tgt_blocks)

    return tile


def pack_kernel(*refs):
    for n, block in enumerate(refs[:-1]):
        refs[-1][n] = block[...]


def first_kernel(tiles, count, place, tgt_mine, tgt_other, *rest):
    sides = len(rest) - 8
    pieces, (out, src, tgt, sq_src, sq_tgt, wide, peaks, totals) = rest[:sides], rest[sides:]
    deep = pieces[0].shape[0]
    for dx, piece in enumerate(pieces):
        x = lax.rem(place[0] + (sides - dx), sides)
        for ds in range(deep):
            s = lax.rem(place[1] + (deep - ds), deep)
            src[x * deep + s] = piece[ds]
    for n in range(tgt_mine.shape[0]):
        tgt[2 * n + place[2]] = tgt_mine[n]
        tgt[2 * n + 1 - place[2]] = tgt_other[n]
    for b in range(tgt.shape[0]):
        sq_tgt[b : b + 1, :] = square_rows(tgt[b])
    for a in range(src.shape[0]):
        sq_src[a : a + 1, :] = square_rows(src[a])
    expand(sq_tgt[...] * -KAPPA, wide)
    sums = tile_sums(source_tiles(tiles, tgt.shape[0]), count[0], tgt, src, wide, peaks, totals)
    out[...] = jnp.broadcast_to(sums[None], out.shape)


def source_kernel(log_cells, tiles, count, src, tgt, parts, out, wide, peaks, totals):
    expand(-log_cells - log_sum(parts[...]), wide)
    sums = tile_sums(source_tiles(tiles, tgt.shape[0]), count[0], tgt, src, wide, peaks, totals)
    out[...] = jnp.broadcast_to(sums[None], out.shape)


def target_kernel(log_cells, tiles, count, src, tgt, parts, sq_src, out, pot, wide, peaks, totals):
    weights = -log_cells - log_sum(parts[...])
    pot[...] = weights * (1.0 / KAPPA) + sq_src[...]
    expand(weights, wide)
    sums = tile_sums(target_tiles(tiles, tgt.shape[0]), count[0], src, tgt, wide, peaks, totals)
    copies, blocks = out.shape[0], out.shape[1]
    if blocks == sums.shape[0]:
        out[...] = jnp.broadcast_to(sums[None], out.shape)
    else:
        cols = sums.shape[0] // blocks
        each = copies // cols
        for col in range(cols):
            piece = sums[col * blocks : (col + 1) * blocks]
            out[col * each : (col + 1) * each] = jnp.broadcast_to(piece[None], (each,) + piece.shape)


def last_kernel(log_cells, parity, parts, sq_tgt, mine, other, tgt_pot, src_pot):
    p = parity[0]
    blocks = tgt_pot.shape[0]
    squares = jnp.where(p == 0, sq_tgt[0:blocks], sq_tgt[blocks : 2 * blocks])
    tgt_pot[...] = (-log_cells - log_sum(parts[...])) * (1.0 / KAPPA) + squares
    src_pot[:, 0, :] = jnp.where(p == 0, mine[...], other[...])
    src_pot[:, 1, :] = jnp.where(p == 0, other[...], mine[...])


def half_step(kernel, outs, near_blocks, slots, scalars, *args):
    return pl.pallas_call(
        kernel,
        out_shape=[s if isinstance(s, jax.ShapeDtypeStruct) else jax.ShapeDtypeStruct(s, F32) for s in outs],
        in_specs=[SMEM] * len(scalars) + [VMEM] * len(args),
        out_specs=[VMEM] * len(outs),
        scratch_shapes=[
            pltpu.VMEM((near_blocks, TILE, TILE), F32),
            pltpu.VMEM((slots + 1, 8, TILE), F32),
            pltpu.VMEM((slots + 1, 8, TILE), F32),
        ],
        compiler_params=PARAMS,
    )(*scalars, *args)


def exchange(copies, peers):
    return lax.all_to_all(copies, peers, 0, 0, tiled=True)


def shifts(block, axis):
    n = lax.axis_size(axis)
    turn = lambda d: lax.ppermute(block, axis, [(i, (i + d) % n) for i in range(n)])
    return [block] + [turn(d) for d in range(1, n)]


def bands(src_embed, tgt_embed):
    receivers = lax.axis_size(("p", "y"))
    tgt = exchange(jnp.broadcast_to(tgt_embed[None], (receivers,) + tgt_embed.shape), ("p", "y"))
    blocks = shifts(src_embed, "s")
    together = pl.pallas_call(
        pack_kernel,
        out_shape=jax.ShapeDtypeStruct((len(blocks),) + src_embed.shape, src_embed.dtype),
        in_specs=[VMEM] * len(blocks),
        out_specs=VMEM,
        compiler_params=PARAMS,
    )(*blocks)
    src_pieces = shifts(together, "x")
    tgt_pieces = shifts(tgt, "core")
    return src_pieces, tgt_pieces


def local(src_embed, tgt_embed, tiles, counts):
    rows, cols = lax.axis_size(ROW), lax.axis_size(COL)
    log_cells = math.log2(rows * cols * TILE)
    parity = lax.axis_index("p").astype(jnp.int32).reshape(1)
    partner = lambda v: lax.ppermute(v, "p", [(0, 1), (1, 0)])

    lists = jnp.concatenate([tiles[0, 0], jnp.broadcast_to(counts[0, 0], (1, TILE))], axis=0)
    other_lists = partner(lists)
    src_pieces, tgt_pieces = bands(src_embed, tgt_embed)
    picked, count = pl.pallas_call(
        pick_kernel,
        out_shape=[jax.ShapeDtypeStruct((2 * TILE + UNROLL,), jnp.int32), jax.ShapeDtypeStruct((1,), jnp.int32)],
        in_specs=[SMEM] * 3,
        out_specs=[SMEM] * 2,
        compiler_params=PARAMS,
    )(lists, other_lists, parity)

    srcs, tgts = (len(pieces) * pieces[0].shape[0] for pieces in (src_pieces, tgt_pieces))
    src_shape = jax.ShapeDtypeStruct((srcs,) + src_embed.shape, src_embed.dtype)
    tgt_shape = jax.ShapeDtypeStruct((tgts,) + tgt_embed.shape, tgt_embed.dtype)
    scalars = (picked, count)
    place = jnp.stack([lax.axis_index(a) for a in ("x", "s", "core")]).astype(jnp.int32)
    slots = srcs * tgts
    src_out, tgt_out = (srcs, srcs, TILE), (tgts, tgts, TILE)
    for sweep in range(ITERS):
        if sweep == 0:
            parts, src, tgt, sq_src, sq_tgt = half_step(
                first_kernel,
                [src_out, src_shape, tgt_shape, (srcs, TILE), (tgts, TILE)],
                tgts,
                slots,
                scalars + (place,),
                *tgt_pieces,
                *src_pieces,
            )
        else:
            (parts,) = half_step(
                functools.partial(source_kernel, log_cells), [src_out], tgts, slots, scalars, src, tgt, parts
            )
        parts = exchange(parts, SRC_PEERS)
        last = sweep == ITERS - 1
        parts, src_pot = half_step(
            functools.partial(target_kernel, log_cells),
            [(tgts, rows, TILE) if last else tgt_out, (srcs, TILE)],
            srcs,
            slots,
            scalars,
            src,
            tgt,
            parts,
            sq_src,
        )
        if last:
            other_pot = partner(src_pot)
        parts = exchange(parts, TGT_PEERS)
    tgt_pot, both = pl.pallas_call(
        functools.partial(last_kernel, log_cells),
        out_shape=[jax.ShapeDtypeStruct((rows, TILE), F32), jax.ShapeDtypeStruct((srcs, 2, TILE), F32)],
        in_specs=[SMEM] + [VMEM] * 4,
        out_specs=[VMEM] * 2,
        compiler_params=PARAMS,
    )(parity, parts, sq_tgt, src_pot, other_pot)
    return (both.reshape(-1), tgt_pot.reshape(-1))


def solution(mesh):
    fine = Mesh(mesh.devices.reshape(4, 2, 4, 4, 2), ROW + COL)
    in_specs = (P(ROW + COL, None), P(COL + ROW, None), P(ROW, COL, None, None), P(ROW, COL))
    return jax.shard_map(local, mesh=fine, in_specs=in_specs, out_specs=(P(ROW), P(COL)), check_vma=False)
```

```python
import functools
import math

import jax
import jax.numpy as jnp
from jax import lax
from jax.experimental import pallas as pl
from jax.experimental.pallas import tpu as pltpu
from jax.sharding import Mesh
from jax.sharding import PartitionSpec as P

TILE = 128
ITERS = 2
ENTROPY = 0.05
KAPPA = math.log2(math.e) / ENTROPY
EMPTY = -1e30
UNROLL = 16
ROW = ("y", "core")
COL = ("x", "s", "p")
SRC_PEERS = ("x", "s")
TGT_PEERS = ("p", "y", "core")
F32 = jnp.float32
NT = (((1,), (1,)), ((), ()))
VMEM = pl.BlockSpec(memory_space=pltpu.VMEM)
SMEM = pl.BlockSpec(memory_space=pltpu.SMEM)
PARAMS = pltpu.CompilerParams(vmem_limit_bytes=24 * 2**20)


def square_rows(cells):
    wide = cells.astype(F32)
    square = wide * wide
    high = square.astype(jnp.bfloat16)
    low = (square - high.astype(F32)).astype(jnp.bfloat16)
    ones = jnp.ones((8, cells.shape[1]), jnp.bfloat16)
    total = lax.dot_general(ones, high, NT, preferred_element_type=F32)
    total += lax.dot_general(ones, low, NT, preferred_element_type=F32)
    return total[0:1]


def log_sum(parts):
    highest = jnp.max(parts, axis=0)
    return highest + jnp.log2(jnp.sum(jnp.exp2(parts - highest[None]), axis=0))


def expand(weights, wide):
    blocks = weights.shape[0]
    columns = jnp.concatenate([weights, jnp.zeros((TILE - blocks, TILE), F32)], axis=0).T
    for n in range(blocks):
        wide[n] = jnp.broadcast_to(columns[:, n : n + 1], (TILE, TILE))


def tile_sums(tile, count, near, far, wide, peaks, totals):
    near_blocks, far_blocks = near.shape[0], far.shape[0]
    spare = near_blocks * far_blocks
    peaks[...] = jnp.full(peaks.shape, EMPTY, F32)
    totals[...] = jnp.zeros(totals.shape, F32)

    @pl.loop(0, (count + UNROLL - 1) // UNROLL)
    def _(step):
        for u in range(UNROLL):
            k = step * UNROLL + u
            n, f = tile(jnp.where(k < count, k, 0))
            inner = lax.dot_general(near[n], far[f], NT, preferred_element_type=F32)
            score = (inner * (2.0 * KAPPA) + wide[n]).reshape(TILE // 8, 8, TILE)
            peak = jnp.max(score, axis=0)
            slot = jnp.where(k < count, f * near_blocks + n, spare)
            peaks[slot] = peak
            totals[slot] = jnp.sum(jnp.exp2(score - peak[None]), axis=0)

    rows = []
    for f in range(far_blocks):
        at = pl.ds(f * near_blocks, near_blocks)
        peak = peaks[at]
        highest = jnp.max(jnp.max(peak, axis=0), axis=0, keepdims=True)
        whole = jnp.sum(totals[at] * jnp.exp2(peak - highest[None]), axis=0)
        whole = jnp.sum(whole, axis=0, keepdims=True)
        rows.append(jnp.where(whole > 0.0, highest + jnp.log2(whole), EMPTY))
    return jnp.concatenate(rows, axis=0)


def pick_kernel(mine, other, parity, picked, total):
    p = parity[0]
    targets = 8

    def scan(lists, col, start):
        def step(k, at):
            a, b = lists[0, k], lists[1, k]
            picked[at] = (a // 2) * (2 * targets) + col * targets + b
            return at + jnp.where((k < lists[2, 0]) & (a % 2 == p), 1, 0)

        return lax.fori_loop(0, TILE, step, start, unroll=8)

    total[0] = scan(other, 1 - p, scan(mine, p, 0))


def source_tiles(tiles, tgt_blocks):
    def tile(k):
        code = tiles[k]
        return lax.rem(code, tgt_blocks), lax.div(code, tgt_blocks)

    return tile


def target_tiles(tiles, tgt_blocks):
    def tile(k):
        code = tiles[k]
        return lax.div(code, tgt_blocks), lax.rem(code, tgt_blocks)

    return tile


def pack_kernel(*refs):
    blocks = refs[0].shape[0]
    for n, piece in enumerate(refs[:-1]):
        refs[-1][n * blocks : (n + 1) * blocks] = piece[...]


def first_kernel(tiles, count, place, tgt_mine, tgt_other, *rest):
    sides = len(rest) - 8
    pieces, (out, src, tgt, sq_src, sq_tgt, wide, peaks, totals) = rest[:sides], rest[sides:]
    deep = pieces[0].shape[0]
    for dx, piece in enumerate(pieces):
        x = lax.rem(place[0] + (sides - dx), sides)
        for ds in range(deep):
            s = lax.rem(place[1] + (deep - ds), deep)
            src[x * deep + s] = piece[ds]
    far = 4
    for n in range(tgt_mine.shape[0]):
        y = lax.rem(place[2] + (far - n // 2), far)
        p = lax.rem(place[3] + n % 2, 2)
        at = p * (2 * far) + 2 * y
        tgt[at + place[4]] = tgt_mine[n]
        tgt[at + 1 - place[4]] = tgt_other[n]
    for b in range(tgt.shape[0]):
        sq_tgt[b : b + 1, :] = square_rows(tgt[b])
    for a in range(src.shape[0]):
        sq_src[a : a + 1, :] = square_rows(src[a])
    expand(sq_tgt[...] * -KAPPA, wide)
    sums = tile_sums(source_tiles(tiles, tgt.shape[0]), count[0], tgt, src, wide, peaks, totals)
    out[...] = jnp.broadcast_to(sums[None], out.shape)


def source_kernel(log_cells, tiles, count, src, tgt, parts, out, wide, peaks, totals):
    expand(-log_cells - log_sum(parts[...]), wide)
    sums = tile_sums(source_tiles(tiles, tgt.shape[0]), count[0], tgt, src, wide, peaks, totals)
    out[...] = jnp.broadcast_to(sums[None], out.shape)


def target_kernel(log_cells, tiles, count, src, tgt, parts, sq_src, out, pot, wide, peaks, totals):
    weights = -log_cells - log_sum(parts[...])
    pot[...] = weights * (1.0 / KAPPA) + sq_src[...]
    expand(weights, wide)
    sums = tile_sums(target_tiles(tiles, tgt.shape[0]), count[0], src, tgt, wide, peaks, totals)
    copies, blocks = out.shape[0], out.shape[1]
    if blocks == sums.shape[0]:
        out[...] = jnp.broadcast_to(sums[None], out.shape)
    else:
        cols = sums.shape[0] // blocks
        each = copies // cols
        for col in range(cols):
            piece = sums[col * blocks : (col + 1) * blocks]
            out[col * each : (col + 1) * each] = jnp.broadcast_to(piece[None], (each,) + piece.shape)


def last_kernel(log_cells, parity, parts, sq_tgt, mine, other, tgt_pot, src_pot):
    p = parity[0]
    blocks = tgt_pot.shape[0]
    squares = jnp.where(p == 0, sq_tgt[0:blocks], sq_tgt[blocks : 2 * blocks])
    tgt_pot[...] = (-log_cells - log_sum(parts[...])) * (1.0 / KAPPA) + squares
    src_pot[:, 0, :] = jnp.where(p == 0, mine[...], other[...])
    src_pot[:, 1, :] = jnp.where(p == 0, other[...], mine[...])


def half_step(kernel, outs, near_blocks, slots, scalars, *args):
    return pl.pallas_call(
        kernel,
        out_shape=[s if isinstance(s, jax.ShapeDtypeStruct) else jax.ShapeDtypeStruct(s, F32) for s in outs],
        in_specs=[SMEM] * len(scalars) + [VMEM] * len(args),
        out_specs=[VMEM] * len(outs),
        scratch_shapes=[
            pltpu.VMEM((near_blocks, TILE, TILE), F32),
            pltpu.VMEM((slots + 1, 8, TILE), F32),
            pltpu.VMEM((slots + 1, 8, TILE), F32),
        ],
        compiler_params=PARAMS,
    )(*scalars, *args)


def exchange(copies, peers):
    return lax.all_to_all(copies, peers, 0, 0, tiled=True)


def shifts(block, axis):
    n = lax.axis_size(axis)
    turn = lambda d: lax.ppermute(block, axis, [(i, (i + d) % n) for i in range(n)])
    return [block] + [turn(d) for d in range(1, n)]


def pack(pieces):
    blocks, rows, width = pieces[0].shape
    return pl.pallas_call(
        pack_kernel,
        out_shape=jax.ShapeDtypeStruct((len(pieces) * blocks, rows, width), pieces[0].dtype),
        in_specs=[VMEM] * len(pieces),
        out_specs=VMEM,
        compiler_params=PARAMS,
    )(*pieces)


def bands(src_embed, tgt_embed):
    src_pieces = shifts(pack(shifts(src_embed[None], "s")), "x")
    tgt_pieces = shifts(pack(shifts(pack(shifts(tgt_embed[None], "p")), "y")), "core")
    return src_pieces, tgt_pieces


def local(src_embed, tgt_embed, tiles, counts):
    rows, cols = lax.axis_size(ROW), lax.axis_size(COL)
    log_cells = math.log2(rows * cols * TILE)
    parity = lax.axis_index("p").astype(jnp.int32).reshape(1)
    partner = lambda v: lax.ppermute(v, "p", [(0, 1), (1, 0)])

    lists = jnp.concatenate([tiles[0, 0], jnp.broadcast_to(counts[0, 0], (1, TILE))], axis=0)
    other_lists = partner(lists)
    src_pieces, tgt_pieces = bands(src_embed, tgt_embed)
    picked, count = pl.pallas_call(
        pick_kernel,
        out_shape=[jax.ShapeDtypeStruct((2 * TILE + UNROLL,), jnp.int32), jax.ShapeDtypeStruct((1,), jnp.int32)],
        in_specs=[SMEM] * 3,
        out_specs=[SMEM] * 2,
        compiler_params=PARAMS,
    )(lists, other_lists, parity)

    srcs, tgts = (len(pieces) * pieces[0].shape[0] for pieces in (src_pieces, tgt_pieces))
    src_shape = jax.ShapeDtypeStruct((srcs,) + src_embed.shape, src_embed.dtype)
    tgt_shape = jax.ShapeDtypeStruct((tgts,) + tgt_embed.shape, tgt_embed.dtype)
    scalars = (picked, count)
    place = jnp.stack([lax.axis_index(a) for a in ("x", "s", "y", "p", "core")]).astype(jnp.int32)
    slots = srcs * tgts
    src_out, tgt_out = (srcs, srcs, TILE), (tgts, tgts, TILE)
    for sweep in range(ITERS):
        if sweep == 0:
            parts, src, tgt, sq_src, sq_tgt = half_step(
                first_kernel,
                [src_out, src_shape, tgt_shape, (srcs, TILE), (tgts, TILE)],
                tgts,
                slots,
                scalars + (place,),
                *tgt_pieces,
                *src_pieces,
            )
        else:
            (parts,) = half_step(
                functools.partial(source_kernel, log_cells), [src_out], tgts, slots, scalars, src, tgt, parts
            )
        parts = exchange(parts, SRC_PEERS)
        last = sweep == ITERS - 1
        parts, src_pot = half_step(
            functools.partial(target_kernel, log_cells),
            [(tgts, rows, TILE) if last else tgt_out, (srcs, TILE)],
            srcs,
            slots,
            scalars,
            src,
            tgt,
            parts,
            sq_src,
        )
        if last:
            other_pot = partner(src_pot)
        parts = exchange(parts, TGT_PEERS)
    tgt_pot, both = pl.pallas_call(
        functools.partial(last_kernel, log_cells),
        out_shape=[jax.ShapeDtypeStruct((rows, TILE), F32), jax.ShapeDtypeStruct((srcs, 2, TILE), F32)],
        in_specs=[SMEM] + [VMEM] * 4,
        out_specs=[VMEM] * 2,
        compiler_params=PARAMS,
    )(parity, parts, sq_tgt, src_pot, other_pot)
    return (both.reshape(-1), tgt_pot.reshape(-1))


def solution(mesh):
    fine = Mesh(mesh.devices.reshape(4, 2, 4, 4, 2), ROW + COL)
    in_specs = (P(ROW + COL, None), P(COL + ROW, None), P(ROW, COL, None, None), P(ROW, COL))
    return jax.shard_map(local, mesh=fine, in_specs=in_specs, out_specs=(P(ROW), P(COL)), check_vma=False)
```

```python
import functools
import math

import jax
import jax.numpy as jnp
from jax import lax
from jax.experimental import pallas as pl
from jax.experimental.pallas import tpu as pltpu
from jax.sharding import Mesh
from jax.sharding import PartitionSpec as P

TILE = 128
ITERS = 2
ENTROPY = 0.05
KAPPA = math.log2(math.e) / ENTROPY
EMPTY = -1e30
UNROLL = 16
ROW = ("y", "core")
COL = ("x", "s", "p")
SRC_PEERS = ("x", "s")
TGT_PEERS = ("p", "y", "core")
F32 = jnp.float32
NT = (((1,), (1,)), ((), ()))
VMEM = pl.BlockSpec(memory_space=pltpu.VMEM)
SMEM = pl.BlockSpec(memory_space=pltpu.SMEM)
PARAMS = pltpu.CompilerParams(vmem_limit_bytes=24 * 2**20)


def square_rows(cells):
    wide = cells.astype(F32)
    square = wide * wide
    high = square.astype(jnp.bfloat16)
    low = (square - high.astype(F32)).astype(jnp.bfloat16)
    ones = jnp.ones((8, cells.shape[1]), jnp.bfloat16)
    total = lax.dot_general(ones, high, NT, preferred_element_type=F32)
    total += lax.dot_general(ones, low, NT, preferred_element_type=F32)
    return total[0:1]


def log_sum(parts):
    highest = jnp.max(parts, axis=0)
    return highest + jnp.log2(jnp.sum(jnp.exp2(parts - highest[None]), axis=0))


def expand(weights, wide):
    blocks = weights.shape[0]
    columns = jnp.concatenate([weights, jnp.zeros((TILE - blocks, TILE), F32)], axis=0).T
    for n in range(blocks):
        wide[n] = jnp.broadcast_to(columns[:, n : n + 1], (TILE, TILE))


def tile_sums(tile, count, near, far, wide, peaks, totals):
    near_blocks, far_blocks = near.shape[0], far.shape[0]
    spare = near_blocks * far_blocks
    peaks[...] = jnp.full(peaks.shape, EMPTY, F32)
    totals[...] = jnp.zeros(totals.shape, F32)

    @pl.loop(0, (count + UNROLL - 1) // UNROLL)
    def _(step):
        for u in range(UNROLL):
            k = step * UNROLL + u
            n, f = tile(jnp.where(k < count, k, 0))
            inner = lax.dot_general(near[n], far[f], NT, preferred_element_type=F32)
            score = (inner * (2.0 * KAPPA) + wide[n]).reshape(TILE // 8, 8, TILE)
            peak = jnp.max(score, axis=0)
            slot = jnp.where(k < count, f * near_blocks + n, spare)
            peaks[slot] = peak
            totals[slot] = jnp.sum(jnp.exp2(score - peak[None]), axis=0)

    rows = []
    for f in range(far_blocks):
        at = pl.ds(f * near_blocks, near_blocks)
        peak = peaks[at]
        highest = jnp.max(jnp.max(peak, axis=0), axis=0, keepdims=True)
        whole = jnp.sum(totals[at] * jnp.exp2(peak - highest[None]), axis=0)
        whole = jnp.sum(whole, axis=0, keepdims=True)
        rows.append(jnp.where(whole > 0.0, highest + jnp.log2(whole), EMPTY))
    return jnp.concatenate(rows, axis=0)


def pick_kernel(mine, other, parity, picked, total):
    p = parity[0]
    targets = 8

    def scan(lists, col, start):
        def step(k, at):
            a, b = lists[0, k], lists[1, k]
            picked[at] = (a // 2) * (2 * targets) + col * targets + b
            return at + jnp.where((k < lists[2, 0]) & (a % 2 == p), 1, 0)

        return lax.fori_loop(0, TILE, step, start, unroll=8)

    total[0] = scan(other, 1 - p, scan(mine, p, 0))


def source_tiles(tiles, tgt_blocks):
    def tile(k):
        code = tiles[k]
        return lax.rem(code, tgt_blocks), lax.div(code, tgt_blocks)

    return tile


def target_tiles(tiles, tgt_blocks):
    def tile(k):
        code = tiles[k]
        return lax.div(code, tgt_blocks), lax.rem(code, tgt_blocks)

    return tile


def pack_kernel(srcs, *refs):
    src, tgt = refs[-2:]
    for n in range(srcs):
        src[n] = refs[n][...]
    for n in range(len(refs) - 2 - srcs):
        tgt[n] = refs[srcs + n][...]


def first_kernel(tiles, count, place, *refs):
    pieces, (out, src, tgt, sq_src, sq_tgt, wide, peaks, totals) = refs[:-8], refs[-8:]
    sides = len(pieces) // 2
    for d in range(sides):
        x, y = (lax.rem(place[axis] + (sides - d), sides) for axis in (0, 2))
        for n in range(pieces[d].shape[0]):
            s = lax.rem(place[1] + (sides - n), sides)
            src[x * sides + s] = pieces[d][n]
        for n in range(pieces[sides + d].shape[0]):
            p, core = place[3] ^ (n % 2), place[4] ^ (n // 2)
            tgt[p * (2 * sides) + 2 * y + core] = pieces[sides + d][n]
    for b in range(tgt.shape[0]):
        sq_tgt[b : b + 1, :] = square_rows(tgt[b])
    for a in range(src.shape[0]):
        sq_src[a : a + 1, :] = square_rows(src[a])
    expand(sq_tgt[...] * -KAPPA, wide)
    sums = tile_sums(source_tiles(tiles, tgt.shape[0]), count[0], tgt, src, wide, peaks, totals)
    out[...] = jnp.broadcast_to(sums[None], out.shape)


def source_kernel(log_cells, tiles, count, src, tgt, parts, out, wide, peaks, totals):
    expand(-log_cells - log_sum(parts[...]), wide)
    sums = tile_sums(source_tiles(tiles, tgt.shape[0]), count[0], tgt, src, wide, peaks, totals)
    out[...] = jnp.broadcast_to(sums[None], out.shape)


def target_kernel(log_cells, tiles, count, src, tgt, parts, sq_src, out, pot, wide, peaks, totals):
    weights = -log_cells - log_sum(parts[...])
    pot[...] = weights * (1.0 / KAPPA) + sq_src[...]
    expand(weights, wide)
    sums = tile_sums(target_tiles(tiles, tgt.shape[0]), count[0], src, tgt, wide, peaks, totals)
    copies, blocks = out.shape[0], out.shape[1]
    if blocks == sums.shape[0]:
        out[...] = jnp.broadcast_to(sums[None], out.shape)
    else:
        cols = sums.shape[0] // blocks
        each = copies // cols
        for col in range(cols):
            piece = sums[col * blocks : (col + 1) * blocks]
            out[col * each : (col + 1) * each] = jnp.broadcast_to(piece[None], (each,) + piece.shape)


def last_kernel(log_cells, parity, parts, sq_tgt, mine, other, tgt_pot, src_pot):
    p = parity[0]
    blocks = tgt_pot.shape[0]
    squares = jnp.where(p == 0, sq_tgt[0:blocks], sq_tgt[blocks : 2 * blocks])
    tgt_pot[...] = (-log_cells - log_sum(parts[...])) * (1.0 / KAPPA) + squares
    src_pot[:, 0, :] = jnp.where(p == 0, mine[...], other[...])
    src_pot[:, 1, :] = jnp.where(p == 0, other[...], mine[...])


def half_step(kernel, outs, near_blocks, slots, scalars, *args):
    return pl.pallas_call(
        kernel,
        out_shape=[s if isinstance(s, jax.ShapeDtypeStruct) else jax.ShapeDtypeStruct(s, F32) for s in outs],
        in_specs=[SMEM] * len(scalars) + [VMEM] * len(args),
        out_specs=[VMEM] * len(outs),
        scratch_shapes=[
            pltpu.VMEM((near_blocks, TILE, TILE), F32),
            pltpu.VMEM((slots + 1, 8, TILE), F32),
            pltpu.VMEM((slots + 1, 8, TILE), F32),
        ],
        compiler_params=PARAMS,
    )(*scalars, *args)


def exchange(copies, peers):
    return lax.all_to_all(copies, peers, 0, 0, tiled=True)


def shifts(block, axis):
    n = lax.axis_size(axis)
    turn = lambda d: lax.ppermute(block, axis, [(i, (i + d) % n) for i in range(n)])
    return [block] + [turn(d) for d in range(1, n)]


def swaps(block, axes):
    n = lax.axis_size(axes)
    return [block] + [lax.ppermute(block, axes, [(i, i ^ d) for i in range(n)]) for d in range(1, n)]


def bands(src_embed, tgt_embed):
    src_blocks, tgt_blocks = shifts(src_embed, "s"), swaps(tgt_embed, ("core", "p"))
    blocks = src_blocks + tgt_blocks
    src, tgt = pl.pallas_call(
        functools.partial(pack_kernel, len(src_blocks)),
        out_shape=[
            jax.ShapeDtypeStruct((len(group),) + group[0].shape, group[0].dtype) for group in (src_blocks, tgt_blocks)
        ],
        in_specs=[VMEM] * len(blocks),
        out_specs=[VMEM] * 2,
        compiler_params=PARAMS,
    )(*blocks)
    return shifts(src, "x"), shifts(tgt, "y")


def local(src_embed, tgt_embed, tiles, counts):
    rows, cols = lax.axis_size(ROW), lax.axis_size(COL)
    log_cells = math.log2(rows * cols * TILE)
    parity = lax.axis_index("p").astype(jnp.int32).reshape(1)
    partner = lambda v: lax.ppermute(v, "p", [(0, 1), (1, 0)])

    lists = jnp.concatenate([tiles[0, 0], jnp.broadcast_to(counts[0, 0], (1, TILE))], axis=0)
    other_lists = partner(lists)
    src_pieces, tgt_pieces = bands(src_embed, tgt_embed)
    picked, count = pl.pallas_call(
        pick_kernel,
        out_shape=[jax.ShapeDtypeStruct((2 * TILE + UNROLL,), jnp.int32), jax.ShapeDtypeStruct((1,), jnp.int32)],
        in_specs=[SMEM] * 3,
        out_specs=[SMEM] * 2,
        compiler_params=PARAMS,
    )(lists, other_lists, parity)

    srcs, tgts = (len(pieces) * pieces[0].shape[0] for pieces in (src_pieces, tgt_pieces))
    src_shape = jax.ShapeDtypeStruct((srcs,) + src_embed.shape, src_embed.dtype)
    tgt_shape = jax.ShapeDtypeStruct((tgts,) + tgt_embed.shape, tgt_embed.dtype)
    scalars = (picked, count)
    place = jnp.stack([lax.axis_index(a) for a in ("x", "s", "y", "p", "core")]).astype(jnp.int32)
    slots = srcs * tgts
    src_out, tgt_out = (srcs, srcs, TILE), (tgts, tgts, TILE)
    for sweep in range(ITERS):
        if sweep == 0:
            parts, src, tgt, sq_src, sq_tgt = half_step(
                first_kernel,
                [src_out, src_shape, tgt_shape, (srcs, TILE), (tgts, TILE)],
                tgts,
                slots,
                scalars + (place,),
                *src_pieces,
                *tgt_pieces,
            )
        else:
            (parts,) = half_step(
                functools.partial(source_kernel, log_cells), [src_out], tgts, slots, scalars, src, tgt, parts
            )
        parts = exchange(parts, SRC_PEERS)
        last = sweep == ITERS - 1
        parts, src_pot = half_step(
            functools.partial(target_kernel, log_cells),
            [(tgts, rows, TILE) if last else tgt_out, (srcs, TILE)],
            srcs,
            slots,
            scalars,
            src,
            tgt,
            parts,
            sq_src,
        )
        if last:
            other_pot = partner(src_pot)
        parts = exchange(parts, TGT_PEERS)
    tgt_pot, both = pl.pallas_call(
        functools.partial(last_kernel, log_cells),
        out_shape=[jax.ShapeDtypeStruct((rows, TILE), F32), jax.ShapeDtypeStruct((srcs, 2, TILE), F32)],
        in_specs=[SMEM] + [VMEM] * 4,
        out_specs=[VMEM] * 2,
        compiler_params=PARAMS,
    )(parity, parts, sq_tgt, src_pot, other_pot)
    return (both.reshape(-1), tgt_pot.reshape(-1))


def solution(mesh):
    fine = Mesh(mesh.devices.reshape(4, 2, 4, 4, 2), ROW + COL)
    in_specs = (P(ROW + COL, None), P(COL + ROW, None), P(ROW, COL, None, None), P(ROW, COL))
    return jax.shard_map(local, mesh=fine, in_specs=in_specs, out_specs=(P(ROW), P(COL)), check_vma=False)
```

```python
import functools
import math

import jax
import jax.numpy as jnp
from jax import lax
from jax.experimental import pallas as pl
from jax.experimental.pallas import tpu as pltpu
from jax.sharding import Mesh
from jax.sharding import PartitionSpec as P

TILE = 128
ITERS = 2
ENTROPY = 0.05
KAPPA = math.log2(math.e) / ENTROPY
EMPTY = -1e30
UNROLL = 16
ROW = ("y", "core")
COL = ("x", "s", "p")
SRC_PEERS = ("x", "s")
TGT_PEERS = ("p", "y", "core")
F32 = jnp.float32
NT = (((1,), (1,)), ((), ()))
VMEM = pl.BlockSpec(memory_space=pltpu.VMEM)
SMEM = pl.BlockSpec(memory_space=pltpu.SMEM)
PARAMS = pltpu.CompilerParams(vmem_limit_bytes=24 * 2**20)


def square_rows(cells):
    wide = cells.astype(F32)
    square = wide * wide
    high = square.astype(jnp.bfloat16)
    low = (square - high.astype(F32)).astype(jnp.bfloat16)
    ones = jnp.ones((8, cells.shape[1]), jnp.bfloat16)
    total = lax.dot_general(ones, high, NT, preferred_element_type=F32)
    total += lax.dot_general(ones, low, NT, preferred_element_type=F32)
    return total[0:1]


def log_sum(parts):
    highest = jnp.max(parts, axis=0)
    return highest + jnp.log2(jnp.sum(jnp.exp2(parts - highest[None]), axis=0))


def expand(weights, wide):
    blocks = weights.shape[0]
    columns = jnp.concatenate([weights, jnp.zeros((TILE - blocks, TILE), F32)], axis=0).T
    for n in range(blocks):
        wide[n] = jnp.broadcast_to(columns[:, n : n + 1], (TILE, TILE))


def tile_sums(tile, count, near, far, wide, peaks, totals):
    near_blocks, far_blocks = near.shape[0], far.shape[0]
    spare = near_blocks * far_blocks
    peaks[...] = jnp.full(peaks.shape, EMPTY, F32)
    totals[...] = jnp.zeros(totals.shape, F32)

    @pl.loop(0, (count + UNROLL - 1) // UNROLL)
    def _(step):
        for u in range(UNROLL):
            k = step * UNROLL + u
            n, f = tile(jnp.where(k < count, k, 0))
            inner = lax.dot_general(near[n], far[f], NT, preferred_element_type=F32)
            score = (inner * (2.0 * KAPPA) + wide[n]).reshape(TILE // 8, 8, TILE)
            peak = jnp.max(score, axis=0)
            slot = jnp.where(k < count, f * near_blocks + n, spare)
            peaks[slot] = peak
            totals[slot] = jnp.sum(jnp.exp2(score - peak[None]), axis=0)

    rows = []
    for f in range(far_blocks):
        at = pl.ds(f * near_blocks, near_blocks)
        peak = peaks[at]
        highest = jnp.max(jnp.max(peak, axis=0), axis=0, keepdims=True)
        whole = jnp.sum(totals[at] * jnp.exp2(peak - highest[None]), axis=0)
        whole = jnp.sum(whole, axis=0, keepdims=True)
        rows.append(jnp.where(whole > 0.0, highest + jnp.log2(whole), EMPTY))
    return jnp.concatenate(rows, axis=0)


def pick_kernel(mine, other, parity, picked, total):
    p = parity[0]
    targets = 8

    def scan(lists, col, start):
        def step(k, at):
            a, b = lists[0, k], lists[1, k]
            picked[at] = (a // 2) * (2 * targets) + col * targets + b
            return at + jnp.where((k < lists[2, 0]) & (a % 2 == p), 1, 0)

        return lax.fori_loop(0, TILE, step, start, unroll=8)

    total[0] = scan(other, 1 - p, scan(mine, p, 0))


def source_tiles(tiles, tgt_blocks):
    def tile(k):
        code = tiles[k]
        return lax.rem(code, tgt_blocks), lax.div(code, tgt_blocks)

    return tile


def target_tiles(tiles, tgt_blocks):
    def tile(k):
        code = tiles[k]
        return lax.div(code, tgt_blocks), lax.rem(code, tgt_blocks)

    return tile


def pack_kernel(src_mine, tgt_mine, lists, *refs):
    src, tgt, sems = refs[-3:]
    sides = src.shape[0] - 1
    copies = [
        pltpu.make_async_copy(src_mine, src.at[0], sems.at[0]),
        pltpu.make_async_copy(tgt_mine, tgt.at[0], sems.at[1]),
    ]
    for copy in copies:
        copy.start()
    for n in range(sides):
        src[n + 1] = refs[n][...]
    for n in range(tgt.shape[0] - 1):
        tgt[n + 1] = refs[sides + n][...]
    for copy in copies:
        copy.wait()


def first_kernel(tiles, count, place, *refs):
    pieces, (out, src, tgt, sq_src, sq_tgt, wide, peaks, totals) = refs[:-8], refs[-8:]
    sides = len(pieces) // 2
    for d in range(sides):
        x = lax.rem(place[0] + (sides - d), sides)
        core, p = place[4] ^ (d // 2), place[3] ^ (d % 2)
        for n in range(sides):
            s, y = (lax.rem(place[axis] + (sides - n), sides) for axis in (1, 2))
            src[x * sides + s] = pieces[d][n]
            tgt[p * (2 * sides) + 2 * y + core] = pieces[sides + d][n]
    for b in range(tgt.shape[0]):
        sq_tgt[b : b + 1, :] = square_rows(tgt[b])
    for a in range(src.shape[0]):
        sq_src[a : a + 1, :] = square_rows(src[a])
    expand(sq_tgt[...] * -KAPPA, wide)
    sums = tile_sums(source_tiles(tiles, tgt.shape[0]), count[0], tgt, src, wide, peaks, totals)
    out[...] = jnp.broadcast_to(sums[None], out.shape)


def source_kernel(log_cells, tiles, count, src, tgt, parts, out, wide, peaks, totals):
    expand(-log_cells - log_sum(parts[...]), wide)
    sums = tile_sums(source_tiles(tiles, tgt.shape[0]), count[0], tgt, src, wide, peaks, totals)
    out[...] = jnp.broadcast_to(sums[None], out.shape)


def target_kernel(log_cells, tiles, count, src, tgt, parts, sq_src, out, pot, wide, peaks, totals):
    weights = -log_cells - log_sum(parts[...])
    pot[...] = weights * (1.0 / KAPPA) + sq_src[...]
    expand(weights, wide)
    sums = tile_sums(target_tiles(tiles, tgt.shape[0]), count[0], src, tgt, wide, peaks, totals)
    copies, blocks = out.shape[0], out.shape[1]
    if blocks == sums.shape[0]:
        out[...] = jnp.broadcast_to(sums[None], out.shape)
    else:
        cols = sums.shape[0] // blocks
        each = copies // cols
        for col in range(cols):
            piece = sums[col * blocks : (col + 1) * blocks]
            out[col * each : (col + 1) * each] = jnp.broadcast_to(piece[None], (each,) + piece.shape)


def last_kernel(log_cells, parity, parts, sq_tgt, mine, other, tgt_pot, src_pot):
    p = parity[0]
    blocks = tgt_pot.shape[0]
    squares = jnp.where(p == 0, sq_tgt[0:blocks], sq_tgt[blocks : 2 * blocks])
    tgt_pot[...] = (-log_cells - log_sum(parts[...])) * (1.0 / KAPPA) + squares
    src_pot[:, 0, :] = jnp.where(p == 0, mine[...], other[...])
    src_pot[:, 1, :] = jnp.where(p == 0, other[...], mine[...])


def half_step(kernel, outs, near_blocks, slots, scalars, *args):
    return pl.pallas_call(
        kernel,
        out_shape=[s if isinstance(s, jax.ShapeDtypeStruct) else jax.ShapeDtypeStruct(s, F32) for s in outs],
        in_specs=[SMEM] * len(scalars) + [VMEM] * len(args),
        out_specs=[VMEM] * len(outs),
        scratch_shapes=[
            pltpu.VMEM((near_blocks, TILE, TILE), F32),
            pltpu.VMEM((slots + 1, 8, TILE), F32),
            pltpu.VMEM((slots + 1, 8, TILE), F32),
        ],
        compiler_params=PARAMS,
    )(*scalars, *args)


def exchange(copies, peers):
    return lax.all_to_all(copies, peers, 0, 0, tiled=True)


def shifts(block, axis):
    n = lax.axis_size(axis)
    turn = lambda d: lax.ppermute(block, axis, [(i, (i + d) % n) for i in range(n)])
    return [block] + [turn(d) for d in range(1, n)]


def swaps(block, axes):
    n = lax.axis_size(axes)
    return [block] + [lax.ppermute(block, axes, [(i, i ^ d) for i in range(n)]) for d in range(1, n)]


def bands(src_embed, tgt_embed, lists):
    src_blocks, tgt_blocks = shifts(src_embed, "s"), shifts(tgt_embed, "y")
    far = src_blocks[1:] + tgt_blocks[1:]
    src, tgt = pl.pallas_call(
        pack_kernel,
        out_shape=[
            jax.ShapeDtypeStruct((len(group),) + group[0].shape, group[0].dtype) for group in (src_blocks, tgt_blocks)
        ],
        in_specs=[pl.BlockSpec(memory_space=pl.ANY)] * 3 + [VMEM] * len(far),
        out_specs=[VMEM] * 2,
        scratch_shapes=[pltpu.SemaphoreType.DMA((2,))],
        compiler_params=PARAMS,
    )(src_embed, tgt_embed, lists, *far)
    return shifts(src, "x"), swaps(tgt, ("core", "p"))


def local(src_embed, tgt_embed, tiles, counts):
    rows, cols = lax.axis_size(ROW), lax.axis_size(COL)
    log_cells = math.log2(rows * cols * TILE)
    parity = lax.axis_index("p").astype(jnp.int32).reshape(1)
    partner = lambda v: lax.ppermute(v, "p", [(0, 1), (1, 0)])

    lists = jnp.concatenate([tiles[0, 0], jnp.broadcast_to(counts[0, 0], (1, TILE))], axis=0)
    other_lists = partner(lists)
    src_pieces, tgt_pieces = bands(src_embed, tgt_embed, other_lists)
    picked, count = pl.pallas_call(
        pick_kernel,
        out_shape=[jax.ShapeDtypeStruct((2 * TILE + UNROLL,), jnp.int32), jax.ShapeDtypeStruct((1,), jnp.int32)],
        in_specs=[SMEM] * 3,
        out_specs=[SMEM] * 2,
        compiler_params=PARAMS,
    )(lists, other_lists, parity)

    srcs, tgts = (len(pieces) * pieces[0].shape[0] for pieces in (src_pieces, tgt_pieces))
    src_shape = jax.ShapeDtypeStruct((srcs,) + src_embed.shape, src_embed.dtype)
    tgt_shape = jax.ShapeDtypeStruct((tgts,) + tgt_embed.shape, tgt_embed.dtype)
    scalars = (picked, count)
    place = jnp.stack([lax.axis_index(a) for a in ("x", "s", "y", "p", "core")]).astype(jnp.int32)
    slots = srcs * tgts
    src_out, tgt_out = (srcs, srcs, TILE), (tgts, tgts, TILE)
    for sweep in range(ITERS):
        if sweep == 0:
            parts, src, tgt, sq_src, sq_tgt = half_step(
                first_kernel,
                [src_out, src_shape, tgt_shape, (srcs, TILE), (tgts, TILE)],
                tgts,
                slots,
                scalars + (place,),
                *src_pieces,
                *tgt_pieces,
            )
        else:
            (parts,) = half_step(
                functools.partial(source_kernel, log_cells), [src_out], tgts, slots, scalars, src, tgt, parts
            )
        parts = exchange(parts, SRC_PEERS)
        last = sweep == ITERS - 1
        parts, src_pot = half_step(
            functools.partial(target_kernel, log_cells),
            [(tgts, rows, TILE) if last else tgt_out, (srcs, TILE)],
            srcs,
            slots,
            scalars,
            src,
            tgt,
            parts,
            sq_src,
        )
        if last:
            other_pot = partner(src_pot)
        parts = exchange(parts, TGT_PEERS)
    tgt_pot, both = pl.pallas_call(
        functools.partial(last_kernel, log_cells),
        out_shape=[jax.ShapeDtypeStruct((rows, TILE), F32), jax.ShapeDtypeStruct((srcs, 2, TILE), F32)],
        in_specs=[SMEM] + [VMEM] * 4,
        out_specs=[VMEM] * 2,
        compiler_params=PARAMS,
    )(parity, parts, sq_tgt, src_pot, other_pot)
    return (both.reshape(-1), tgt_pot.reshape(-1))


def solution(mesh):
    fine = Mesh(mesh.devices.reshape(4, 2, 4, 4, 2), ROW + COL)
    in_specs = (P(ROW + COL, None), P(COL + ROW, None), P(ROW, COL, None, None), P(ROW, COL))
    return jax.shard_map(local, mesh=fine, in_specs=in_specs, out_specs=(P(ROW), P(COL)), check_vma=False)
```

```python
import functools
import math

import jax
import jax.numpy as jnp
from jax import lax
from jax.experimental import pallas as pl
from jax.experimental.pallas import tpu as pltpu
from jax.sharding import Mesh
from jax.sharding import PartitionSpec as P

TILE = 128
ITERS = 2
ENTROPY = 0.05
KAPPA = math.log2(math.e) / ENTROPY
EMPTY = -1e30
UNROLL = 16
ROW = ("y", "core")
COL = ("x", "s", "p")
SRC_PEERS = ("x", "s")
TGT_PEERS = ("p", "y", "core")
F32 = jnp.float32
NT = (((1,), (1,)), ((), ()))
VMEM = pl.BlockSpec(memory_space=pltpu.VMEM)
SMEM = pl.BlockSpec(memory_space=pltpu.SMEM)
PARAMS = pltpu.CompilerParams(vmem_limit_bytes=24 * 2**20)


def square_rows(cells):
    wide = cells.astype(F32)
    square = wide * wide
    high = square.astype(jnp.bfloat16)
    low = (square - high.astype(F32)).astype(jnp.bfloat16)
    ones = jnp.ones((8, cells.shape[1]), jnp.bfloat16)
    total = lax.dot_general(ones, high, NT, preferred_element_type=F32)
    total += lax.dot_general(ones, low, NT, preferred_element_type=F32)
    return total[0:1]


def log_sum(parts):
    highest = jnp.max(parts, axis=0)
    return highest + jnp.log2(jnp.sum(jnp.exp2(parts - highest[None]), axis=0))


def expand(weights, wide):
    blocks = weights.shape[0]
    columns = jnp.concatenate([weights, jnp.zeros((TILE - blocks, TILE), F32)], axis=0).T
    for n in range(blocks):
        wide[n] = jnp.broadcast_to(columns[:, n : n + 1], (TILE, TILE))


def tile_sums(tile, count, near, far, wide, peaks, totals):
    near_blocks, far_blocks = near.shape[0], far.shape[0]
    spare = near_blocks * far_blocks
    peaks[...] = jnp.full(peaks.shape, EMPTY, F32)
    totals[...] = jnp.zeros(totals.shape, F32)

    @pl.loop(0, (count + UNROLL - 1) // UNROLL)
    def _(step):
        for u in range(UNROLL):
            k = step * UNROLL + u
            n, f = tile(jnp.where(k < count, k, 0))
            inner = lax.dot_general(near[n], far[f], NT, preferred_element_type=F32)
            score = (inner * (2.0 * KAPPA) + wide[n]).reshape(TILE // 8, 8, TILE)
            peak = jnp.max(score, axis=0)
            slot = jnp.where(k < count, f * near_blocks + n, spare)
            peaks[slot] = peak
            totals[slot] = jnp.sum(jnp.exp2(score - peak[None]), axis=0)

    rows = []
    for f in range(far_blocks):
        at = pl.ds(f * near_blocks, near_blocks)
        peak = peaks[at]
        highest = jnp.max(jnp.max(peak, axis=0), axis=0, keepdims=True)
        whole = jnp.sum(totals[at] * jnp.exp2(peak - highest[None]), axis=0)
        whole = jnp.sum(whole, axis=0, keepdims=True)
        rows.append(jnp.where(whole > 0.0, highest + jnp.log2(whole), EMPTY))
    return jnp.concatenate(rows, axis=0)


def pick_kernel(mine, other, parity, picked, total):
    p = parity[0]
    targets = 8

    def scan(lists, col, start):
        def step(k, at):
            a, b = lists[0, k], lists[1, k]
            picked[at] = (a // 2) * (2 * targets) + col * targets + b
            return at + jnp.where((k < lists[2, 0]) & (a % 2 == p), 1, 0)

        return lax.fori_loop(0, TILE, step, start, unroll=8)

    total[0] = scan(other, 1 - p, scan(mine, p, 0))


def source_tiles(tiles, tgt_blocks):
    def tile(k):
        code = tiles[k]
        return lax.rem(code, tgt_blocks), lax.div(code, tgt_blocks)

    return tile


def target_tiles(tiles, tgt_blocks):
    def tile(k):
        code = tiles[k]
        return lax.div(code, tgt_blocks), lax.rem(code, tgt_blocks)

    return tile


def own_kernel(src_mine, tgt_mine, src, tgt):
    src[...] = src_mine[...]
    tgt[...] = tgt_mine[...]


def pack_kernel(lists, *refs):
    src, tgt = refs[-2:]
    sides = src.shape[0]
    for n in range(sides):
        src[n] = refs[n][...]
    for n in range(tgt.shape[0]):
        tgt[n] = refs[sides + n][...]


def first_kernel(tiles, count, place, *refs):
    pieces, (out, src, tgt, sq_src, sq_tgt, wide, peaks, totals) = refs[:-8], refs[-8:]
    sides = len(pieces) // 2
    for d in range(sides):
        x = lax.rem(place[0] + (sides - d), sides)
        p, core = place[3] ^ (d // 2), place[4] ^ (d % 2)
        for n in range(sides):
            s, y = (lax.rem(place[axis] + (sides - n), sides) for axis in (1, 2))
            src[x * sides + s] = pieces[d][n]
            tgt[p * (2 * sides) + 2 * y + core] = pieces[sides + d][n]
    for b in range(tgt.shape[0]):
        sq_tgt[b : b + 1, :] = square_rows(tgt[b])
    for a in range(src.shape[0]):
        sq_src[a : a + 1, :] = square_rows(src[a])
    expand(sq_tgt[...] * -KAPPA, wide)
    sums = tile_sums(source_tiles(tiles, tgt.shape[0]), count[0], tgt, src, wide, peaks, totals)
    out[...] = jnp.broadcast_to(sums[None], out.shape)


def source_kernel(log_cells, tiles, count, src, tgt, parts, out, wide, peaks, totals):
    expand(-log_cells - log_sum(parts[...]), wide)
    sums = tile_sums(source_tiles(tiles, tgt.shape[0]), count[0], tgt, src, wide, peaks, totals)
    out[...] = jnp.broadcast_to(sums[None], out.shape)


def target_kernel(log_cells, tiles, count, src, tgt, parts, sq_src, out, pot, wide, peaks, totals):
    weights = -log_cells - log_sum(parts[...])
    pot[...] = weights * (1.0 / KAPPA) + sq_src[...]
    expand(weights, wide)
    sums = tile_sums(target_tiles(tiles, tgt.shape[0]), count[0], src, tgt, wide, peaks, totals)
    copies, blocks = out.shape[0], out.shape[1]
    if blocks == sums.shape[0]:
        out[...] = jnp.broadcast_to(sums[None], out.shape)
    else:
        cols = sums.shape[0] // blocks
        each = copies // cols
        for col in range(cols):
            piece = sums[col * blocks : (col + 1) * blocks]
            out[col * each : (col + 1) * each] = jnp.broadcast_to(piece[None], (each,) + piece.shape)


def last_kernel(log_cells, parity, parts, sq_tgt, mine, other, tgt_pot, src_pot):
    p = parity[0]
    blocks = tgt_pot.shape[0]
    squares = jnp.where(p == 0, sq_tgt[0:blocks], sq_tgt[blocks : 2 * blocks])
    tgt_pot[...] = (-log_cells - log_sum(parts[...])) * (1.0 / KAPPA) + squares
    src_pot[:, 0, :] = jnp.where(p == 0, mine[...], other[...])
    src_pot[:, 1, :] = jnp.where(p == 0, other[...], mine[...])


def half_step(kernel, outs, near_blocks, slots, scalars, *args):
    return pl.pallas_call(
        kernel,
        out_shape=[s if isinstance(s, jax.ShapeDtypeStruct) else jax.ShapeDtypeStruct(s, F32) for s in outs],
        in_specs=[SMEM] * len(scalars) + [VMEM] * len(args),
        out_specs=[VMEM] * len(outs),
        scratch_shapes=[
            pltpu.VMEM((near_blocks, TILE, TILE), F32),
            pltpu.VMEM((slots + 1, 8, TILE), F32),
            pltpu.VMEM((slots + 1, 8, TILE), F32),
        ],
        compiler_params=PARAMS,
    )(*scalars, *args)


def exchange(copies, peers):
    return lax.all_to_all(copies, peers, 0, 0, tiled=True)


def shifts(block, axis):
    n = lax.axis_size(axis)
    turn = lambda d: lax.ppermute(block, axis, [(i, (i + d) % n) for i in range(n)])
    return [block] + [turn(d) for d in range(1, n)]


def bands(src_embed, tgt_embed, lists):
    block = jax.ShapeDtypeStruct(src_embed.shape, src_embed.dtype)
    own = pl.pallas_call(
        own_kernel, out_shape=[block] * 2, in_specs=[VMEM] * 2, out_specs=[VMEM] * 2, compiler_params=PARAMS
    )(src_embed, tgt_embed)
    src_blocks, tgt_blocks = shifts(src_embed, "s")[1:], shifts(tgt_embed, "y")[1:]
    blocks = [own[0]] + src_blocks + [own[1]] + tgt_blocks
    group = jax.ShapeDtypeStruct((1 + len(src_blocks),) + src_embed.shape, src_embed.dtype)
    src, tgt = pl.pallas_call(
        pack_kernel,
        out_shape=[group] * 2,
        in_specs=[pl.BlockSpec(memory_space=pl.ANY)] + [VMEM] * len(blocks),
        out_specs=[VMEM] * 2,
        compiler_params=PARAMS,
    )(lists, *blocks)
    tgt_pieces = [piece for side in shifts(tgt, "p") for piece in shifts(side, "core")]
    return shifts(src, "x"), tgt_pieces


def local(src_embed, tgt_embed, tiles, counts):
    rows, cols = lax.axis_size(ROW), lax.axis_size(COL)
    log_cells = math.log2(rows * cols * TILE)
    parity = lax.axis_index("p").astype(jnp.int32).reshape(1)
    partner = lambda v: lax.ppermute(v, "p", [(0, 1), (1, 0)])

    lists = jnp.concatenate([tiles[0, 0], jnp.broadcast_to(counts[0, 0], (1, TILE))], axis=0)
    other_lists = partner(lists)
    src_pieces, tgt_pieces = bands(src_embed, tgt_embed, other_lists)
    picked, count = pl.pallas_call(
        pick_kernel,
        out_shape=[jax.ShapeDtypeStruct((2 * TILE + UNROLL,), jnp.int32), jax.ShapeDtypeStruct((1,), jnp.int32)],
        in_specs=[SMEM] * 3,
        out_specs=[SMEM] * 2,
        compiler_params=PARAMS,
    )(lists, other_lists, parity)

    srcs, tgts = (len(pieces) * pieces[0].shape[0] for pieces in (src_pieces, tgt_pieces))
    src_shape = jax.ShapeDtypeStruct((srcs,) + src_embed.shape, src_embed.dtype)
    tgt_shape = jax.ShapeDtypeStruct((tgts,) + tgt_embed.shape, tgt_embed.dtype)
    scalars = (picked, count)
    place = jnp.stack([lax.axis_index(a) for a in ("x", "s", "y", "p", "core")]).astype(jnp.int32)
    slots = srcs * tgts
    src_out, tgt_out = (srcs, srcs, TILE), (tgts, tgts, TILE)
    for sweep in range(ITERS):
        if sweep == 0:
            parts, src, tgt, sq_src, sq_tgt = half_step(
                first_kernel,
                [src_out, src_shape, tgt_shape, (srcs, TILE), (tgts, TILE)],
                tgts,
                slots,
                scalars + (place,),
                *src_pieces,
                *tgt_pieces,
            )
        else:
            (parts,) = half_step(
                functools.partial(source_kernel, log_cells), [src_out], tgts, slots, scalars, src, tgt, parts
            )
        parts = exchange(parts, SRC_PEERS)
        last = sweep == ITERS - 1
        parts, src_pot = half_step(
            functools.partial(target_kernel, log_cells),
            [(tgts, rows, TILE) if last else tgt_out, (srcs, TILE)],
            srcs,
            slots,
            scalars,
            src,
            tgt,
            parts,
            sq_src,
        )
        if last:
            other_pot = partner(src_pot)
        parts = exchange(parts, TGT_PEERS)
    tgt_pot, both = pl.pallas_call(
        functools.partial(last_kernel, log_cells),
        out_shape=[jax.ShapeDtypeStruct((rows, TILE), F32), jax.ShapeDtypeStruct((srcs, 2, TILE), F32)],
        in_specs=[SMEM] + [VMEM] * 4,
        out_specs=[VMEM] * 2,
        compiler_params=PARAMS,
    )(parity, parts, sq_tgt, src_pot, other_pot)
    return (both.reshape(-1), tgt_pot.reshape(-1))


def solution(mesh):
    fine = Mesh(mesh.devices.reshape(4, 2, 4, 4, 2), ROW + COL)
    in_specs = (P(ROW + COL, None), P(COL + ROW, None), P(ROW, COL, None, None), P(ROW, COL))
    return jax.shard_map(local, mesh=fine, in_specs=in_specs, out_specs=(P(ROW), P(COL)), check_vma=False)
```

```python
import functools
import math

import jax
import jax.numpy as jnp
from jax import lax
from jax.experimental import pallas as pl
from jax.experimental.pallas import tpu as pltpu
from jax.sharding import Mesh
from jax.sharding import PartitionSpec as P

TILE = 128
ITERS = 2
ENTROPY = 0.05
KAPPA = math.log2(math.e) / ENTROPY
EMPTY = -1e30
UNROLL = 16
ROW = ("y", "core")
COL = ("x", "s", "p")
SRC_PEERS = ("x", "s")
TGT_PEERS = ("p", "y", "core")
F32 = jnp.float32
NT = (((1,), (1,)), ((), ()))
VMEM = pl.BlockSpec(memory_space=pltpu.VMEM)
SMEM = pl.BlockSpec(memory_space=pltpu.SMEM)
ANY = pl.BlockSpec(memory_space=pl.ANY)
PARAMS = pltpu.CompilerParams(vmem_limit_bytes=24 * 2**20)


def square_rows(cells):
    wide = cells.astype(F32)
    square = wide * wide
    high = square.astype(jnp.bfloat16)
    low = (square - high.astype(F32)).astype(jnp.bfloat16)
    ones = jnp.ones((8, cells.shape[1]), jnp.bfloat16)
    total = lax.dot_general(ones, high, NT, preferred_element_type=F32)
    total += lax.dot_general(ones, low, NT, preferred_element_type=F32)
    return total[0:1]


def log_sum(parts):
    highest = jnp.max(parts, axis=0)
    return highest + jnp.log2(jnp.sum(jnp.exp2(parts - highest[None]), axis=0))


def expand(weights, wide):
    blocks = weights.shape[0]
    columns = jnp.concatenate([weights, jnp.zeros((TILE - blocks, TILE), F32)], axis=0).T
    for n in range(blocks):
        wide[n] = jnp.broadcast_to(columns[:, n : n + 1], (TILE, TILE))


def tile_sums(tile, count, near, far, wide, peaks, totals):
    near_blocks, far_blocks = near.shape[0], far.shape[0]
    spare = near_blocks * far_blocks
    peaks[...] = jnp.full(peaks.shape, EMPTY, F32)
    totals[...] = jnp.zeros(totals.shape, F32)

    @pl.loop(0, (count + UNROLL - 1) // UNROLL)
    def _(step):
        for u in range(UNROLL):
            k = step * UNROLL + u
            n, f = tile(jnp.where(k < count, k, 0))
            inner = lax.dot_general(near[n], far[f], NT, preferred_element_type=F32)
            score = (inner * (2.0 * KAPPA) + wide[n]).reshape(TILE // 8, 8, TILE)
            peak = jnp.max(score, axis=0)
            slot = jnp.where(k < count, f * near_blocks + n, spare)
            peaks[slot] = peak
            totals[slot] = jnp.sum(jnp.exp2(score - peak[None]), axis=0)

    rows = []
    for f in range(far_blocks):
        at = pl.ds(f * near_blocks, near_blocks)
        peak = peaks[at]
        highest = jnp.max(jnp.max(peak, axis=0), axis=0, keepdims=True)
        whole = jnp.sum(totals[at] * jnp.exp2(peak - highest[None]), axis=0)
        whole = jnp.sum(whole, axis=0, keepdims=True)
        rows.append(jnp.where(whole > 0.0, highest + jnp.log2(whole), EMPTY))
    return jnp.concatenate(rows, axis=0)


def pick_kernel(mine, other, place, picked):
    p = place[3]
    targets = 8

    def scan(lists, col, start):
        def step(k, at):
            a, b = lists[0, k], lists[1, k]
            picked[1 + at // TILE, at % TILE] = (a // 2) * (2 * targets) + col * targets + b
            return at + jnp.where((k < lists[2, 0]) & (a % 2 == p), 1, 0)

        return lax.fori_loop(0, TILE, step, start, unroll=8)

    picked[0, 0] = scan(other, 1 - p, scan(mine, p, 0))
    for n in range(place.shape[0]):
        picked[0, 1 + n] = place[n]


def tile_code(tiles, k):
    return tiles[1 + k // TILE, k % TILE]


def source_tiles(tiles, tgt_blocks):
    def tile(k):
        code = tile_code(tiles, k)
        return code % tgt_blocks, code // tgt_blocks

    return tile


def target_tiles(tiles, tgt_blocks):
    def tile(k):
        code = tile_code(tiles, k)
        return code // tgt_blocks, code % tgt_blocks

    return tile


def own_kernel(src_mine, tgt_mine, src, tgt):
    src[...] = src_mine[...]
    tgt[...] = tgt_mine[...]


def pack_kernel(lists, *refs):
    src, tgt = refs[-2:]
    sides = src.shape[0]
    for n in range(sides):
        src[n] = refs[n][...]
    for n in range(tgt.shape[0]):
        tgt[n] = refs[sides + n][...]


def join_kernel(*refs):
    blocks = refs[0].shape[0]
    for n, piece in enumerate(refs[:-1]):
        refs[-1][n * blocks : (n + 1) * blocks] = piece[...]


def first_kernel(picked, *refs):
    pieces, (out, src, tgt, sq_src, sq_tgt, wide, peaks, totals, tiles, sem) = refs[:-10], refs[-10:]
    fetch = pltpu.make_async_copy(picked, tiles, sem)
    fetch.start()
    tgt_pieces = pieces[4:]
    sides, cores = len(pieces) - len(tgt_pieces), len(tgt_pieces)
    fetch.wait()
    place = [tiles[0, 1 + n] for n in range(5)]
    for d in range(sides):
        x = lax.rem(place[0] + (sides - d), sides)
        for n in range(pieces[d].shape[0]):
            s = lax.rem(place[1] + (sides - n), sides)
            src[x * sides + s] = pieces[d][n]
    for d, piece in enumerate(tgt_pieces):
        core = place[4] ^ d
        for n in range(piece.shape[0]):
            p, y = place[3] ^ (n // sides), lax.rem(place[2] + (sides - n % sides), sides)
            tgt[p * (cores * sides) + cores * y + core] = piece[n]
    for b in range(tgt.shape[0]):
        sq_tgt[b : b + 1, :] = square_rows(tgt[b])
    for a in range(src.shape[0]):
        sq_src[a : a + 1, :] = square_rows(src[a])
    expand(sq_tgt[...] * -KAPPA, wide)
    sums = tile_sums(source_tiles(tiles, tgt.shape[0]), tiles[0, 0], tgt, src, wide, peaks, totals)
    out[...] = jnp.broadcast_to(sums[None], out.shape)


def source_kernel(log_cells, picked, src, tgt, parts, out, wide, peaks, totals, tiles, sem):
    fetch = pltpu.make_async_copy(picked, tiles, sem)
    fetch.start()
    expand(-log_cells - log_sum(parts[...]), wide)
    fetch.wait()
    sums = tile_sums(source_tiles(tiles, tgt.shape[0]), tiles[0, 0], tgt, src, wide, peaks, totals)
    out[...] = jnp.broadcast_to(sums[None], out.shape)


def target_kernel(log_cells, picked, src, tgt, parts, sq_src, out, pot, wide, peaks, totals, tiles, sem):
    fetch = pltpu.make_async_copy(picked, tiles, sem)
    fetch.start()
    weights = -log_cells - log_sum(parts[...])
    pot[...] = weights * (1.0 / KAPPA) + sq_src[...]
    expand(weights, wide)
    fetch.wait()
    sums = tile_sums(target_tiles(tiles, tgt.shape[0]), tiles[0, 0], src, tgt, wide, peaks, totals)
    copies, blocks = out.shape[0], out.shape[1]
    if blocks == sums.shape[0]:
        out[...] = jnp.broadcast_to(sums[None], out.shape)
    else:
        cols = sums.shape[0] // blocks
        each = copies // cols
        for col in range(cols):
            piece = sums[col * blocks : (col + 1) * blocks]
            out[col * each : (col + 1) * each] = jnp.broadcast_to(piece[None], (each,) + piece.shape)


def last_kernel(log_cells, parity, parts, sq_tgt, mine, other, tgt_pot, src_pot):
    p = parity[0]
    blocks = tgt_pot.shape[0]
    squares = jnp.where(p == 0, sq_tgt[0:blocks], sq_tgt[blocks : 2 * blocks])
    tgt_pot[...] = (-log_cells - log_sum(parts[...])) * (1.0 / KAPPA) + squares
    src_pot[:, 0, :] = jnp.where(p == 0, mine[...], other[...])
    src_pot[:, 1, :] = jnp.where(p == 0, other[...], mine[...])


def half_step(kernel, outs, near_blocks, slots, picked, *args):
    return pl.pallas_call(
        kernel,
        out_shape=[s if isinstance(s, jax.ShapeDtypeStruct) else jax.ShapeDtypeStruct(s, F32) for s in outs],
        in_specs=[ANY] + [VMEM] * len(args),
        out_specs=[VMEM] * len(outs),
        scratch_shapes=[
            pltpu.VMEM((near_blocks, TILE, TILE), F32),
            pltpu.VMEM((slots + 1, 8, TILE), F32),
            pltpu.VMEM((slots + 1, 8, TILE), F32),
            pltpu.SMEM(picked.shape, picked.dtype),
            pltpu.SemaphoreType.DMA,
        ],
        compiler_params=PARAMS,
    )(picked, *args)


def exchange(copies, peers):
    return lax.all_to_all(copies, peers, 0, 0, tiled=True)


def shifts(block, axis):
    n = lax.axis_size(axis)
    turn = lambda d: lax.ppermute(block, axis, [(i, (i + d) % n) for i in range(n)])
    return [block] + [turn(d) for d in range(1, n)]


def bands(src_embed, tgt_embed, lists):
    block = jax.ShapeDtypeStruct(src_embed.shape, src_embed.dtype)
    own = pl.pallas_call(
        own_kernel, out_shape=[block] * 2, in_specs=[VMEM] * 2, out_specs=[VMEM] * 2, compiler_params=PARAMS
    )(src_embed, tgt_embed)
    src_blocks, tgt_blocks = shifts(src_embed, "s")[1:], shifts(tgt_embed, "y")[1:]
    blocks = [own[0]] + src_blocks + [own[1]] + tgt_blocks
    group = jax.ShapeDtypeStruct((1 + len(src_blocks),) + src_embed.shape, src_embed.dtype)
    src, tgt = pl.pallas_call(
        pack_kernel,
        out_shape=[group] * 2,
        in_specs=[ANY] + [VMEM] * len(blocks),
        out_specs=[VMEM] * 2,
        compiler_params=PARAMS,
    )(lists, *blocks)
    src_pieces, tgt_pieces = shifts(src, "x"), shifts(tgt, "p")
    both = pl.pallas_call(
        join_kernel,
        out_shape=jax.ShapeDtypeStruct((len(tgt_pieces) * tgt.shape[0],) + tgt.shape[1:], tgt.dtype),
        in_specs=[VMEM] * len(tgt_pieces),
        out_specs=VMEM,
        compiler_params=PARAMS,
    )(*tgt_pieces)
    return src_pieces, shifts(both, "core")


def local(src_embed, tgt_embed, tiles, counts):
    rows, cols = lax.axis_size(ROW), lax.axis_size(COL)
    log_cells = math.log2(rows * cols * TILE)
    parity = lax.axis_index("p").astype(jnp.int32).reshape(1)
    partner = lambda v: lax.ppermute(v, "p", [(0, 1), (1, 0)])

    lists = jnp.concatenate([tiles[0, 0], jnp.broadcast_to(counts[0, 0], (1, TILE))], axis=0)
    other_lists = partner(lists)
    src_pieces, tgt_pieces = bands(src_embed, tgt_embed, other_lists)
    place = jnp.stack([lax.axis_index(a) for a in ("x", "s", "y", "p", "core")]).astype(jnp.int32)
    picked = pl.pallas_call(
        pick_kernel,
        out_shape=jax.ShapeDtypeStruct((8, TILE), jnp.int32),
        in_specs=[SMEM] * 3,
        out_specs=SMEM,
        compiler_params=PARAMS,
    )(lists, other_lists, place)

    srcs, tgts = (len(pieces) * pieces[0].shape[0] for pieces in (src_pieces, tgt_pieces))
    src_shape = jax.ShapeDtypeStruct((srcs,) + src_embed.shape, src_embed.dtype)
    tgt_shape = jax.ShapeDtypeStruct((tgts,) + tgt_embed.shape, tgt_embed.dtype)
    slots = srcs * tgts
    src_out, tgt_out = (srcs, srcs, TILE), (tgts, tgts, TILE)
    for sweep in range(ITERS):
        if sweep == 0:
            parts, src, tgt, sq_src, sq_tgt = half_step(
                first_kernel,
                [src_out, src_shape, tgt_shape, (srcs, TILE), (tgts, TILE)],
                tgts,
                slots,
                picked,
                *src_pieces,
                *tgt_pieces,
            )
        else:
            (parts,) = half_step(
                functools.partial(source_kernel, log_cells), [src_out], tgts, slots, picked, src, tgt, parts
            )
        parts = exchange(parts, SRC_PEERS)
        last = sweep == ITERS - 1
        parts, src_pot = half_step(
            functools.partial(target_kernel, log_cells),
            [(tgts, rows, TILE) if last else tgt_out, (srcs, TILE)],
            srcs,
            slots,
            picked,
            src,
            tgt,
            parts,
            sq_src,
        )
        if last:
            other_pot = partner(src_pot)
        parts = exchange(parts, TGT_PEERS)
    tgt_pot, both = pl.pallas_call(
        functools.partial(last_kernel, log_cells),
        out_shape=[jax.ShapeDtypeStruct((rows, TILE), F32), jax.ShapeDtypeStruct((srcs, 2, TILE), F32)],
        in_specs=[SMEM] + [VMEM] * 4,
        out_specs=[VMEM] * 2,
        compiler_params=PARAMS,
    )(parity, parts, sq_tgt, src_pot, other_pot)
    return (both.reshape(-1), tgt_pot.reshape(-1))


def solution(mesh):
    fine = Mesh(mesh.devices.reshape(4, 2, 4, 4, 2), ROW + COL)
    in_specs = (P(ROW + COL, None), P(COL + ROW, None), P(ROW, COL, None, None), P(ROW, COL))
    return jax.shard_map(local, mesh=fine, in_specs=in_specs, out_specs=(P(ROW), P(COL)), check_vma=False)
```

```python
import functools
import math

import jax
import jax.numpy as jnp
from jax import lax
from jax.experimental import pallas as pl
from jax.experimental.pallas import tpu as pltpu
from jax.sharding import Mesh
from jax.sharding import PartitionSpec as P

TILE = 128
LOG_TILE = 7
ITERS = 2
ENTROPY = 0.05
KAPPA = math.log2(math.e) / ENTROPY
EMPTY = -1e30
UNROLL = 16
ROW = ("y", "core")
COL = ("x", "s", "p")
SRC_PEERS = ("x", "s")
TGT_PEERS = ("p", "y", "core")
F32 = jnp.float32
NT = (((1,), (1,)), ((), ()))
VMEM = pl.BlockSpec(memory_space=pltpu.VMEM)
SMEM = pl.BlockSpec(memory_space=pltpu.SMEM)
ANY = pl.BlockSpec(memory_space=pl.ANY)
PARAMS = pltpu.CompilerParams(vmem_limit_bytes=24 * 2**20)


def square_rows(cells):
    wide = cells.astype(F32)
    square = wide * wide
    high = square.astype(jnp.bfloat16)
    low = (square - high.astype(F32)).astype(jnp.bfloat16)
    ones = jnp.ones((8, cells.shape[1]), jnp.bfloat16)
    total = lax.dot_general(ones, high, NT, preferred_element_type=F32)
    total += lax.dot_general(ones, low, NT, preferred_element_type=F32)
    return total[0:1]


def log_sum(parts):
    highest = jnp.max(parts, axis=0)
    return highest + jnp.log2(jnp.sum(jnp.exp2(parts - highest[None]), axis=0))


def expand(weights, wide):
    blocks = weights.shape[0]
    columns = jnp.concatenate([weights, jnp.zeros((TILE - blocks, TILE), F32)], axis=0).T
    for n in range(blocks):
        wide[n] = jnp.broadcast_to(columns[:, n : n + 1], (TILE, TILE))


def tile_sums(tile, count, near, far, wide, peaks, totals):
    near_blocks, far_blocks = near.shape[0], far.shape[0]
    spare = near_blocks * far_blocks
    peaks[...] = jnp.full(peaks.shape, EMPTY, F32)
    totals[...] = jnp.zeros(totals.shape, F32)

    @pl.loop(0, (count + UNROLL - 1) // UNROLL)
    def _(step):
        for u in range(UNROLL):
            k = step * UNROLL + u
            n, f = tile(jnp.where(k < count, k, 0))
            inner = lax.dot_general(near[n], far[f], NT, preferred_element_type=F32)
            score = (inner * (2.0 * KAPPA) + wide[n]).reshape(TILE // 8, 8, TILE)
            peak = jnp.max(score, axis=0)
            slot = jnp.where(k < count, f * near_blocks + n, spare)
            peaks[slot] = peak
            totals[slot] = jnp.sum(jnp.exp2(score - peak[None]), axis=0)

    rows = []
    for f in range(far_blocks):
        at = pl.ds(f * near_blocks, near_blocks)
        peak = peaks[at]
        highest = jnp.max(jnp.max(peak, axis=0), axis=0, keepdims=True)
        whole = jnp.sum(totals[at] * jnp.exp2(peak - highest[None]), axis=0)
        whole = jnp.sum(whole, axis=0, keepdims=True)
        rows.append(jnp.where(whole > 0.0, highest + jnp.log2(whole), EMPTY))
    return jnp.concatenate(rows, axis=0)


def pick_kernel(mine, other, place, picked):
    p = place[3]
    targets = 8

    def scan(lists, col, start):
        count = lists[2, 0]

        def step(k, at):
            a, b = lists[0, k], lists[1, k]
            picked[1 + (at >> LOG_TILE), at & (TILE - 1)] = (a >> 1) * (2 * targets) + col * targets + b
            return at + jnp.where((k < count) & ((a & 1) == p), 1, 0)

        return lax.fori_loop(0, TILE, step, start, unroll=8)

    picked[0, 0] = scan(other, 1 - p, scan(mine, p, 0))
    for n in range(place.shape[0]):
        picked[0, 1 + n] = place[n]


def tile_code(tiles, k):
    return tiles[1 + (k >> LOG_TILE), k & (TILE - 1)]


def source_tiles(tiles, tgt_blocks):
    def tile(k):
        code = tile_code(tiles, k)
        return lax.rem(code, tgt_blocks), lax.div(code, tgt_blocks)

    return tile


def target_tiles(tiles, tgt_blocks):
    def tile(k):
        code = tile_code(tiles, k)
        return lax.div(code, tgt_blocks), lax.rem(code, tgt_blocks)

    return tile


def own_kernel(src_mine, tgt_mine, src, tgt):
    src[...] = src_mine[...]
    tgt[...] = tgt_mine[...]


def pack_kernel(lists, *refs):
    src, tgt = refs[-2:]
    sides = src.shape[0]
    for n in range(sides):
        src[n] = refs[n][...]
    for n in range(tgt.shape[0]):
        tgt[n] = refs[sides + n][...]


def join_kernel(after, *refs):
    blocks = refs[0].shape[0]
    for n, piece in enumerate(refs[:-1]):
        refs[-1][n * blocks : (n + 1) * blocks] = piece[...]


def first_kernel(picked, *refs):
    pieces, (out, src, tgt, sq_src, sq_tgt, wide, peaks, totals, tiles, sem) = refs[:-10], refs[-10:]
    fetch = pltpu.make_async_copy(picked, tiles, sem)
    fetch.start()
    tgt_pieces = pieces[4:]
    sides, cores = len(pieces) - len(tgt_pieces), len(tgt_pieces)
    fetch.wait()
    place = [tiles[0, 1 + n] for n in range(5)]
    for d in range(sides):
        x = lax.rem(place[0] + (sides - d), sides)
        for n in range(pieces[d].shape[0]):
            s = lax.rem(place[1] + (sides - n), sides)
            src[x * sides + s] = pieces[d][n]
    for d, piece in enumerate(tgt_pieces):
        core = place[4] ^ d
        for n in range(piece.shape[0]):
            p, y = place[3] ^ (n // sides), lax.rem(place[2] + (sides - n % sides), sides)
            tgt[p * (cores * sides) + cores * y + core] = piece[n]
    for b in range(tgt.shape[0]):
        sq_tgt[b : b + 1, :] = square_rows(tgt[b])
    for a in range(src.shape[0]):
        sq_src[a : a + 1, :] = square_rows(src[a])
    expand(sq_tgt[...] * -KAPPA, wide)
    sums = tile_sums(source_tiles(tiles, tgt.shape[0]), tiles[0, 0], tgt, src, wide, peaks, totals)
    out[...] = jnp.broadcast_to(sums[None], out.shape)


def source_kernel(log_cells, picked, src, tgt, parts, out, wide, peaks, totals, tiles, sem):
    fetch = pltpu.make_async_copy(picked, tiles, sem)
    fetch.start()
    expand(-log_cells - log_sum(parts[...]), wide)
    fetch.wait()
    sums = tile_sums(source_tiles(tiles, tgt.shape[0]), tiles[0, 0], tgt, src, wide, peaks, totals)
    out[...] = jnp.broadcast_to(sums[None], out.shape)


def target_kernel(log_cells, picked, src, tgt, parts, sq_src, out, pot, wide, peaks, totals, tiles, sem):
    fetch = pltpu.make_async_copy(picked, tiles, sem)
    fetch.start()
    weights = -log_cells - log_sum(parts[...])
    pot[...] = weights * (1.0 / KAPPA) + sq_src[...]
    expand(weights, wide)
    fetch.wait()
    sums = tile_sums(target_tiles(tiles, tgt.shape[0]), tiles[0, 0], src, tgt, wide, peaks, totals)
    copies, blocks = out.shape[0], out.shape[1]
    if blocks == sums.shape[0]:
        out[...] = jnp.broadcast_to(sums[None], out.shape)
    else:
        cols = sums.shape[0] // blocks
        each = copies // cols
        for col in range(cols):
            piece = sums[col * blocks : (col + 1) * blocks]
            out[col * each : (col + 1) * each] = jnp.broadcast_to(piece[None], (each,) + piece.shape)


def last_kernel(log_cells, parity, parts, sq_tgt, mine, other, tgt_pot, src_pot):
    p = parity[0]
    blocks = tgt_pot.shape[0]
    squares = jnp.where(p == 0, sq_tgt[0:blocks], sq_tgt[blocks : 2 * blocks])
    tgt_pot[...] = (-log_cells - log_sum(parts[...])) * (1.0 / KAPPA) + squares
    src_pot[:, 0, :] = jnp.where(p == 0, mine[...], other[...])
    src_pot[:, 1, :] = jnp.where(p == 0, other[...], mine[...])


def half_step(kernel, outs, near_blocks, slots, picked, *args):
    return pl.pallas_call(
        kernel,
        out_shape=[s if isinstance(s, jax.ShapeDtypeStruct) else jax.ShapeDtypeStruct(s, F32) for s in outs],
        in_specs=[ANY] + [VMEM] * len(args),
        out_specs=[VMEM] * len(outs),
        scratch_shapes=[
            pltpu.VMEM((near_blocks, TILE, TILE), F32),
            pltpu.VMEM((slots + 1, 8, TILE), F32),
            pltpu.VMEM((slots + 1, 8, TILE), F32),
            pltpu.SMEM(picked.shape, picked.dtype),
            pltpu.SemaphoreType.DMA,
        ],
        compiler_params=PARAMS,
    )(picked, *args)


def exchange(copies, peers):
    return lax.all_to_all(copies, peers, 0, 0, tiled=True)


def shifts(block, axis):
    n = lax.axis_size(axis)
    turn = lambda d: lax.ppermute(block, axis, [(i, (i + d) % n) for i in range(n)])
    return [block] + [turn(d) for d in range(1, n)]


def bands(src_embed, tgt_embed, lists):
    block = jax.ShapeDtypeStruct(src_embed.shape, src_embed.dtype)
    own = pl.pallas_call(
        own_kernel, out_shape=[block] * 2, in_specs=[VMEM] * 2, out_specs=[VMEM] * 2, compiler_params=PARAMS
    )(src_embed, tgt_embed)
    src_blocks, tgt_blocks = shifts(src_embed, "s")[1:], shifts(tgt_embed, "y")[1:]
    blocks = [own[0]] + src_blocks + [own[1]] + tgt_blocks
    group = jax.ShapeDtypeStruct((1 + len(src_blocks),) + src_embed.shape, src_embed.dtype)
    src, tgt = pl.pallas_call(
        pack_kernel,
        out_shape=[group] * 2,
        in_specs=[ANY] + [VMEM] * len(blocks),
        out_specs=[VMEM] * 2,
        compiler_params=PARAMS,
    )(lists, *blocks)
    src_pieces, tgt_pieces = shifts(src, "x"), shifts(tgt, "p")
    both = pl.pallas_call(
        join_kernel,
        out_shape=jax.ShapeDtypeStruct((len(tgt_pieces) * tgt.shape[0],) + tgt.shape[1:], tgt.dtype),
        in_specs=[ANY] + [VMEM] * len(tgt_pieces),
        out_specs=VMEM,
        compiler_params=PARAMS,
    )(src_pieces[-1], *tgt_pieces)
    return src_pieces, shifts(both, "core")


def local(src_embed, tgt_embed, tiles, counts):
    rows, cols = lax.axis_size(ROW), lax.axis_size(COL)
    log_cells = math.log2(rows * cols * TILE)
    parity = lax.axis_index("p").astype(jnp.int32).reshape(1)
    partner = lambda v: lax.ppermute(v, "p", [(0, 1), (1, 0)])

    lists = jnp.concatenate([tiles[0, 0], jnp.broadcast_to(counts[0, 0], (1, TILE))], axis=0)
    other_lists = partner(lists)
    src_pieces, tgt_pieces = bands(src_embed, tgt_embed, other_lists)
    place = jnp.stack([lax.axis_index(a) for a in ("x", "s", "y", "p", "core")]).astype(jnp.int32)
    picked = pl.pallas_call(
        pick_kernel,
        out_shape=jax.ShapeDtypeStruct((8, TILE), jnp.int32),
        in_specs=[SMEM] * 3,
        out_specs=SMEM,
        compiler_params=PARAMS,
    )(lists, other_lists, place)

    srcs, tgts = (len(pieces) * pieces[0].shape[0] for pieces in (src_pieces, tgt_pieces))
    src_shape = jax.ShapeDtypeStruct((srcs,) + src_embed.shape, src_embed.dtype)
    tgt_shape = jax.ShapeDtypeStruct((tgts,) + tgt_embed.shape, tgt_embed.dtype)
    slots = srcs * tgts
    src_out, tgt_out = (srcs, srcs, TILE), (tgts, tgts, TILE)
    for sweep in range(ITERS):
        if sweep == 0:
            parts, src, tgt, sq_src, sq_tgt = half_step(
                first_kernel,
                [src_out, src_shape, tgt_shape, (srcs, TILE), (tgts, TILE)],
                tgts,
                slots,
                picked,
                *src_pieces,
                *tgt_pieces,
            )
        else:
            (parts,) = half_step(
                functools.partial(source_kernel, log_cells), [src_out], tgts, slots, picked, src, tgt, parts
            )
        parts = exchange(parts, SRC_PEERS)
        last = sweep == ITERS - 1
        parts, src_pot = half_step(
            functools.partial(target_kernel, log_cells),
            [(tgts, rows, TILE) if last else tgt_out, (srcs, TILE)],
            srcs,
            slots,
            picked,
            src,
            tgt,
            parts,
            sq_src,
        )
        if last:
            other_pot = partner(src_pot)
        parts = exchange(parts, TGT_PEERS)
    tgt_pot, both = pl.pallas_call(
        functools.partial(last_kernel, log_cells),
        out_shape=[jax.ShapeDtypeStruct((rows, TILE), F32), jax.ShapeDtypeStruct((srcs, 2, TILE), F32)],
        in_specs=[SMEM] + [VMEM] * 4,
        out_specs=[VMEM] * 2,
        compiler_params=PARAMS,
    )(parity, parts, sq_tgt, src_pot, other_pot)
    return (both.reshape(-1), tgt_pot.reshape(-1))


def solution(mesh):
    fine = Mesh(mesh.devices.reshape(4, 2, 4, 4, 2), ROW + COL)
    in_specs = (P(ROW + COL, None), P(COL + ROW, None), P(ROW, COL, None, None), P(ROW, COL))
    return jax.shard_map(local, mesh=fine, in_specs=in_specs, out_specs=(P(ROW), P(COL)), check_vma=False)
```

```python
import functools
import math

import jax
import jax.numpy as jnp
from jax import lax
from jax.experimental import pallas as pl
from jax.experimental.pallas import tpu as pltpu
from jax.sharding import Mesh
from jax.sharding import PartitionSpec as P

TILE = 128
LOG_TILE = 7
ITERS = 2
ENTROPY = 0.05
KAPPA = math.log2(math.e) / ENTROPY
EMPTY = -1e30
UNROLL = 16
ROW = ("y", "core")
COL = ("x", "s", "p")
SRC_PEERS = ("x", "s")
TGT_PEERS = ("p", "y", "core")
F32 = jnp.float32
NT = (((1,), (1,)), ((), ()))
VMEM = pl.BlockSpec(memory_space=pltpu.VMEM)
SMEM = pl.BlockSpec(memory_space=pltpu.SMEM)
ANY = pl.BlockSpec(memory_space=pl.ANY)
PARAMS = pltpu.CompilerParams(vmem_limit_bytes=24 * 2**20)


def square_rows(cells):
    wide = cells.astype(F32)
    square = wide * wide
    high = square.astype(jnp.bfloat16)
    low = (square - high.astype(F32)).astype(jnp.bfloat16)
    ones = jnp.ones((8, cells.shape[1]), jnp.bfloat16)
    total = lax.dot_general(ones, high, NT, preferred_element_type=F32)
    total += lax.dot_general(ones, low, NT, preferred_element_type=F32)
    return total[0:1]


def log_sum(parts):
    highest = jnp.max(parts, axis=0)
    return highest + jnp.log2(jnp.sum(jnp.exp2(parts - highest[None]), axis=0))


def expand(weights, wide):
    blocks = weights.shape[0]
    columns = jnp.concatenate([weights, jnp.zeros((TILE - blocks, TILE), F32)], axis=0).T
    for n in range(blocks):
        wide[n] = jnp.broadcast_to(columns[:, n : n + 1], (TILE, TILE))


def tile_sums(tile, count, near, far, wide, peaks, totals):
    near_blocks, far_blocks = near.shape[0], far.shape[0]
    spare = near_blocks * far_blocks
    peaks[...] = jnp.full(peaks.shape, EMPTY, F32)
    totals[...] = jnp.zeros(totals.shape, F32)

    @pl.loop(0, (count + UNROLL - 1) // UNROLL)
    def _(step):
        for u in range(UNROLL):
            k = step * UNROLL + u
            n, f = tile(jnp.where(k < count, k, 0))
            inner = lax.dot_general(near[n], far[f], NT, preferred_element_type=F32)
            score = (inner * (2.0 * KAPPA) + wide[n]).reshape(TILE // 8, 8, TILE)
            peak = jnp.max(score, axis=0)
            slot = jnp.where(k < count, f * near_blocks + n, spare)
            peaks[slot] = peak
            totals[slot] = jnp.sum(jnp.exp2(score - peak[None]), axis=0)

    rows = []
    for f in range(far_blocks):
        at = pl.ds(f * near_blocks, near_blocks)
        peak = peaks[at]
        highest = jnp.max(jnp.max(peak, axis=0), axis=0, keepdims=True)
        whole = jnp.sum(totals[at] * jnp.exp2(peak - highest[None]), axis=0)
        whole = jnp.sum(whole, axis=0, keepdims=True)
        rows.append(jnp.where(whole > 0.0, highest + jnp.log2(whole), EMPTY))
    return jnp.concatenate(rows, axis=0)


def pick_kernel(mine, other, place, picked):
    p = place[3]
    targets = 8

    def scan(lists, col, start):
        count = lists[2, 0]

        def step(k, at):
            a, b = lists[0, k], lists[1, k]
            picked[1 + (at >> LOG_TILE), at & (TILE - 1)] = (a >> 1) * (2 * targets) + col * targets + b
            return at + jnp.where((k < count) & ((a & 1) == p), 1, 0)

        return lax.fori_loop(0, TILE, step, start, unroll=8)

    picked[0, 0] = scan(other, 1 - p, scan(mine, p, 0))
    for n in range(place.shape[0]):
        picked[0, 1 + n] = place[n]


def tile_code(tiles, k):
    return tiles[1 + (k >> LOG_TILE), k & (TILE - 1)]


def source_tiles(tiles, tgt_blocks):
    def tile(k):
        code = tile_code(tiles, k)
        return lax.rem(code, tgt_blocks), lax.div(code, tgt_blocks)

    return tile


def target_tiles(tiles, tgt_blocks):
    def tile(k):
        code = tile_code(tiles, k)
        return lax.div(code, tgt_blocks), lax.rem(code, tgt_blocks)

    return tile


def own_kernel(src_mine, tgt_mine, src, tgt):
    src[...] = src_mine[...]
    tgt[...] = tgt_mine[...]


def pack_kernel(lists, *refs):
    src, tgt = refs[-2:]
    sides = src.shape[0]
    for n in range(sides):
        src[n] = refs[n][...]
    for n in range(tgt.shape[0]):
        tgt[n] = refs[sides + n][...]


def after_kernel(first, block, out):
    out[...] = block[...]


def first_kernel(picked, *refs):
    pieces, (out, src, tgt, sq_src, sq_tgt, wide, peaks, totals, tiles, sem) = refs[:-10], refs[-10:]
    fetch = pltpu.make_async_copy(picked, tiles, sem)
    fetch.start()
    sides = len(pieces) // 2
    fetch.wait()
    place = [tiles[0, 1 + n] for n in range(5)]
    for d in range(sides):
        x = lax.rem(place[0] + (sides - d), sides)
        p, core = place[3] ^ (d // 2), place[4] ^ (d % 2)
        for n in range(sides):
            s, y = (lax.rem(place[axis] + (sides - n), sides) for axis in (1, 2))
            src[x * sides + s] = pieces[d][n]
            tgt[p * (2 * sides) + 2 * y + core] = pieces[sides + d][n]
    for b in range(tgt.shape[0]):
        sq_tgt[b : b + 1, :] = square_rows(tgt[b])
    for a in range(src.shape[0]):
        sq_src[a : a + 1, :] = square_rows(src[a])
    expand(sq_tgt[...] * -KAPPA, wide)
    sums = tile_sums(source_tiles(tiles, tgt.shape[0]), tiles[0, 0], tgt, src, wide, peaks, totals)
    out[...] = jnp.broadcast_to(sums[None], out.shape)


def source_kernel(log_cells, picked, src, tgt, parts, out, wide, peaks, totals, tiles, sem):
    fetch = pltpu.make_async_copy(picked, tiles, sem)
    fetch.start()
    expand(-log_cells - log_sum(parts[...]), wide)
    fetch.wait()
    sums = tile_sums(source_tiles(tiles, tgt.shape[0]), tiles[0, 0], tgt, src, wide, peaks, totals)
    out[...] = jnp.broadcast_to(sums[None], out.shape)


def target_kernel(log_cells, picked, src, tgt, parts, sq_src, out, pot, wide, peaks, totals, tiles, sem):
    fetch = pltpu.make_async_copy(picked, tiles, sem)
    fetch.start()
    weights = -log_cells - log_sum(parts[...])
    pot[...] = weights * (1.0 / KAPPA) + sq_src[...]
    expand(weights, wide)
    fetch.wait()
    sums = tile_sums(target_tiles(tiles, tgt.shape[0]), tiles[0, 0], src, tgt, wide, peaks, totals)
    copies, blocks = out.shape[0], out.shape[1]
    if blocks == sums.shape[0]:
        out[...] = jnp.broadcast_to(sums[None], out.shape)
    else:
        cols = sums.shape[0] // blocks
        each = copies // cols
        for col in range(cols):
            piece = sums[col * blocks : (col + 1) * blocks]
            out[col * each : (col + 1) * each] = jnp.broadcast_to(piece[None], (each,) + piece.shape)


def last_kernel(log_cells, parity, parts, sq_tgt, mine, other, tgt_pot, src_pot):
    p = parity[0]
    blocks = tgt_pot.shape[0]
    squares = jnp.where(p == 0, sq_tgt[0:blocks], sq_tgt[blocks : 2 * blocks])
    tgt_pot[...] = (-log_cells - log_sum(parts[...])) * (1.0 / KAPPA) + squares
    src_pot[:, 0, :] = jnp.where(p == 0, mine[...], other[...])
    src_pot[:, 1, :] = jnp.where(p == 0, other[...], mine[...])


def half_step(kernel, outs, near_blocks, slots, picked, *args):
    return pl.pallas_call(
        kernel,
        out_shape=[s if isinstance(s, jax.ShapeDtypeStruct) else jax.ShapeDtypeStruct(s, F32) for s in outs],
        in_specs=[ANY] + [VMEM] * len(args),
        out_specs=[VMEM] * len(outs),
        scratch_shapes=[
            pltpu.VMEM((near_blocks, TILE, TILE), F32),
            pltpu.VMEM((slots + 1, 8, TILE), F32),
            pltpu.VMEM((slots + 1, 8, TILE), F32),
            pltpu.SMEM(picked.shape, picked.dtype),
            pltpu.SemaphoreType.DMA,
        ],
        compiler_params=PARAMS,
    )(picked, *args)


def exchange(copies, peers):
    return lax.all_to_all(copies, peers, 0, 0, tiled=True)


def shifts(block, axis):
    n = lax.axis_size(axis)
    turn = lambda d: lax.ppermute(block, axis, [(i, (i + d) % n) for i in range(n)])
    return [block] + [turn(d) for d in range(1, n)]


def bands(src_embed, tgt_embed, lists):
    block = jax.ShapeDtypeStruct(src_embed.shape, src_embed.dtype)
    own = pl.pallas_call(
        own_kernel, out_shape=[block] * 2, in_specs=[VMEM] * 2, out_specs=[VMEM] * 2, compiler_params=PARAMS
    )(src_embed, tgt_embed)
    src_blocks, tgt_blocks = shifts(src_embed, "s")[1:], shifts(tgt_embed, "y")[1:]
    blocks = [own[0]] + src_blocks + [own[1]] + tgt_blocks
    group = jax.ShapeDtypeStruct((1 + len(src_blocks),) + src_embed.shape, src_embed.dtype)
    src, tgt = pl.pallas_call(
        pack_kernel,
        out_shape=[group] * 2,
        in_specs=[ANY] + [VMEM] * len(blocks),
        out_specs=[VMEM] * 2,
        compiler_params=PARAMS,
    )(lists, *blocks)
    mine, partner = shifts(tgt, "p")
    mine = pl.pallas_call(
        after_kernel, out_shape=group, in_specs=[ANY, VMEM], out_specs=VMEM, compiler_params=PARAMS
    )(partner, mine)
    return shifts(src, "x"), [piece for side in (mine, partner) for piece in shifts(side, "core")]


def local(src_embed, tgt_embed, tiles, counts):
    rows, cols = lax.axis_size(ROW), lax.axis_size(COL)
    log_cells = math.log2(rows * cols * TILE)
    parity = lax.axis_index("p").astype(jnp.int32).reshape(1)
    partner = lambda v: lax.ppermute(v, "p", [(0, 1), (1, 0)])

    lists = jnp.concatenate([tiles[0, 0], jnp.broadcast_to(counts[0, 0], (1, TILE))], axis=0)
    other_lists = partner(lists)
    src_pieces, tgt_pieces = bands(src_embed, tgt_embed, other_lists)
    place = jnp.stack([lax.axis_index(a) for a in ("x", "s", "y", "p", "core")]).astype(jnp.int32)
    picked = pl.pallas_call(
        pick_kernel,
        out_shape=jax.ShapeDtypeStruct((8, TILE), jnp.int32),
        in_specs=[SMEM] * 3,
        out_specs=SMEM,
        compiler_params=PARAMS,
    )(lists, other_lists, place)

    srcs, tgts = (len(pieces) * pieces[0].shape[0] for pieces in (src_pieces, tgt_pieces))
    src_shape = jax.ShapeDtypeStruct((srcs,) + src_embed.shape, src_embed.dtype)
    tgt_shape = jax.ShapeDtypeStruct((tgts,) + tgt_embed.shape, tgt_embed.dtype)
    slots = srcs * tgts
    src_out, tgt_out = (srcs, srcs, TILE), (tgts, tgts, TILE)
    for sweep in range(ITERS):
        if sweep == 0:
            parts, src, tgt, sq_src, sq_tgt = half_step(
                first_kernel,
                [src_out, src_shape, tgt_shape, (srcs, TILE), (tgts, TILE)],
                tgts,
                slots,
                picked,
                *src_pieces,
                *tgt_pieces,
            )
        else:
            (parts,) = half_step(
                functools.partial(source_kernel, log_cells), [src_out], tgts, slots, picked, src, tgt, parts
            )
        parts = exchange(parts, SRC_PEERS)
        last = sweep == ITERS - 1
        parts, src_pot = half_step(
            functools.partial(target_kernel, log_cells),
            [(tgts, rows, TILE) if last else tgt_out, (srcs, TILE)],
            srcs,
            slots,
            picked,
            src,
            tgt,
            parts,
            sq_src,
        )
        if last:
            other_pot = partner(src_pot)
        parts = exchange(parts, TGT_PEERS)
    tgt_pot, both = pl.pallas_call(
        functools.partial(last_kernel, log_cells),
        out_shape=[jax.ShapeDtypeStruct((rows, TILE), F32), jax.ShapeDtypeStruct((srcs, 2, TILE), F32)],
        in_specs=[SMEM] + [VMEM] * 4,
        out_specs=[VMEM] * 2,
        compiler_params=PARAMS,
    )(parity, parts, sq_tgt, src_pot, other_pot)
    return (both.reshape(-1), tgt_pot.reshape(-1))


def solution(mesh):
    fine = Mesh(mesh.devices.reshape(4, 2, 4, 4, 2), ROW + COL)
    in_specs = (P(ROW + COL, None), P(COL + ROW, None), P(ROW, COL, None, None), P(ROW, COL))
    return jax.shard_map(local, mesh=fine, in_specs=in_specs, out_specs=(P(ROW), P(COL)), check_vma=False)
```

```python
import functools
import math

import jax
import jax.numpy as jnp
from jax import lax
from jax.experimental import pallas as pl
from jax.experimental.pallas import tpu as pltpu
from jax.sharding import Mesh
from jax.sharding import PartitionSpec as P

TILE = 128
LOG_TILE = 7
ITERS = 2
ENTROPY = 0.05
KAPPA = math.log2(math.e) / ENTROPY
EMPTY = -1e30
UNROLL = 16
ROW = ("y", "core")
COL = ("x", "s", "p")
SRC_PEERS = ("x", "s")
TGT_PEERS = ("p", "y", "core")
F32 = jnp.float32
NT = (((1,), (1,)), ((), ()))
VMEM = pl.BlockSpec(memory_space=pltpu.VMEM)
SMEM = pl.BlockSpec(memory_space=pltpu.SMEM)
ANY = pl.BlockSpec(memory_space=pl.ANY)
PARAMS = pltpu.CompilerParams(vmem_limit_bytes=24 * 2**20)


def square_rows(cells):
    wide = cells.astype(F32)
    square = wide * wide
    high = square.astype(jnp.bfloat16)
    low = (square - high.astype(F32)).astype(jnp.bfloat16)
    ones = jnp.ones((8, cells.shape[1]), jnp.bfloat16)
    total = lax.dot_general(ones, high, NT, preferred_element_type=F32)
    total += lax.dot_general(ones, low, NT, preferred_element_type=F32)
    return total[0:1]


def log_sum(parts):
    highest = jnp.max(parts, axis=0)
    return highest + jnp.log2(jnp.sum(jnp.exp2(parts - highest[None]), axis=0))


def expand(weights, wide):
    blocks = weights.shape[0]
    columns = jnp.concatenate([weights, jnp.zeros((TILE - blocks, TILE), F32)], axis=0).T
    for n in range(blocks):
        wide[n] = jnp.broadcast_to(columns[:, n : n + 1], (TILE, TILE))


def tile_sums(tile, count, near, far, wide, peaks, totals):
    near_blocks, far_blocks = near.shape[0], far.shape[0]
    spare = near_blocks * far_blocks
    peaks[...] = jnp.full(peaks.shape, EMPTY, F32)
    totals[...] = jnp.zeros(totals.shape, F32)

    @pl.loop(0, (count + UNROLL - 1) // UNROLL)
    def _(step):
        for u in range(UNROLL):
            k = step * UNROLL + u
            n, f = tile(jnp.where(k < count, k, 0))
            inner = lax.dot_general(near[n], far[f], NT, preferred_element_type=F32)
            score = (inner * (2.0 * KAPPA) + wide[n]).reshape(TILE // 8, 8, TILE)
            peak = jnp.max(score, axis=0)
            slot = jnp.where(k < count, f * near_blocks + n, spare)
            peaks[slot] = peak
            totals[slot] = jnp.sum(jnp.exp2(score - peak[None]), axis=0)

    rows = []
    for f in range(far_blocks):
        at = pl.ds(f * near_blocks, near_blocks)
        peak = peaks[at]
        highest = jnp.max(jnp.max(peak, axis=0), axis=0, keepdims=True)
        whole = jnp.sum(totals[at] * jnp.exp2(peak - highest[None]), axis=0)
        whole = jnp.sum(whole, axis=0, keepdims=True)
        rows.append(jnp.where(whole > 0.0, highest + jnp.log2(whole), EMPTY))
    return jnp.concatenate(rows, axis=0)


def pick_kernel(mine, other, place, picked):
    p = place[3]
    targets = 8
    slots = 2 * TILE

    def put(lists, k, col, at):
        a, b = lists[0, k], lists[1, k]
        picked[1 + (at >> LOG_TILE), at & (TILE - 1)] = (a >> 1) * (2 * targets) + col * targets + b
        return jnp.where((k < lists[2, 0]) & ((a & 1) == p), 1, 0)

    def step(k, ends):
        front, back = ends
        front = front + put(mine, k, p, front)
        return front, back - put(other, k, 1 - p, back)

    front, back = lax.fori_loop(0, TILE, step, (jnp.int32(0), jnp.int32(slots - 1)), unroll=8)
    picked[0, 0] = front
    picked[0, 1] = front + (slots - 1) - back
    for n in range(place.shape[0]):
        picked[0, 2 + n] = place[n]


def tile_code(tiles, k):
    first = tiles[0, 0]
    at = jnp.where(k < first, k, 2 * TILE - 1 + first - k)
    return tiles[1 + (at >> LOG_TILE), at & (TILE - 1)]


def source_tiles(tiles, tgt_blocks):
    def tile(k):
        code = tile_code(tiles, k)
        return lax.rem(code, tgt_blocks), lax.div(code, tgt_blocks)

    return tile


def target_tiles(tiles, tgt_blocks):
    def tile(k):
        code = tile_code(tiles, k)
        return lax.div(code, tgt_blocks), lax.rem(code, tgt_blocks)

    return tile


def pack_kernel(lists, own, *refs):
    src, tgt = refs[-2:]
    sides = src.shape[0]
    src[0] = own[0]
    tgt[0] = own[1]
    for n in range(1, sides):
        src[n] = refs[n - 1][...]
        tgt[n] = refs[sides - 1 + n - 1][...]


def after_kernel(first, block, out):
    out[...] = block[...]


def square_kernel(src, sq_src):
    for a in range(src.shape[0]):
        sq_src[a : a + 1, :] = square_rows(src[a])


def first_kernel(picked, *refs):
    pieces, (out, src, tgt, sq_src, sq_tgt, wide, peaks, totals, tiles, sem) = refs[:-10], refs[-10:]
    fetch = pltpu.make_async_copy(picked, tiles, sem)
    fetch.start()
    sides = len(pieces) // 2
    fetch.wait()
    place = [tiles[0, 2 + n] for n in range(5)]
    for d in range(sides):
        x = lax.rem(place[0] + (sides - d), sides)
        p, core = place[3] ^ (d // 2), place[4] ^ (d % 2)
        for n in range(sides):
            s, y = (lax.rem(place[axis] + (sides - n), sides) for axis in (1, 2))
            src[x * sides + s] = pieces[d][n]
            tgt[p * (2 * sides) + 2 * y + core] = pieces[sides + d][n]
    for b in range(tgt.shape[0]):
        sq_tgt[b : b + 1, :] = square_rows(tgt[b])
    for a in range(src.shape[0]):
        sq_src[a : a + 1, :] = square_rows(src[a])
    expand(sq_tgt[...] * -KAPPA, wide)
    sums = tile_sums(source_tiles(tiles, tgt.shape[0]), tiles[0, 1], tgt, src, wide, peaks, totals)
    out[...] = jnp.broadcast_to(sums[None], out.shape)


def source_kernel(log_cells, picked, src, tgt, parts, out, wide, peaks, totals, tiles, sem):
    fetch = pltpu.make_async_copy(picked, tiles, sem)
    fetch.start()
    expand(-log_cells - log_sum(parts[...]), wide)
    fetch.wait()
    sums = tile_sums(source_tiles(tiles, tgt.shape[0]), tiles[0, 1], tgt, src, wide, peaks, totals)
    out[...] = jnp.broadcast_to(sums[None], out.shape)


def target_kernel(log_cells, picked, src, tgt, parts, *refs):
    refs, (wide, peaks, totals, tiles, sem) = refs[:-5], refs[-5:]
    fetch = pltpu.make_async_copy(picked, tiles, sem)
    fetch.start()
    weights = -log_cells - log_sum(parts[...])
    expand(weights, wide)
    fetch.wait()
    sums = tile_sums(target_tiles(tiles, tgt.shape[0]), tiles[0, 1], src, tgt, wide, peaks, totals)
    if len(refs) == 1:
        (out,) = refs
        out[...] = jnp.broadcast_to(sums[None], out.shape)
    else:
        sq_src, out, pot = refs
        pot[...] = weights * (1.0 / KAPPA) + sq_src[...]
        copies, blocks = out.shape[0], out.shape[1]
        cols = sums.shape[0] // blocks
        each = copies // cols
        for col in range(cols):
            piece = sums[col * blocks : (col + 1) * blocks]
            out[col * each : (col + 1) * each] = jnp.broadcast_to(piece[None], (each,) + piece.shape)


def last_kernel(log_cells, parity, parts, sq_tgt, mine, other, tgt_pot, src_pot):
    p = parity[0]
    blocks = tgt_pot.shape[0]
    squares = jnp.where(p == 0, sq_tgt[0:blocks], sq_tgt[blocks : 2 * blocks])
    tgt_pot[...] = (-log_cells - log_sum(parts[...])) * (1.0 / KAPPA) + squares
    src_pot[:, 0, :] = jnp.where(p == 0, mine[...], other[...])
    src_pot[:, 1, :] = jnp.where(p == 0, other[...], mine[...])


def half_step(kernel, outs, near_blocks, slots, picked, *args):
    return pl.pallas_call(
        kernel,
        out_shape=[s if isinstance(s, jax.ShapeDtypeStruct) else jax.ShapeDtypeStruct(s, F32) for s in outs],
        in_specs=[ANY] + [VMEM] * len(args),
        out_specs=[VMEM] * len(outs),
        scratch_shapes=[
            pltpu.VMEM((near_blocks, TILE, TILE), F32),
            pltpu.VMEM((slots + 1, 8, TILE), F32),
            pltpu.VMEM((slots + 1, 8, TILE), F32),
            pltpu.SMEM(picked.shape, picked.dtype),
            pltpu.SemaphoreType.DMA,
        ],
        compiler_params=PARAMS,
    )(picked, *args)


def exchange(copies, peers):
    return lax.all_to_all(copies, peers, 0, 0, tiled=True)


def shifts(block, axis):
    n = lax.axis_size(axis)
    turn = lambda d: lax.ppermute(block, axis, [(i, (i + d) % n) for i in range(n)])
    return [block] + [turn(d) for d in range(1, n)]


def bands(src_embed, tgt_embed, lists):
    own = jnp.stack([src_embed, tgt_embed])
    far = shifts(src_embed, "s")[1:] + shifts(tgt_embed, "y")[1:]
    group = jax.ShapeDtypeStruct((lax.axis_size("s"),) + src_embed.shape, src_embed.dtype)
    src, tgt = pl.pallas_call(
        pack_kernel,
        out_shape=[group] * 2,
        in_specs=[ANY] + [VMEM] * (1 + len(far)),
        out_specs=[VMEM] * 2,
        compiler_params=PARAMS,
    )(lists, own, *far)
    src_pieces = shifts(src, "x")
    mine, partner = shifts(tgt, "p")
    mine = pl.pallas_call(
        after_kernel, out_shape=group, in_specs=[ANY, VMEM], out_specs=VMEM, compiler_params=PARAMS
    )(partner, mine)
    return src_pieces, [piece for side in (mine, partner) for piece in shifts(side, "core")]


def local(src_embed, tgt_embed, tiles, counts):
    rows, cols = lax.axis_size(ROW), lax.axis_size(COL)
    log_cells = math.log2(rows * cols * TILE)
    parity = lax.axis_index("p").astype(jnp.int32).reshape(1)
    partner = lambda v: lax.ppermute(v, "p", [(0, 1), (1, 0)])

    lists = jnp.concatenate([tiles[0, 0], jnp.broadcast_to(counts[0, 0], (1, TILE))], axis=0)
    other_lists = partner(lists)
    place = jnp.stack([lax.axis_index(a) for a in ("x", "s", "y", "p", "core")]).astype(jnp.int32)
    src_pieces, tgt_pieces = bands(src_embed, tgt_embed, other_lists)
    picked = pl.pallas_call(
        pick_kernel,
        out_shape=jax.ShapeDtypeStruct((8, TILE), jnp.int32),
        in_specs=[SMEM] * 3,
        out_specs=SMEM,
        compiler_params=PARAMS,
    )(lists, other_lists, place)

    srcs, tgts = (len(pieces) * pieces[0].shape[0] for pieces in (src_pieces, tgt_pieces))
    tgt_shape = jax.ShapeDtypeStruct((tgts,) + tgt_embed.shape, tgt_embed.dtype)
    src_shape = jax.ShapeDtypeStruct((srcs,) + src_embed.shape, src_embed.dtype)
    slots = srcs * tgts
    src_out, tgt_out = (srcs, srcs, TILE), (tgts, tgts, TILE)
    for sweep in range(ITERS):
        if sweep == 0:
            outs = [src_out, src_shape, tgt_shape, (srcs, TILE), (tgts, TILE)]
            parts, src, tgt, sq_src, sq_tgt = half_step(first_kernel, outs, tgts, slots, picked, *src_pieces, *tgt_pieces)
        else:
            (parts,) = half_step(
                functools.partial(source_kernel, log_cells), [src_out], tgts, slots, picked, src, tgt, parts
            )
        parts = exchange(parts, SRC_PEERS)
        step = functools.partial(target_kernel, log_cells)
        if sweep < ITERS - 1:
            (parts,) = half_step(step, [tgt_out], srcs, slots, picked, src, tgt, parts)
        else:
            outs = [(tgts, rows, TILE), (srcs, TILE)]
            parts, src_pot = half_step(step, outs, srcs, slots, picked, src, tgt, parts, sq_src)
            other_pot = partner(src_pot)
        parts = exchange(parts, TGT_PEERS)
    tgt_pot, both = pl.pallas_call(
        functools.partial(last_kernel, log_cells),
        out_shape=[jax.ShapeDtypeStruct((rows, TILE), F32), jax.ShapeDtypeStruct((srcs, 2, TILE), F32)],
        in_specs=[SMEM] + [VMEM] * 4,
        out_specs=[VMEM] * 2,
        compiler_params=PARAMS,
    )(parity, parts, sq_tgt, src_pot, other_pot)
    return (both.reshape(-1), tgt_pot.reshape(-1))


def solution(mesh):
    fine = Mesh(mesh.devices.reshape(4, 2, 4, 4, 2), ROW + COL)
    in_specs = (P(ROW + COL, None), P(COL + ROW, None), P(ROW, COL, None, None), P(ROW, COL))
    return jax.shard_map(local, mesh=fine, in_specs=in_specs, out_specs=(P(ROW), P(COL)), check_vma=False)
```

```python
import functools
import math

import jax
import jax.numpy as jnp
from jax import lax
from jax.experimental import pallas as pl
from jax.experimental.pallas import tpu as pltpu
from jax.sharding import Mesh
from jax.sharding import PartitionSpec as P

TILE = 128
LOG_TILE = 7
ENTROPY = 0.05
KAPPA = math.log2(math.e) / ENTROPY
EMPTY = -1e30
UNROLL = 16
ROW = ("y", "core")
COL = ("x", "s", "p")
SRC_PEERS = ("x", "s")
TGT_PEERS = ("p", "y", "core")
F32 = jnp.float32
NT = (((1,), (1,)), ((), ()))
VMEM = pl.BlockSpec(memory_space=pltpu.VMEM)
SMEM = pl.BlockSpec(memory_space=pltpu.SMEM)
ANY = pl.BlockSpec(memory_space=pl.ANY)
PARAMS = pltpu.CompilerParams(vmem_limit_bytes=48 * 2**20)


def square_rows(cells):
    wide = cells.astype(F32)
    square = wide * wide
    high = square.astype(jnp.bfloat16)
    low = (square - high.astype(F32)).astype(jnp.bfloat16)
    ones = jnp.ones((8, cells.shape[1]), jnp.bfloat16)
    total = lax.dot_general(ones, high, NT, preferred_element_type=F32)
    total += lax.dot_general(ones, low, NT, preferred_element_type=F32)
    return total[0:1]


def log_sum(parts):
    highest = jnp.max(parts, axis=0)
    return highest + jnp.log2(jnp.sum(jnp.exp2(parts - highest[None]), axis=0))


def expand(weights, wide):
    blocks = weights.shape[0]
    columns = jnp.concatenate([weights, jnp.zeros((TILE - blocks, TILE), F32)], axis=0).T
    for n in range(blocks):
        wide[n] = jnp.broadcast_to(columns[:, n : n + 1], (TILE, TILE))


def dot_tiles(near, far, saved, stage, sems):
    def out(step):
        half = step & 1
        return pltpu.make_async_copy(stage.at[half], saved.at[pl.ds(step * UNROLL, UNROLL)], sems.at[half])

    def before(step, steps):
        pl.when(step >= 2)(lambda: out(step - 2).wait())

    def tile(step, u, n, f):
        inner = lax.dot_general(near[n], far[f], NT, preferred_element_type=F32) * (2.0 * KAPPA)
        stage[step & 1, u] = inner
        return inner

    def after(step):
        out(step).start()

    def end(steps):
        pl.when(steps >= 2)(lambda: out(steps - 2).wait())
        pl.when(steps >= 1)(lambda: out(steps - 1).wait())

    return before, tile, after, end


def saved_tiles(saved, stage, sems):
    def fetch(step):
        half = step & 1
        return pltpu.make_async_copy(saved.at[pl.ds(step * UNROLL, UNROLL)], stage.at[half], sems.at[half])

    def before(step, steps):
        pl.when(step + 1 < steps)(lambda: fetch(step + 1).start())
        fetch(step).wait()

    def tile(step, u, n, f):
        return stage[step & 1, u]

    def after(step):
        pass

    def end(steps):
        pl.when(steps == 0)(lambda: fetch(0).wait())

    return fetch, (before, tile, after, end)


def tile_sums(place_of, count, source, near_blocks, far_blocks, wide, peaks, totals):
    spare = near_blocks * far_blocks
    before, tile, after, end = source
    peaks[...] = jnp.full(peaks.shape, EMPTY, F32)
    totals[...] = jnp.zeros(totals.shape, F32)
    steps = (count + UNROLL - 1) // UNROLL

    @pl.loop(0, steps)
    def _(step):
        before(step, steps)
        for u in range(UNROLL):
            k = step * UNROLL + u
            n, f = place_of(jnp.where(k < count, k, 0))
            score = (tile(step, u, n, f) + wide[n]).reshape(TILE // 8, 8, TILE)
            peak = jnp.max(score, axis=0)
            slot = jnp.where(k < count, f * near_blocks + n, spare)
            peaks[slot] = peak
            totals[slot] = jnp.sum(jnp.exp2(score - peak[None]), axis=0)
        after(step)

    end(steps)
    rows = []
    for f in range(far_blocks):
        at = pl.ds(f * near_blocks, near_blocks)
        peak = peaks[at]
        highest = jnp.max(jnp.max(peak, axis=0), axis=0, keepdims=True)
        whole = jnp.sum(totals[at] * jnp.exp2(peak - highest[None]), axis=0)
        whole = jnp.sum(whole, axis=0, keepdims=True)
        rows.append(jnp.where(whole > 0.0, highest + jnp.log2(whole), EMPTY))
    return jnp.concatenate(rows, axis=0)


def pick_kernel(mine, other, place, picked):
    p = place[3]
    targets = 8
    slots = 2 * TILE

    def put(lists, k, col, at):
        a, b = lists[0, k], lists[1, k]
        picked[1 + (at >> LOG_TILE), at & (TILE - 1)] = (a >> 1) * (2 * targets) + col * targets + b
        return jnp.where((k < lists[2, 0]) & ((a & 1) == p), 1, 0)

    def step(k, ends):
        front, back = ends
        front = front + put(mine, k, p, front)
        return front, back - put(other, k, 1 - p, back)

    front, back = lax.fori_loop(0, TILE, step, (jnp.int32(0), jnp.int32(slots - 1)), unroll=8)
    picked[0, 0] = front
    picked[0, 1] = front + (slots - 1) - back
    for n in range(place.shape[0]):
        picked[0, 2 + n] = place[n]


def tile_code(tiles, k):
    first = tiles[0, 0]
    at = jnp.where(k < first, k, 2 * TILE - 1 + first - k)
    return tiles[1 + (at >> LOG_TILE), at & (TILE - 1)]


def source_tiles(tiles, tgt_blocks):
    def tile(k):
        code = tile_code(tiles, k)
        return lax.rem(code, tgt_blocks), lax.div(code, tgt_blocks)

    return tile


def target_tiles(tiles, tgt_blocks):
    def tile(k):
        code = tile_code(tiles, k)
        return lax.div(code, tgt_blocks), lax.rem(code, tgt_blocks)

    return tile


def pack_kernel(lists, own, *refs):
    src, tgt = refs[-2:]
    sides = src.shape[0]
    src[0] = own[0]
    tgt[0] = own[1]
    for n in range(1, sides):
        src[n] = refs[n - 1][...]
        tgt[n] = refs[sides - 1 + n - 1][...]


def after_kernel(first, block, out):
    out[...] = block[...]


def square_kernel(src, sq_src):
    for a in range(src.shape[0]):
        sq_src[a : a + 1, :] = square_rows(src[a])


def first_kernel(picked, *refs):
    pieces, refs = refs[:-13], refs[-13:]
    out, src, tgt, sq_src, sq_tgt, saved, wide, peaks, totals, tiles, sem, stage, sems = refs
    fetch = pltpu.make_async_copy(picked, tiles, sem)
    fetch.start()
    sides = len(pieces) // 2
    fetch.wait()
    place = [tiles[0, 2 + n] for n in range(5)]
    for d in range(sides):
        x = lax.rem(place[0] + (sides - d), sides)
        p, core = place[3] ^ (d // 2), place[4] ^ (d % 2)
        for n in range(sides):
            s, y = (lax.rem(place[axis] + (sides - n), sides) for axis in (1, 2))
            src[x * sides + s] = pieces[d][n]
            tgt[p * (2 * sides) + 2 * y + core] = pieces[sides + d][n]
    srcs, tgts = src.shape[0], tgt.shape[0]
    for b in range(tgts):
        sq_tgt[b : b + 1, :] = square_rows(tgt[b])
    for a in range(srcs):
        sq_src[a : a + 1, :] = square_rows(src[a])
    expand(sq_tgt[...] * -KAPPA, wide)
    source = dot_tiles(tgt, src, saved, stage, sems)
    sums = tile_sums(source_tiles(tiles, tgts), tiles[0, 1], source, tgts, srcs, wide, peaks, totals)
    out[...] = jnp.broadcast_to(sums[None], out.shape)


def target_kernel(log_cells, picked, src, tgt, parts, out, saved, wide, peaks, totals, tiles, sem, stage, sems):
    fetch = pltpu.make_async_copy(picked, tiles, sem)
    fetch.start()
    expand(-log_cells - log_sum(parts[...]), wide)
    fetch.wait()
    srcs, tgts = src.shape[0], tgt.shape[0]
    source = dot_tiles(src, tgt, saved, stage, sems)
    sums = tile_sums(target_tiles(tiles, tgts), tiles[0, 1], source, srcs, tgts, wide, peaks, totals)
    out[...] = jnp.broadcast_to(sums[None], out.shape)


def again_source_kernel(log_cells, picked, saved, parts, out, wide, peaks, totals, tiles, sem, stage, sems):
    fetch = pltpu.make_async_copy(picked, tiles, sem)
    fetch.start()
    read, source = saved_tiles(saved, stage, sems)
    read(0).start()
    tgts, srcs = parts.shape[1], out.shape[1]
    expand(-log_cells - log_sum(parts[...]), wide)
    fetch.wait()
    sums = tile_sums(source_tiles(tiles, tgts), tiles[0, 1], source, tgts, srcs, wide, peaks, totals)
    out[...] = jnp.broadcast_to(sums[None], out.shape)


def again_target_kernel(
    log_cells, tgts, picked, saved, parts, sq_src, out, pot, wide, peaks, totals, tiles, sem, stage, sems
):
    fetch = pltpu.make_async_copy(picked, tiles, sem)
    fetch.start()
    read, source = saved_tiles(saved, stage, sems)
    read(0).start()
    srcs = parts.shape[1]
    weights = -log_cells - log_sum(parts[...])
    pot[...] = weights * (1.0 / KAPPA) + sq_src[...]
    expand(weights, wide)
    fetch.wait()
    sums = tile_sums(target_tiles(tiles, tgts), tiles[0, 1], source, srcs, tgts, wide, peaks, totals)
    copies, blocks = out.shape[0], out.shape[1]
    cols = tgts // blocks
    each = copies // cols
    for col in range(cols):
        piece = sums[col * blocks : (col + 1) * blocks]
        out[col * each : (col + 1) * each] = jnp.broadcast_to(piece[None], (each,) + piece.shape)


def last_kernel(log_cells, parity, parts, sq_tgt, mine, other, tgt_pot, src_pot):
    p = parity[0]
    blocks = tgt_pot.shape[0]
    squares = jnp.where(p == 0, sq_tgt[0:blocks], sq_tgt[blocks : 2 * blocks])
    tgt_pot[...] = (-log_cells - log_sum(parts[...])) * (1.0 / KAPPA) + squares
    src_pot[:, 0, :] = jnp.where(p == 0, mine[...], other[...])
    src_pot[:, 1, :] = jnp.where(p == 0, other[...], mine[...])


def half_step(kernel, outs, near_blocks, slots, picked, *args, reads=0, writes=0):
    return pl.pallas_call(
        kernel,
        out_shape=[s if isinstance(s, jax.ShapeDtypeStruct) else jax.ShapeDtypeStruct(s, F32) for s in outs],
        in_specs=[ANY] * (1 + reads) + [VMEM] * (len(args) - reads),
        out_specs=[VMEM] * (len(outs) - writes) + [ANY] * writes,
        scratch_shapes=[
            pltpu.VMEM((near_blocks, TILE, TILE), F32),
            pltpu.VMEM((slots + 1, 8, TILE), F32),
            pltpu.VMEM((slots + 1, 8, TILE), F32),
            pltpu.SMEM(picked.shape, picked.dtype),
            pltpu.SemaphoreType.DMA,
            pltpu.VMEM((2, UNROLL, TILE, TILE), F32),
            pltpu.SemaphoreType.DMA((2,)),
        ],
        compiler_params=PARAMS,
    )(picked, *args)


def exchange(copies, peers):
    return lax.all_to_all(copies, peers, 0, 0, tiled=True)


def shifts(block, axis):
    n = lax.axis_size(axis)
    turn = lambda d: lax.ppermute(block, axis, [(i, (i + d) % n) for i in range(n)])
    return [block] + [turn(d) for d in range(1, n)]


def bands(src_embed, tgt_embed, lists):
    own = jnp.stack([src_embed, tgt_embed])
    far = shifts(src_embed, "s")[1:] + shifts(tgt_embed, "y")[1:]
    group = jax.ShapeDtypeStruct((lax.axis_size("s"),) + src_embed.shape, src_embed.dtype)
    src, tgt = pl.pallas_call(
        pack_kernel,
        out_shape=[group] * 2,
        in_specs=[ANY] + [VMEM] * (1 + len(far)),
        out_specs=[VMEM] * 2,
        compiler_params=PARAMS,
    )(lists, own, *far)
    src_pieces = shifts(src, "x")
    mine, partner = shifts(tgt, "p")
    mine = pl.pallas_call(
        after_kernel, out_shape=group, in_specs=[ANY, VMEM], out_specs=VMEM, compiler_params=PARAMS
    )(partner, mine)
    return src_pieces, [piece for side in (mine, partner) for piece in shifts(side, "core")]


def local(src_embed, tgt_embed, tiles, counts):
    rows, cols = lax.axis_size(ROW), lax.axis_size(COL)
    log_cells = math.log2(rows * cols * TILE)
    parity = lax.axis_index("p").astype(jnp.int32).reshape(1)
    partner = lambda v: lax.ppermute(v, "p", [(0, 1), (1, 0)])

    lists = jnp.concatenate([tiles[0, 0], jnp.broadcast_to(counts[0, 0], (1, TILE))], axis=0)
    other_lists = partner(lists)
    place = jnp.stack([lax.axis_index(a) for a in ("x", "s", "y", "p", "core")]).astype(jnp.int32)
    src_pieces, tgt_pieces = bands(src_embed, tgt_embed, other_lists)
    picked = pl.pallas_call(
        pick_kernel,
        out_shape=jax.ShapeDtypeStruct((8, TILE), jnp.int32),
        in_specs=[SMEM] * 3,
        out_specs=SMEM,
        compiler_params=PARAMS,
    )(lists, other_lists, place)

    srcs, tgts = (len(pieces) * pieces[0].shape[0] for pieces in (src_pieces, tgt_pieces))
    tgt_shape = jax.ShapeDtypeStruct((tgts,) + tgt_embed.shape, tgt_embed.dtype)
    src_shape = jax.ShapeDtypeStruct((srcs,) + src_embed.shape, src_embed.dtype)
    slots = srcs * tgts
    src_out, tgt_out, all_tiles = (srcs, srcs, TILE), (tgts, tgts, TILE), (slots, TILE, TILE)
    outs = [src_out, src_shape, tgt_shape, (srcs, TILE), (tgts, TILE), all_tiles]
    parts, src, tgt, sq_src, sq_tgt, src_saved = half_step(
        first_kernel, outs, tgts, slots, picked, *src_pieces, *tgt_pieces, writes=1
    )
    parts = exchange(parts, SRC_PEERS)
    step = functools.partial(target_kernel, log_cells)
    parts, tgt_saved = half_step(step, [tgt_out, all_tiles], srcs, slots, picked, src, tgt, parts, writes=1)
    parts = exchange(parts, TGT_PEERS)
    step = functools.partial(again_source_kernel, log_cells)
    (parts,) = half_step(step, [src_out], tgts, slots, picked, src_saved, parts, reads=1)
    parts = exchange(parts, SRC_PEERS)
    step = functools.partial(again_target_kernel, log_cells, tgts)
    outs = [(tgts, rows, TILE), (srcs, TILE)]
    parts, src_pot = half_step(step, outs, srcs, slots, picked, tgt_saved, parts, sq_src, reads=1)
    other_pot = partner(src_pot)
    parts = exchange(parts, TGT_PEERS)
    tgt_pot, both = pl.pallas_call(
        functools.partial(last_kernel, log_cells),
        out_shape=[jax.ShapeDtypeStruct((rows, TILE), F32), jax.ShapeDtypeStruct((srcs, 2, TILE), F32)],
        in_specs=[SMEM] + [VMEM] * 4,
        out_specs=[VMEM] * 2,
        compiler_params=PARAMS,
    )(parity, parts, sq_tgt, src_pot, other_pot)
    return (both.reshape(-1), tgt_pot.reshape(-1))


def solution(mesh):
    fine = Mesh(mesh.devices.reshape(4, 2, 4, 4, 2), ROW + COL)
    in_specs = (P(ROW + COL, None), P(COL + ROW, None), P(ROW, COL, None, None), P(ROW, COL))
    return jax.shard_map(local, mesh=fine, in_specs=in_specs, out_specs=(P(ROW), P(COL)), check_vma=False)
```

```python
import functools
import math

import jax
import jax.numpy as jnp
from jax import lax
from jax.experimental import pallas as pl
from jax.experimental.pallas import tpu as pltpu
from jax.sharding import Mesh
from jax.sharding import PartitionSpec as P

TILE = 128
LOG_TILE = 7
ENTROPY = 0.05
KAPPA = math.log2(math.e) / ENTROPY
EMPTY = -1e30
UNROLL = 16
ROW = ("y", "core")
COL = ("x", "s", "p")
SRC_PEERS = ("x", "s")
TGT_PEERS = ("p", "y", "core")
F32 = jnp.float32
NT = (((1,), (1,)), ((), ()))
VMEM = pl.BlockSpec(memory_space=pltpu.VMEM)
SMEM = pl.BlockSpec(memory_space=pltpu.SMEM)
ANY = pl.BlockSpec(memory_space=pl.ANY)
PARAMS = pltpu.CompilerParams(vmem_limit_bytes=10 * 2**20)


def square_rows(cells):
    wide = cells.astype(F32)
    square = wide * wide
    high = square.astype(jnp.bfloat16)
    low = (square - high.astype(F32)).astype(jnp.bfloat16)
    ones = jnp.ones((8, cells.shape[1]), jnp.bfloat16)
    total = lax.dot_general(ones, high, NT, preferred_element_type=F32)
    total += lax.dot_general(ones, low, NT, preferred_element_type=F32)
    return total[0:1]


def log_sum(parts):
    highest = jnp.max(parts, axis=0)
    return highest + jnp.log2(jnp.sum(jnp.exp2(parts - highest[None]), axis=0))


def expand(weights, wide):
    blocks = weights.shape[0]
    columns = jnp.concatenate([weights, jnp.zeros((TILE - blocks, TILE), F32)], axis=0).T
    for n in range(blocks):
        wide[n] = jnp.broadcast_to(columns[:, n : n + 1], (TILE, TILE))


def dot_tiles(near, far, saved):
    def tile(at, n, f):
        inner = lax.dot_general(near[n], far[f], NT, preferred_element_type=F32) * (2.0 * KAPPA)
        saved[at] = inner
        return inner

    return tile


def tile_sums(place_of, count, source, near_blocks, far_blocks, wide, peaks, totals):
    spare = near_blocks * far_blocks
    peaks[...] = jnp.full(peaks.shape, EMPTY, F32)
    totals[...] = jnp.zeros(totals.shape, F32)
    steps = (count + UNROLL - 1) // UNROLL

    @pl.loop(0, steps)
    def _(step):
        for u in range(UNROLL):
            k = step * UNROLL + u
            n, f = place_of(jnp.where(k < count, k, 0))
            score = (source(k, n, f) + wide[n]).reshape(TILE // 8, 8, TILE)
            peak = jnp.max(score, axis=0)
            slot = jnp.where(k < count, f * near_blocks + n, spare)
            peaks[slot] = peak
            totals[slot] = jnp.sum(jnp.exp2(score - peak[None]), axis=0)

    rows = []
    for f in range(far_blocks):
        at = pl.ds(f * near_blocks, near_blocks)
        peak = peaks[at]
        highest = jnp.max(jnp.max(peak, axis=0), axis=0, keepdims=True)
        whole = jnp.sum(totals[at] * jnp.exp2(peak - highest[None]), axis=0)
        whole = jnp.sum(whole, axis=0, keepdims=True)
        rows.append(jnp.where(whole > 0.0, highest + jnp.log2(whole), EMPTY))
    return jnp.concatenate(rows, axis=0)


def pick_kernel(mine, other, place, picked):
    p = place[3]
    targets = 8
    slots = 2 * TILE

    def put(lists, k, col, at):
        a, b = lists[0, k], lists[1, k]
        picked[1 + (at >> LOG_TILE), at & (TILE - 1)] = (a >> 1) * (2 * targets) + col * targets + b
        return jnp.where((k < lists[2, 0]) & ((a & 1) == p), 1, 0)

    def step(k, ends):
        front, back = ends
        front = front + put(mine, k, p, front)
        return front, back - put(other, k, 1 - p, back)

    front, back = lax.fori_loop(0, TILE, step, (jnp.int32(0), jnp.int32(slots - 1)), unroll=8)
    picked[0, 0] = front
    picked[0, 1] = front + (slots - 1) - back
    for n in range(place.shape[0]):
        picked[0, 2 + n] = place[n]


def tile_code(tiles, k):
    first = tiles[0, 0]
    at = jnp.where(k < first, k, 2 * TILE - 1 + first - k)
    return tiles[1 + (at >> LOG_TILE), at & (TILE - 1)]


def source_tiles(tiles, tgt_blocks):
    def tile(k):
        code = tile_code(tiles, k)
        return lax.rem(code, tgt_blocks), lax.div(code, tgt_blocks)

    return tile


def target_tiles(tiles, tgt_blocks):
    def tile(k):
        code = tile_code(tiles, k)
        return lax.div(code, tgt_blocks), lax.rem(code, tgt_blocks)

    return tile


def pack_kernel(lists, own, *refs):
    src, tgt = refs[-2:]
    sides = src.shape[0]
    src[0] = own[0]
    tgt[0] = own[1]
    for n in range(1, sides):
        src[n] = refs[n - 1][...]
        tgt[n] = refs[sides - 1 + n - 1][...]


def after_kernel(first, block, out):
    out[...] = block[...]


def square_kernel(src, sq_src):
    for a in range(src.shape[0]):
        sq_src[a : a + 1, :] = square_rows(src[a])


def first_kernel(picked, *refs):
    pieces, refs = refs[:-11], refs[-11:]
    out, src, tgt, sq_src, sq_tgt, saved, wide, peaks, totals, tiles, sem = refs
    fetch = pltpu.make_async_copy(picked, tiles, sem)
    fetch.start()
    sides = len(pieces) // 2
    fetch.wait()
    place = [tiles[0, 2 + n] for n in range(5)]
    for d in range(sides):
        x = lax.rem(place[0] + (sides - d), sides)
        p, core = place[3] ^ (d // 2), place[4] ^ (d % 2)
        for n in range(sides):
            s, y = (lax.rem(place[axis] + (sides - n), sides) for axis in (1, 2))
            src[x * sides + s] = pieces[d][n]
            tgt[p * (2 * sides) + 2 * y + core] = pieces[sides + d][n]
    srcs, tgts = src.shape[0], tgt.shape[0]
    for b in range(tgts):
        sq_tgt[b : b + 1, :] = square_rows(tgt[b])
    for a in range(srcs):
        sq_src[a : a + 1, :] = square_rows(src[a])
    expand(sq_tgt[...] * -KAPPA, wide)
    source = dot_tiles(tgt, src, saved)
    sums = tile_sums(source_tiles(tiles, tgts), tiles[0, 1], source, tgts, srcs, wide, peaks, totals)
    out[...] = jnp.broadcast_to(sums[None], out.shape)


def target_kernel(log_cells, picked, src, tgt, parts, out, saved, wide, peaks, totals, tiles, sem):
    fetch = pltpu.make_async_copy(picked, tiles, sem)
    fetch.start()
    expand(-log_cells - log_sum(parts[...]), wide)
    fetch.wait()
    srcs, tgts = src.shape[0], tgt.shape[0]
    source = dot_tiles(src, tgt, saved)
    sums = tile_sums(target_tiles(tiles, tgts), tiles[0, 1], source, srcs, tgts, wide, peaks, totals)
    out[...] = jnp.broadcast_to(sums[None], out.shape)


def again_source_kernel(log_cells, picked, saved, parts, out, wide, peaks, totals, tiles, sem):
    fetch = pltpu.make_async_copy(picked, tiles, sem)
    fetch.start()
    source = lambda at, n, f: saved[at]
    tgts, srcs = parts.shape[1], out.shape[1]
    expand(-log_cells - log_sum(parts[...]), wide)
    fetch.wait()
    sums = tile_sums(source_tiles(tiles, tgts), tiles[0, 1], source, tgts, srcs, wide, peaks, totals)
    out[...] = jnp.broadcast_to(sums[None], out.shape)


def again_target_kernel(
    log_cells, tgts, picked, saved, parts, sq_src, out, pot, wide, peaks, totals, tiles, sem
):
    fetch = pltpu.make_async_copy(picked, tiles, sem)
    fetch.start()
    source = lambda at, n, f: saved[at]
    srcs = parts.shape[1]
    weights = -log_cells - log_sum(parts[...])
    pot[...] = weights * (1.0 / KAPPA) + sq_src[...]
    expand(weights, wide)
    fetch.wait()
    sums = tile_sums(target_tiles(tiles, tgts), tiles[0, 1], source, srcs, tgts, wide, peaks, totals)
    copies, blocks = out.shape[0], out.shape[1]
    cols = tgts // blocks
    each = copies // cols
    for col in range(cols):
        piece = sums[col * blocks : (col + 1) * blocks]
        out[col * each : (col + 1) * each] = jnp.broadcast_to(piece[None], (each,) + piece.shape)


def last_kernel(log_cells, parity, parts, sq_tgt, mine, other, tgt_pot, src_pot):
    p = parity[0]
    blocks = tgt_pot.shape[0]
    squares = jnp.where(p == 0, sq_tgt[0:blocks], sq_tgt[blocks : 2 * blocks])
    tgt_pot[...] = (-log_cells - log_sum(parts[...])) * (1.0 / KAPPA) + squares
    src_pot[:, 0, :] = jnp.where(p == 0, mine[...], other[...])
    src_pot[:, 1, :] = jnp.where(p == 0, other[...], mine[...])


def half_step(kernel, outs, near_blocks, slots, picked, *args):
    return pl.pallas_call(
        kernel,
        out_shape=[s if isinstance(s, jax.ShapeDtypeStruct) else jax.ShapeDtypeStruct(s, F32) for s in outs],
        in_specs=[ANY] + [VMEM] * len(args),
        out_specs=[VMEM] * len(outs),
        scratch_shapes=[
            pltpu.VMEM((near_blocks, TILE, TILE), F32),
            pltpu.VMEM((slots + 1, 8, TILE), F32),
            pltpu.VMEM((slots + 1, 8, TILE), F32),
            pltpu.SMEM(picked.shape, picked.dtype),
            pltpu.SemaphoreType.DMA,
        ],
        compiler_params=PARAMS,
    )(picked, *args)


def exchange(copies, peers):
    return lax.all_to_all(copies, peers, 0, 0, tiled=True)


def shifts(block, axis):
    n = lax.axis_size(axis)
    turn = lambda d: lax.ppermute(block, axis, [(i, (i + d) % n) for i in range(n)])
    return [block] + [turn(d) for d in range(1, n)]


def bands(src_embed, tgt_embed, lists):
    own = jnp.stack([src_embed, tgt_embed])
    far = shifts(src_embed, "s")[1:] + shifts(tgt_embed, "y")[1:]
    group = jax.ShapeDtypeStruct((lax.axis_size("s"),) + src_embed.shape, src_embed.dtype)
    src, tgt = pl.pallas_call(
        pack_kernel,
        out_shape=[group] * 2,
        in_specs=[ANY] + [VMEM] * (1 + len(far)),
        out_specs=[VMEM] * 2,
        compiler_params=PARAMS,
    )(lists, own, *far)
    src_pieces = shifts(src, "x")
    mine, partner = shifts(tgt, "p")
    mine = pl.pallas_call(
        after_kernel, out_shape=group, in_specs=[ANY, VMEM], out_specs=VMEM, compiler_params=PARAMS
    )(partner, mine)
    return src_pieces, [piece for side in (mine, partner) for piece in shifts(side, "core")]


def local(src_embed, tgt_embed, tiles, counts):
    rows, cols = lax.axis_size(ROW), lax.axis_size(COL)
    log_cells = math.log2(rows * cols * TILE)
    parity = lax.axis_index("p").astype(jnp.int32).reshape(1)
    partner = lambda v: lax.ppermute(v, "p", [(0, 1), (1, 0)])

    lists = jnp.concatenate([tiles[0, 0], jnp.broadcast_to(counts[0, 0], (1, TILE))], axis=0)
    other_lists = partner(lists)
    place = jnp.stack([lax.axis_index(a) for a in ("x", "s", "y", "p", "core")]).astype(jnp.int32)
    src_pieces, tgt_pieces = bands(src_embed, tgt_embed, other_lists)
    picked = pl.pallas_call(
        pick_kernel,
        out_shape=jax.ShapeDtypeStruct((8, TILE), jnp.int32),
        in_specs=[SMEM] * 3,
        out_specs=SMEM,
        compiler_params=PARAMS,
    )(lists, other_lists, place)

    srcs, tgts = (len(pieces) * pieces[0].shape[0] for pieces in (src_pieces, tgt_pieces))
    tgt_shape = jax.ShapeDtypeStruct((tgts,) + tgt_embed.shape, tgt_embed.dtype)
    src_shape = jax.ShapeDtypeStruct((srcs,) + src_embed.shape, src_embed.dtype)
    slots = srcs * tgts
    src_out, tgt_out, all_tiles = (srcs, srcs, TILE), (tgts, tgts, TILE), (slots, TILE, TILE)
    outs = [src_out, src_shape, tgt_shape, (srcs, TILE), (tgts, TILE), all_tiles]
    parts, src, tgt, sq_src, sq_tgt, src_saved = half_step(
        first_kernel, outs, tgts, slots, picked, *src_pieces, *tgt_pieces
    )
    parts = exchange(parts, SRC_PEERS)
    step = functools.partial(target_kernel, log_cells)
    parts, tgt_saved = half_step(step, [tgt_out, all_tiles], srcs, slots, picked, src, tgt, parts)
    parts = exchange(parts, TGT_PEERS)
    step = functools.partial(again_source_kernel, log_cells)
    (parts,) = half_step(step, [src_out], tgts, slots, picked, src_saved, parts)
    parts = exchange(parts, SRC_PEERS)
    step = functools.partial(again_target_kernel, log_cells, tgts)
    outs = [(tgts, rows, TILE), (srcs, TILE)]
    parts, src_pot = half_step(step, outs, srcs, slots, picked, tgt_saved, parts, sq_src)
    other_pot = partner(src_pot)
    parts = exchange(parts, TGT_PEERS)
    tgt_pot, both = pl.pallas_call(
        functools.partial(last_kernel, log_cells),
        out_shape=[jax.ShapeDtypeStruct((rows, TILE), F32), jax.ShapeDtypeStruct((srcs, 2, TILE), F32)],
        in_specs=[SMEM] + [VMEM] * 4,
        out_specs=[VMEM] * 2,
        compiler_params=PARAMS,
    )(parity, parts, sq_tgt, src_pot, other_pot)
    return (both.reshape(-1), tgt_pot.reshape(-1))


def solution(mesh):
    fine = Mesh(mesh.devices.reshape(4, 2, 4, 4, 2), ROW + COL)
    in_specs = (P(ROW + COL, None), P(COL + ROW, None), P(ROW, COL, None, None), P(ROW, COL))
    return jax.shard_map(local, mesh=fine, in_specs=in_specs, out_specs=(P(ROW), P(COL)), check_vma=False)
```

```python
import functools
import math

import jax
import jax.numpy as jnp
from jax import lax
from jax.experimental import pallas as pl
from jax.experimental.pallas import tpu as pltpu
from jax.sharding import Mesh
from jax.sharding import PartitionSpec as P

TILE = 128
LOG_TILE = 7
ENTROPY = 0.05
KAPPA = math.log2(math.e) / ENTROPY
EMPTY = -1e30
UNROLL = 16
ROW = ("y", "core")
COL = ("x", "s", "p")
SRC_PEERS = ("x", "s")
TGT_PEERS = ("p", "y", "core")
F32 = jnp.float32
NT = (((1,), (1,)), ((), ()))
VMEM = pl.BlockSpec(memory_space=pltpu.VMEM)
SMEM = pl.BlockSpec(memory_space=pltpu.SMEM)
ANY = pl.BlockSpec(memory_space=pl.ANY)
PARAMS = pltpu.CompilerParams(vmem_limit_bytes=10 * 2**20)


def square_rows(cells):
    wide = cells.astype(F32)
    square = wide * wide
    high = square.astype(jnp.bfloat16)
    low = (square - high.astype(F32)).astype(jnp.bfloat16)
    ones = jnp.ones((8, cells.shape[1]), jnp.bfloat16)
    total = lax.dot_general(ones, high, NT, preferred_element_type=F32)
    total += lax.dot_general(ones, low, NT, preferred_element_type=F32)
    return total[0:1]


def log_sum(parts):
    highest = jnp.max(parts, axis=0)
    return highest + jnp.log2(jnp.sum(jnp.exp2(parts - highest[None]), axis=0))


def expand(weights, wide):
    blocks = weights.shape[0]
    columns = jnp.concatenate([weights, jnp.zeros((TILE - blocks, TILE), F32)], axis=0).T
    for n in range(blocks):
        wide[n] = jnp.broadcast_to(columns[:, n : n + 1], (TILE, TILE))


def dot_tiles(near, far, saved):
    def tile(at, n, f):
        inner = lax.dot_general(near[n], far[f], NT, preferred_element_type=F32) * (2.0 * KAPPA)
        saved[at] = inner
        return inner

    return tile


def tile_sums(place_of, count, source, near_blocks, far_blocks, wide, peaks, totals):
    spare = near_blocks * far_blocks
    peaks[...] = jnp.full(peaks.shape, EMPTY, F32)
    totals[...] = jnp.zeros(totals.shape, F32)
    steps = (count + UNROLL - 1) // UNROLL

    @pl.loop(0, steps)
    def _(step):
        for u in range(UNROLL):
            k = step * UNROLL + u
            n, f = place_of(jnp.where(k < count, k, 0))
            score = (source(k, n, f) + wide[n]).reshape(TILE // 8, 8, TILE)
            peak = jnp.max(score, axis=0)
            slot = jnp.where(k < count, f * near_blocks + n, spare)
            peaks[slot] = peak
            totals[slot] = jnp.sum(jnp.exp2(score - peak[None]), axis=0)

    rows = []
    for f in range(far_blocks):
        at = pl.ds(f * near_blocks, near_blocks)
        peak = peaks[at]
        highest = jnp.max(jnp.max(peak, axis=0), axis=0, keepdims=True)
        whole = jnp.sum(totals[at] * jnp.exp2(peak - highest[None]), axis=0)
        whole = jnp.sum(whole, axis=0, keepdims=True)
        rows.append(jnp.where(whole > 0.0, highest + jnp.log2(whole), EMPTY))
    return jnp.concatenate(rows, axis=0)


def pick_kernel(mine, other, place, picked):
    p = place[3]
    targets = 8
    slots = 2 * TILE

    def put(lists, k, col, at):
        a, b = lists[0, k], lists[1, k]
        picked[1 + (at >> LOG_TILE), at & (TILE - 1)] = (a >> 1) * (2 * targets) + col * targets + b
        return jnp.where((k < lists[2, 0]) & ((a & 1) == p), 1, 0)

    def step(k, ends):
        front, back = ends
        front = front + put(mine, k, p, front)
        return front, back - put(other, k, 1 - p, back)

    front, back = lax.fori_loop(0, TILE, step, (jnp.int32(0), jnp.int32(slots - 1)), unroll=8)
    picked[0, 0] = front
    picked[0, 1] = front + (slots - 1) - back
    for n in range(place.shape[0]):
        picked[0, 2 + n] = place[n]


def tile_code(tiles, k):
    first = tiles[0, 0]
    at = jnp.where(k < first, k, 2 * TILE - 1 + first - k)
    return tiles[1 + (at >> LOG_TILE), at & (TILE - 1)]


def source_tiles(tiles, tgt_blocks):
    def tile(k):
        code = tile_code(tiles, k)
        return lax.rem(code, tgt_blocks), lax.div(code, tgt_blocks)

    return tile


def target_tiles(tiles, tgt_blocks):
    def tile(k):
        code = tile_code(tiles, k)
        return lax.div(code, tgt_blocks), lax.rem(code, tgt_blocks)

    return tile


def pack_kernel(lists, own, *refs):
    src, tgt = refs[-2:]
    sides = src.shape[0]
    src[0] = own[0]
    tgt[0:TILE] = own[1]
    for n in range(1, sides):
        src[n] = refs[n - 1][...]
        tgt[n * TILE : (n + 1) * TILE] = refs[sides - 1 + n - 1][...]
    rows = lists[...].astype(F32).astype(tgt.dtype)
    tgt[sides * TILE :, 0:TILE] = rows
    tgt[sides * TILE :, TILE:] = jnp.zeros_like(rows)


def after_kernel(theirs, ours, mine, partner, lists):
    for n in range(mine.shape[0]):
        mine[n] = ours[n * TILE : (n + 1) * TILE]
        partner[n] = theirs[n * TILE : (n + 1) * TILE]
    lists[...] = theirs[mine.shape[0] * TILE :, 0:TILE].astype(F32).astype(jnp.int32)


def first_kernel(picked, *refs):
    pieces, refs = refs[:-11], refs[-11:]
    out, src, tgt, sq_src, sq_tgt, saved, wide, peaks, totals, tiles, sem = refs
    fetch = pltpu.make_async_copy(picked, tiles, sem)
    fetch.start()
    sides = len(pieces) // 2
    fetch.wait()
    place = [tiles[0, 2 + n] for n in range(5)]
    for d in range(sides):
        x = lax.rem(place[0] + (sides - d), sides)
        p, core = place[3] ^ (d // 2), place[4] ^ (d % 2)
        for n in range(sides):
            s, y = (lax.rem(place[axis] + (sides - n), sides) for axis in (1, 2))
            src[x * sides + s] = pieces[d][n]
            tgt[p * (2 * sides) + 2 * y + core] = pieces[sides + d][n]
    srcs, tgts = src.shape[0], tgt.shape[0]
    for b in range(tgts):
        sq_tgt[b : b + 1, :] = square_rows(tgt[b])
    for a in range(srcs):
        sq_src[a : a + 1, :] = square_rows(src[a])
    expand(sq_tgt[...] * -KAPPA, wide)
    source = dot_tiles(tgt, src, saved)
    sums = tile_sums(source_tiles(tiles, tgts), tiles[0, 1], source, tgts, srcs, wide, peaks, totals)
    out[...] = jnp.broadcast_to(sums[None], out.shape)


def target_kernel(log_cells, picked, src, tgt, parts, out, saved, wide, peaks, totals, tiles, sem):
    fetch = pltpu.make_async_copy(picked, tiles, sem)
    fetch.start()
    expand(-log_cells - log_sum(parts[...]), wide)
    fetch.wait()
    srcs, tgts = src.shape[0], tgt.shape[0]
    source = dot_tiles(src, tgt, saved)
    sums = tile_sums(target_tiles(tiles, tgts), tiles[0, 1], source, srcs, tgts, wide, peaks, totals)
    out[...] = jnp.broadcast_to(sums[None], out.shape)


def again_source_kernel(log_cells, picked, saved, parts, out, wide, peaks, totals, tiles, sem):
    fetch = pltpu.make_async_copy(picked, tiles, sem)
    fetch.start()
    source = lambda at, n, f: saved[at]
    tgts, srcs = parts.shape[1], out.shape[1]
    expand(-log_cells - log_sum(parts[...]), wide)
    fetch.wait()
    sums = tile_sums(source_tiles(tiles, tgts), tiles[0, 1], source, tgts, srcs, wide, peaks, totals)
    out[...] = jnp.broadcast_to(sums[None], out.shape)


def again_target_kernel(
    log_cells, tgts, picked, saved, parts, sq_src, out, pot, wide, peaks, totals, tiles, sem
):
    fetch = pltpu.make_async_copy(picked, tiles, sem)
    fetch.start()
    source = lambda at, n, f: saved[at]
    srcs = parts.shape[1]
    weights = -log_cells - log_sum(parts[...])
    pot[...] = weights * (1.0 / KAPPA) + sq_src[...]
    expand(weights, wide)
    fetch.wait()
    sums = tile_sums(target_tiles(tiles, tgts), tiles[0, 1], source, srcs, tgts, wide, peaks, totals)
    copies, blocks = out.shape[0], out.shape[1]
    cols = tgts // blocks
    each = copies // cols
    for col in range(cols):
        piece = sums[col * blocks : (col + 1) * blocks]
        out[col * each : (col + 1) * each] = jnp.broadcast_to(piece[None], (each,) + piece.shape)


def last_kernel(log_cells, parity, parts, sq_tgt, mine, other, tgt_pot, src_pot):
    p = parity[0]
    blocks = tgt_pot.shape[0]
    squares = jnp.where(p == 0, sq_tgt[0:blocks], sq_tgt[blocks : 2 * blocks])
    tgt_pot[...] = (-log_cells - log_sum(parts[...])) * (1.0 / KAPPA) + squares
    src_pot[:, 0, :] = jnp.where(p == 0, mine[...], other[...])
    src_pot[:, 1, :] = jnp.where(p == 0, other[...], mine[...])


def half_step(kernel, outs, near_blocks, slots, picked, *args):
    return pl.pallas_call(
        kernel,
        out_shape=[s if isinstance(s, jax.ShapeDtypeStruct) else jax.ShapeDtypeStruct(s, F32) for s in outs],
        in_specs=[ANY] + [VMEM] * len(args),
        out_specs=[VMEM] * len(outs),
        scratch_shapes=[
            pltpu.VMEM((near_blocks, TILE, TILE), F32),
            pltpu.VMEM((slots + 1, 8, TILE), F32),
            pltpu.VMEM((slots + 1, 8, TILE), F32),
            pltpu.SMEM(picked.shape, picked.dtype),
            pltpu.SemaphoreType.DMA,
        ],
        compiler_params=PARAMS,
    )(picked, *args)


def exchange(copies, peers):
    return lax.all_to_all(copies, peers, 0, 0, tiled=True)


def shifts(block, axis):
    n = lax.axis_size(axis)
    turn = lambda d: lax.ppermute(block, axis, [(i, (i + d) % n) for i in range(n)])
    return [block] + [turn(d) for d in range(1, n)]


def bands(src_embed, tgt_embed, lists):
    own = jnp.stack([src_embed, tgt_embed])
    far = shifts(src_embed, "s")[1:] + shifts(tgt_embed, "y")[1:]
    group = jax.ShapeDtypeStruct((lax.axis_size("s"),) + src_embed.shape, src_embed.dtype)
    rows, width = group.shape[0] * TILE + lists.shape[0], src_embed.shape[1]
    src, tgt = pl.pallas_call(
        pack_kernel,
        out_shape=[group, jax.ShapeDtypeStruct((rows, width), tgt_embed.dtype)],
        in_specs=[VMEM] * (2 + len(far)),
        out_specs=[VMEM] * 2,
        compiler_params=PARAMS,
    )(lists, own, *far)
    src_pieces = shifts(src, "x")
    ours, theirs = shifts(tgt, "p")
    mine, partner, other_lists = pl.pallas_call(
        after_kernel,
        out_shape=[group, group, jax.ShapeDtypeStruct(lists.shape, lists.dtype)],
        in_specs=[VMEM] * 2,
        out_specs=[VMEM] * 3,
        compiler_params=PARAMS,
    )(theirs, ours)
    return src_pieces, [piece for side in (mine, partner) for piece in shifts(side, "core")], other_lists


def local(src_embed, tgt_embed, tiles, counts):
    rows, cols = lax.axis_size(ROW), lax.axis_size(COL)
    log_cells = math.log2(rows * cols * TILE)
    parity = lax.axis_index("p").astype(jnp.int32).reshape(1)
    partner = lambda v: lax.ppermute(v, "p", [(0, 1), (1, 0)])

    lists = jnp.concatenate([tiles[0, 0], jnp.broadcast_to(counts[0, 0], (14, TILE))], axis=0)
    place = jnp.stack([lax.axis_index(a) for a in ("x", "s", "y", "p", "core")]).astype(jnp.int32)
    src_pieces, tgt_pieces, other_lists = bands(src_embed, tgt_embed, lists)
    picked = pl.pallas_call(
        pick_kernel,
        out_shape=jax.ShapeDtypeStruct((8, TILE), jnp.int32),
        in_specs=[SMEM] * 3,
        out_specs=SMEM,
        compiler_params=PARAMS,
    )(lists, other_lists, place)

    srcs, tgts = (len(pieces) * pieces[0].shape[0] for pieces in (src_pieces, tgt_pieces))
    tgt_shape = jax.ShapeDtypeStruct((tgts,) + tgt_embed.shape, tgt_embed.dtype)
    src_shape = jax.ShapeDtypeStruct((srcs,) + src_embed.shape, src_embed.dtype)
    slots = srcs * tgts
    src_out, tgt_out, all_tiles = (srcs, srcs, TILE), (tgts, tgts, TILE), (slots, TILE, TILE)
    outs = [src_out, src_shape, tgt_shape, (srcs, TILE), (tgts, TILE), all_tiles]
    parts, src, tgt, sq_src, sq_tgt, src_saved = half_step(
        first_kernel, outs, tgts, slots, picked, *src_pieces, *tgt_pieces
    )
    parts = exchange(parts, SRC_PEERS)
    step = functools.partial(target_kernel, log_cells)
    parts, tgt_saved = half_step(step, [tgt_out, all_tiles], srcs, slots, picked, src, tgt, parts)
    parts = exchange(parts, TGT_PEERS)
    step = functools.partial(again_source_kernel, log_cells)
    (parts,) = half_step(step, [src_out], tgts, slots, picked, src_saved, parts)
    parts = exchange(parts, SRC_PEERS)
    step = functools.partial(again_target_kernel, log_cells, tgts)
    outs = [(tgts, rows, TILE), (srcs, TILE)]
    parts, src_pot = half_step(step, outs, srcs, slots, picked, tgt_saved, parts, sq_src)
    other_pot = partner(src_pot)
    parts = exchange(parts, TGT_PEERS)
    tgt_pot, both = pl.pallas_call(
        functools.partial(last_kernel, log_cells),
        out_shape=[jax.ShapeDtypeStruct((rows, TILE), F32), jax.ShapeDtypeStruct((srcs, 2, TILE), F32)],
        in_specs=[SMEM] + [VMEM] * 4,
        out_specs=[VMEM] * 2,
        compiler_params=PARAMS,
    )(parity, parts, sq_tgt, src_pot, other_pot)
    return (both.reshape(-1), tgt_pot.reshape(-1))


def solution(mesh):
    fine = Mesh(mesh.devices.reshape(4, 2, 4, 4, 2), ROW + COL)
    in_specs = (P(ROW + COL, None), P(COL + ROW, None), P(ROW, COL, None, None), P(ROW, COL))
    return jax.shard_map(local, mesh=fine, in_specs=in_specs, out_specs=(P(ROW), P(COL)), check_vma=False)
```

```python
import functools
import math

import jax
import jax.numpy as jnp
from jax import lax
from jax.experimental import pallas as pl
from jax.experimental.pallas import tpu as pltpu
from jax.sharding import Mesh
from jax.sharding import PartitionSpec as P

TILE = 128
LOG_TILE = 7
ENTROPY = 0.05
KAPPA = math.log2(math.e) / ENTROPY
EMPTY = -1e30
SUM_STEP = 16
DOT_STEP = 32
ROW = ("y", "core")
COL = ("x", "s", "p")
SRC_PEERS = ("x", "s")
TGT_PEERS = ("p", "y", "core")
F32 = jnp.float32
NT = (((1,), (1,)), ((), ()))
VMEM = pl.BlockSpec(memory_space=pltpu.VMEM)
SMEM = pl.BlockSpec(memory_space=pltpu.SMEM)
ANY = pl.BlockSpec(memory_space=pl.ANY)
PARAMS = pltpu.CompilerParams(vmem_limit_bytes=10 * 2**20)


def square_rows(cells):
    wide = cells.astype(F32)
    square = wide * wide
    high = square.astype(jnp.bfloat16)
    low = (square - high.astype(F32)).astype(jnp.bfloat16)
    ones = jnp.ones((8, cells.shape[1]), jnp.bfloat16)
    total = lax.dot_general(ones, high, NT, preferred_element_type=F32)
    total += lax.dot_general(ones, low, NT, preferred_element_type=F32)
    return total[0:1]


def log_sum(parts):
    highest = jnp.max(parts, axis=0)
    return highest + jnp.log2(jnp.sum(jnp.exp2(parts - highest[None]), axis=0))


def expand(weights, wide):
    blocks = weights.shape[0]
    columns = jnp.concatenate([weights, jnp.zeros((TILE - blocks, TILE), F32)], axis=0).T
    for n in range(blocks):
        wide[n] = jnp.broadcast_to(columns[:, n : n + 1], (TILE, TILE))


def dot_tiles(near, far, saved):
    def tile(at, n, f):
        inner = lax.dot_general(near[n], far[f], NT, preferred_element_type=F32) * (2.0 * KAPPA)
        saved[at] = inner
        return inner

    return tile


def tile_sums(place_of, count, source, near_blocks, far_blocks, wide, peaks, totals, group=SUM_STEP):
    spare = near_blocks * far_blocks
    peaks[...] = jnp.full(peaks.shape, EMPTY, F32)
    totals[...] = jnp.zeros(totals.shape, F32)
    steps = (count + group - 1) // group

    @pl.loop(0, steps)
    def _(step):
        for u in range(group):
            k = step * group + u
            n, f = place_of(jnp.where(k < count, k, 0))
            score = (source(k, n, f) + wide[n]).reshape(TILE // 8, 8, TILE)
            peak = jnp.max(score, axis=0)
            slot = jnp.where(k < count, f * near_blocks + n, spare)
            peaks[slot] = peak
            totals[slot] = jnp.sum(jnp.exp2(score - peak[None]), axis=0)

    rows = []
    for f in range(far_blocks):
        at = pl.ds(f * near_blocks, near_blocks)
        peak = peaks[at]
        highest = jnp.max(jnp.max(peak, axis=0), axis=0, keepdims=True)
        whole = jnp.sum(totals[at] * jnp.exp2(peak - highest[None]), axis=0)
        whole = jnp.sum(whole, axis=0, keepdims=True)
        rows.append(jnp.where(whole > 0.0, highest + jnp.log2(whole), EMPTY))
    return jnp.concatenate(rows, axis=0)


def pick_kernel(mine, other, place, picked):
    p = place[3]
    targets = 8
    slots = 2 * TILE

    def put(lists, k, col, at):
        a, b = lists[0, k], lists[1, k]
        picked[1 + (at >> LOG_TILE), at & (TILE - 1)] = (a >> 1) * (2 * targets) + col * targets + b
        return jnp.where((k < lists[2, 0]) & ((a & 1) == p), 1, 0)

    def step(k, ends):
        front, back = ends
        front = front + put(mine, k, p, front)
        return front, back - put(other, k, 1 - p, back)

    front, back = lax.fori_loop(0, TILE, step, (jnp.int32(0), jnp.int32(slots - 1)), unroll=8)
    picked[0, 0] = front
    picked[0, 1] = front + (slots - 1) - back
    for n in range(place.shape[0]):
        picked[0, 2 + n] = place[n]


def tile_code(tiles, k):
    first = tiles[0, 0]
    at = jnp.where(k < first, k, 2 * TILE - 1 + first - k)
    return tiles[1 + (at >> LOG_TILE), at & (TILE - 1)]


def source_tiles(tiles, tgt_blocks):
    def tile(k):
        code = tile_code(tiles, k)
        return lax.rem(code, tgt_blocks), lax.div(code, tgt_blocks)

    return tile


def target_tiles(tiles, tgt_blocks):
    def tile(k):
        code = tile_code(tiles, k)
        return lax.div(code, tgt_blocks), lax.rem(code, tgt_blocks)

    return tile


def pack_kernel(lists, own, *refs):
    src, tgt = refs[-2:]
    sides = src.shape[0]
    src[0] = own[0]
    tgt[0:TILE] = own[1]
    for n in range(1, sides):
        src[n] = refs[n - 1][...]
        tgt[n * TILE : (n + 1) * TILE] = refs[sides - 1 + n - 1][...]
    rows = lists[...].astype(F32).astype(tgt.dtype)
    tgt[sides * TILE :, 0:TILE] = rows
    tgt[sides * TILE :, TILE:] = jnp.zeros_like(rows)


def after_kernel(theirs, ours, mine, partner, lists):
    for n in range(mine.shape[0]):
        mine[n] = ours[n * TILE : (n + 1) * TILE]
        partner[n] = theirs[n * TILE : (n + 1) * TILE]
    lists[...] = theirs[mine.shape[0] * TILE :, 0:TILE].astype(F32).astype(jnp.int32)


def first_kernel(picked, *refs):
    pieces, refs = refs[:-11], refs[-11:]
    out, src, tgt, sq_src, sq_tgt, saved, wide, peaks, totals, tiles, sem = refs
    fetch = pltpu.make_async_copy(picked, tiles, sem)
    fetch.start()
    sides = len(pieces) // 2
    fetch.wait()
    place = [tiles[0, 2 + n] for n in range(5)]
    for d in range(sides):
        x = lax.rem(place[0] + (sides - d), sides)
        p, core = place[3] ^ (d // 2), place[4] ^ (d % 2)
        for n in range(sides):
            s, y = (lax.rem(place[axis] + (sides - n), sides) for axis in (1, 2))
            src[x * sides + s] = pieces[d][n]
            tgt[p * (2 * sides) + 2 * y + core] = pieces[sides + d][n]
    srcs, tgts = src.shape[0], tgt.shape[0]
    for b in range(tgts):
        sq_tgt[b : b + 1, :] = square_rows(tgt[b])
    for a in range(srcs):
        sq_src[a : a + 1, :] = square_rows(src[a])
    expand(sq_tgt[...] * -KAPPA, wide)
    source = dot_tiles(tgt, src, saved)
    sums = tile_sums(source_tiles(tiles, tgts), tiles[0, 1], source, tgts, srcs, wide, peaks, totals, DOT_STEP)
    out[...] = jnp.broadcast_to(sums[None], out.shape)


def target_kernel(log_cells, picked, src, tgt, parts, out, saved, wide, peaks, totals, tiles, sem):
    fetch = pltpu.make_async_copy(picked, tiles, sem)
    fetch.start()
    expand(-log_cells - log_sum(parts[...]), wide)
    fetch.wait()
    srcs, tgts = src.shape[0], tgt.shape[0]
    source = dot_tiles(src, tgt, saved)
    sums = tile_sums(target_tiles(tiles, tgts), tiles[0, 1], source, srcs, tgts, wide, peaks, totals, DOT_STEP)
    out[...] = jnp.broadcast_to(sums[None], out.shape)


def again_source_kernel(log_cells, picked, saved, parts, out, wide, peaks, totals, tiles, sem):
    fetch = pltpu.make_async_copy(picked, tiles, sem)
    fetch.start()
    source = lambda at, n, f: saved[at]
    tgts, srcs = parts.shape[1], out.shape[1]
    expand(-log_cells - log_sum(parts[...]), wide)
    fetch.wait()
    sums = tile_sums(source_tiles(tiles, tgts), tiles[0, 1], source, tgts, srcs, wide, peaks, totals)
    out[...] = jnp.broadcast_to(sums[None], out.shape)


def again_target_kernel(
    log_cells, tgts, picked, saved, parts, sq_src, out, pot, wide, peaks, totals, tiles, sem
):
    fetch = pltpu.make_async_copy(picked, tiles, sem)
    fetch.start()
    source = lambda at, n, f: saved[at]
    srcs = parts.shape[1]
    weights = -log_cells - log_sum(parts[...])
    pot[...] = weights * (1.0 / KAPPA) + sq_src[...]
    expand(weights, wide)
    fetch.wait()
    sums = tile_sums(target_tiles(tiles, tgts), tiles[0, 1], source, srcs, tgts, wide, peaks, totals)
    copies, blocks = out.shape[0], out.shape[1]
    cols = tgts // blocks
    each = copies // cols
    for col in range(cols):
        piece = sums[col * blocks : (col + 1) * blocks]
        out[col * each : (col + 1) * each] = jnp.broadcast_to(piece[None], (each,) + piece.shape)


def last_kernel(log_cells, parity, parts, sq_tgt, mine, other, tgt_pot, src_pot):
    p = parity[0]
    blocks = tgt_pot.shape[0]
    squares = jnp.where(p == 0, sq_tgt[0:blocks], sq_tgt[blocks : 2 * blocks])
    tgt_pot[...] = (-log_cells - log_sum(parts[...])) * (1.0 / KAPPA) + squares
    src_pot[:, 0, :] = jnp.where(p == 0, mine[...], other[...])
    src_pot[:, 1, :] = jnp.where(p == 0, other[...], mine[...])


def half_step(kernel, outs, near_blocks, slots, picked, *args):
    return pl.pallas_call(
        kernel,
        out_shape=[s if isinstance(s, jax.ShapeDtypeStruct) else jax.ShapeDtypeStruct(s, F32) for s in outs],
        in_specs=[ANY] + [VMEM] * len(args),
        out_specs=[VMEM] * len(outs),
        scratch_shapes=[
            pltpu.VMEM((near_blocks, TILE, TILE), F32),
            pltpu.VMEM((slots + 1, 8, TILE), F32),
            pltpu.VMEM((slots + 1, 8, TILE), F32),
            pltpu.SMEM(picked.shape, picked.dtype),
            pltpu.SemaphoreType.DMA,
        ],
        compiler_params=PARAMS,
    )(picked, *args)


def exchange(copies, peers):
    return lax.all_to_all(copies, peers, 0, 0, tiled=True)


def shifts(block, axis):
    n = lax.axis_size(axis)
    turn = lambda d: lax.ppermute(block, axis, [(i, (i + d) % n) for i in range(n)])
    return [block] + [turn(d) for d in range(1, n)]


def bands(src_embed, tgt_embed, lists):
    own = jnp.stack([src_embed, tgt_embed])
    far = shifts(src_embed, "s")[1:] + shifts(tgt_embed, "y")[1:]
    group = jax.ShapeDtypeStruct((lax.axis_size("s"),) + src_embed.shape, src_embed.dtype)
    rows, width = group.shape[0] * TILE + lists.shape[0], src_embed.shape[1]
    src, tgt = pl.pallas_call(
        pack_kernel,
        out_shape=[group, jax.ShapeDtypeStruct((rows, width), tgt_embed.dtype)],
        in_specs=[VMEM] * (2 + len(far)),
        out_specs=[VMEM] * 2,
        compiler_params=PARAMS,
    )(lists, own, *far)
    src_pieces = shifts(src, "x")
    ours, theirs = shifts(tgt, "p")
    mine, partner, other_lists = pl.pallas_call(
        after_kernel,
        out_shape=[group, group, jax.ShapeDtypeStruct(lists.shape, lists.dtype)],
        in_specs=[VMEM] * 2,
        out_specs=[VMEM] * 3,
        compiler_params=PARAMS,
    )(theirs, ours)
    return src_pieces, [piece for side in (mine, partner) for piece in shifts(side, "core")], other_lists


def local(src_embed, tgt_embed, tiles, counts):
    rows, cols = lax.axis_size(ROW), lax.axis_size(COL)
    log_cells = math.log2(rows * cols * TILE)
    parity = lax.axis_index("p").astype(jnp.int32).reshape(1)
    partner = lambda v: lax.ppermute(v, "p", [(0, 1), (1, 0)])

    lists = jnp.concatenate([tiles[0, 0], jnp.broadcast_to(counts[0, 0], (14, TILE))], axis=0)
    place = jnp.stack([lax.axis_index(a) for a in ("x", "s", "y", "p", "core")]).astype(jnp.int32)
    src_pieces, tgt_pieces, other_lists = bands(src_embed, tgt_embed, lists)
    picked = pl.pallas_call(
        pick_kernel,
        out_shape=jax.ShapeDtypeStruct((8, TILE), jnp.int32),
        in_specs=[SMEM] * 3,
        out_specs=SMEM,
        compiler_params=PARAMS,
    )(lists, other_lists, place)

    srcs, tgts = (len(pieces) * pieces[0].shape[0] for pieces in (src_pieces, tgt_pieces))
    tgt_shape = jax.ShapeDtypeStruct((tgts,) + tgt_embed.shape, tgt_embed.dtype)
    src_shape = jax.ShapeDtypeStruct((srcs,) + src_embed.shape, src_embed.dtype)
    slots = srcs * tgts
    src_out, tgt_out, all_tiles = (srcs, srcs, TILE), (tgts, tgts, TILE), (slots, TILE, TILE)
    outs = [src_out, src_shape, tgt_shape, (srcs, TILE), (tgts, TILE), all_tiles]
    parts, src, tgt, sq_src, sq_tgt, src_saved = half_step(
        first_kernel, outs, tgts, slots, picked, *src_pieces, *tgt_pieces
    )
    parts = exchange(parts, SRC_PEERS)
    step = functools.partial(target_kernel, log_cells)
    parts, tgt_saved = half_step(step, [tgt_out, all_tiles], srcs, slots, picked, src, tgt, parts)
    parts = exchange(parts, TGT_PEERS)
    step = functools.partial(again_source_kernel, log_cells)
    (parts,) = half_step(step, [src_out], tgts, slots, picked, src_saved, parts)
    parts = exchange(parts, SRC_PEERS)
    step = functools.partial(again_target_kernel, log_cells, tgts)
    outs = [(tgts, rows, TILE), (srcs, TILE)]
    parts, src_pot = half_step(step, outs, srcs, slots, picked, tgt_saved, parts, sq_src)
    other_pot = partner(src_pot)
    parts = exchange(parts, TGT_PEERS)
    tgt_pot, both = pl.pallas_call(
        functools.partial(last_kernel, log_cells),
        out_shape=[jax.ShapeDtypeStruct((rows, TILE), F32), jax.ShapeDtypeStruct((srcs, 2, TILE), F32)],
        in_specs=[SMEM] + [VMEM] * 4,
        out_specs=[VMEM] * 2,
        compiler_params=PARAMS,
    )(parity, parts, sq_tgt, src_pot, other_pot)
    return (both.reshape(-1), tgt_pot.reshape(-1))


def solution(mesh):
    fine = Mesh(mesh.devices.reshape(4, 2, 4, 4, 2), ROW + COL)
    in_specs = (P(ROW + COL, None), P(COL + ROW, None), P(ROW, COL, None, None), P(ROW, COL))
    return jax.shard_map(local, mesh=fine, in_specs=in_specs, out_specs=(P(ROW), P(COL)), check_vma=False)
```
